128 devices in a mesh: dp: 8 (over y_hi, z), seq: 16 (over x, y_lo, core).
Axes of the slice: x: 4, y: 4 (y_hi: 2, y_lo: 2; y = y_hi * 2 + y_lo), z: 4, core: 2. Of those that a mesh axis runs over, the one named last changes fastest.
Arguments:
- hidden_in: bfloat16 [16384, 1024], P(('dp', 'seq')), may hold values from -24 to 24
- mixer_weight: bfloat16 [1024, 4096], P('seq'), may hold values from -0.1875 to 0.1875
- output_weight: bfloat16 [1024, 1024], P('seq'), may hold values from -0.1875 to 0.1875
- gate_up_weight: bfloat16 [1024, 5632], P('seq'), may hold values from -0.1875 to 0.1875
- down_weight: bfloat16 [2816, 1024], P('seq'), may hold values from -0.109375 to 0.109375
- mixer_norm_gain: bfloat16 [1024], P('seq'), may hold values from 0.5 to 1.5
- head_group_gain: bfloat16 [1024], P('seq'), may hold values from 0.5 to 1.5
- feedforward_gain: bfloat16 [1024], P('seq'), may hold values from 0.5 to 1.5
- forget_floor: float32 [1024], replicated, may hold values from 0.8 to 1
- out_grad: bfloat16 [16384, 1024], P(('dp', 'seq')), may hold values from -6 to 6
Outputs:
- output: bfloat16 [16384, 1024], P(('dp', 'seq'))
- input_grad: bfloat16 [16384, 1024], P(('dp', 'seq'))
- mix_weight_grad: float32 [1024, 4096], P('seq')
- out_weight_grad: float32 [1024, 1024], P('seq')
- upgate_weight_grad: float32 [1024, 5632], P('seq')
- down_weight_grad: float32 [2816, 1024], P('seq')
- mixer_gain_grad: float32 [1024], P('seq')
- group_gain_grad: float32 [1024], P('seq')
- ffn_gain_grad: float32 [1024], P('seq')
- forget_floor_grad: float32 [1024], replicated
The draws below stay inside these ranges and needn't reach their ends.
All inputs are finite; a program needn't handle non-finite values.
Results may differ from the reference program's by a relative error of at most 0.023.
Values may be sent and summed in bfloat16 or wider, within the bound.
No kernel may reach another device: no remote copies, remote signals or barrier semaphores. Data moves between devices by JAX's collectives and lax.ppermute only.
A program may use at most 128 MiB of HBM per device.

```python
import math
import jax
import jax.numpy as jnp
from jax import lax

D = 1024
HEADS = 8
HEAD_DIM = 128
FF = 2816
BLOCK = 64
LENGTH = 2048
SEQS = 8
TOKENS = 16384


def draw_forget_floor(key, part):
    key_order = jax.random.fold_in(key, 11)
    key_slow = jax.random.fold_in(key, 12)
    key_fast = jax.random.fold_in(key, 13)
    order = jax.random.permutation(key_order, HEADS)
    slow_count = HEADS // 2
    slow_heads = (order < slow_count)[:, None]
    slow_loss = jnp.exp(jax.random.uniform(key_slow, (HEADS, HEAD_DIM), jnp.float32, math.log(2.0), math.log(4.4))) / LENGTH
    fast_loss = jax.random.uniform(key_fast, (HEADS, HEAD_DIM), jnp.float32, 0.05, 0.2)
    loss = jnp.where(slow_heads, slow_loss, fast_loss)
    return (1.0 - loss).reshape(D).astype(jnp.float32)


def with_spikes(drawn, rng, source, target, blocks, factor):
    owner, partner = [(jnp.arange(drawn.shape[axis_at]) // (drawn.shape[axis_at] // blocks)).reshape([-1 if axis == axis_at else 1 for axis in range(drawn.ndim)]) for axis_at in (source, target)]
    chosen = jax.random.permutation(rng, blocks)[partner]
    strong = (owner == chosen) | (owner == (partner + blocks // 2) % blocks)
    return jnp.where(strong, factor * drawn, drawn)


def block_scale(rng, extent, cuts, low, largest):
    gain, own = 1.0, jax.random.fold_in(rng, 6)
    for dim, parts in cuts:
        draws = jnp.exp(jax.random.uniform(jax.random.fold_in(own, dim), (parts,), jnp.float32, low / len(cuts), largest / len(cuts)))
        gain = gain * jnp.repeat(draws, extent[dim] // parts).reshape([-1 if axis == dim else 1 for axis in range(len(extent))])
    return gain


def bell_draw(stream_key, extent, spread, most, pieces=(), dtype=jnp.bfloat16):
    array = jax.random.normal(stream_key, extent, jnp.float32) * spread
    if len(pieces) > 0:
        array = block_scale(stream_key, extent, pieces, -0.22, 0.18) * array
    return jnp.clip(array, min=-most, max=most).astype(dtype)


def bell_draw_with(rng, dims, spread, limit, cuts, heavy, dtype=jnp.bfloat16):
    drawn = spread * jax.random.normal(rng, dims, jnp.float32)
    if cuts:
        drawn = drawn * block_scale(rng, dims, cuts, -0.22, 0.18)
    return jnp.clip(with_spikes(drawn, jax.random.fold_in(rng, 3), *heavy), -limit, limit).astype(dtype)


def setup_inputs(seed: int = 0) -> dict:
    key_list = jax.random.split(jax.random.key(seed), 11)
    return {
        "hidden_in": bell_draw_with(key_list[0], (TOKENS, D), 1.0, 24.0, ((0, 128),), (0, 1, 128, 5.5)),
        "mixer_weight": bell_draw(key_list[1], (D, 4 * D), D ** -0.5, 0.1875, ((0, 16),)),
        "output_weight": bell_draw(key_list[2], (D, D), D ** -0.5, 0.1875, ((0, 16),)),
        "gate_up_weight": bell_draw(key_list[3], (D, 2 * FF), D ** -0.5, 0.1875, ((0, 16),)),
        "down_weight": bell_draw(key_list[4], (FF, D), FF ** -0.5, 0.109375, ((0, 16),)),
        "mixer_norm_gain": jnp.clip(1.0 + 0.1 * jax.random.normal(key_list[5], (D,), jnp.float32), 0.5, 1.5).astype(jnp.bfloat16),
        "head_group_gain": jnp.clip(1.0 + 0.1 * jax.random.normal(key_list[6], (D,), jnp.float32), 0.5, 1.5).astype(jnp.bfloat16),
        "feedforward_gain": jnp.clip(1.0 + 0.1 * jax.random.normal(key_list[7], (D,), jnp.float32), 0.5, 1.5).astype(jnp.bfloat16),
        "forget_floor": draw_forget_floor(jax.random.fold_in(key_list[10], 71), 0),
        "out_grad": bell_draw(key_list[9], (TOKENS, D), 1.0, 6.0, ((0, 128),)),
    }


EPS = 1e-06
PRECISION_HIGH = lax.Precision.HIGHEST

@jax.custom_vjp
def lower_bound(v):
    return lax.optimization_barrier(v.astype(jnp.bfloat16)).astype(jnp.float32)

@jax.custom_vjp
def low_back(v):
    return v

def low_keep(v):
    return (lower_bound(v), None)

def low_pass(kept, grad):
    return (grad,)

def back_keep(v):
    return (v, None)

def back_low(kept, grad):
    return (lower_bound(grad),)
lower_bound.defvjp(low_keep, low_pass)
low_back.defvjp(back_keep, back_low)

def root_mean_scale(operand):
    return lax.rsqrt(lax.optimization_barrier(jnp.mean(operand * operand, axis=-1, keepdims=True)) + EPS)

def recurrence(query_rows, key_rows, rows_of_value, decay_rate):
    shape = (SEQS, LENGTH // BLOCK, BLOCK, HEADS, HEAD_DIM)

    def arrange(operand):
        return jnp.moveaxis(operand.reshape(shape), 0, 2)

    def token_step(carried_state, items):
        query_t, key_t, value_t, decay_t = items
        carried_state = decay_t[..., None] * carried_state + key_t[..., None] * value_t[..., None, :]
        return (carried_state, jnp.einsum('nhk,nhkv->nhv', query_t, carried_state, precision=PRECISION_HIGH))

    @jax.checkpoint
    def block_step(carried_state, items):
        return lax.scan(token_step, carried_state, items)
    state_zero = jnp.zeros((SEQS, HEADS, HEAD_DIM, HEAD_DIM), jnp.float32)
    inputs = (arrange(query_rows), arrange(key_rows), arrange(rows_of_value), arrange(decay_rate))
    _, layer_outputs = lax.scan(block_step, state_zero, inputs)
    return jnp.moveaxis(layer_outputs, 2, 0).reshape(TOKENS, D)

def layer(token_rows, mix_w, out_w, upgate_w, down_w, first_gain, gain_group, second_gain, floor_rate):
    first_scale = root_mean_scale(token_rows)
    first_centered = token_rows * first_scale
    input_normalized = lower_bound(first_centered * first_gain)
    projected_rows = low_back(jnp.dot(input_normalized, mix_w, precision=PRECISION_HIGH))
    query_pre = projected_rows[:, :D]
    forget_pre = projected_rows[:, D:2 * D]
    value_pre = projected_rows[:, 2 * D:3 * D]
    gate_preactivation = projected_rows[:, 3 * D:]
    decay_rate = floor_rate + (1.0 - floor_rate) * jax.nn.sigmoid(forget_pre)
    query_rows = lower_bound(jax.nn.silu(query_pre))
    key_rows = lower_bound(1.0 - decay_rate)
    rows_of_value = lower_bound(value_pre)
    mixer_out = recurrence(query_rows, key_rows, rows_of_value, decay_rate)
    heads_view = mixer_out.reshape(TOKENS, HEADS, HEAD_DIM)
    normalized_heads = (heads_view * root_mean_scale(heads_view)).reshape(TOKENS, D)
    output_normalized = lower_bound(normalized_heads * jax.nn.silu(gate_preactivation) * gain_group)
    branch_output = low_back(jnp.dot(output_normalized, out_w, precision=PRECISION_HIGH))
    middle_value = token_rows + branch_output
    second_centered = middle_value * root_mean_scale(middle_value)
    feedforward_normed = lower_bound(second_centered * second_gain)
    gate_and_up = low_back(jnp.dot(feedforward_normed, upgate_w, precision=PRECISION_HIGH))
    hidden_act = lower_bound(jax.nn.silu(gate_and_up[:, :FF]) * gate_and_up[:, FF:])
    ffn_out = low_back(jnp.dot(hidden_act, down_w, precision=PRECISION_HIGH))
    return middle_value + ffn_out

def reference(hidden_in, mixer_weight, output_weight, gate_up_weight, down_weight, mixer_norm_gain, head_group_gain, feedforward_gain, forget_floor, out_grad):
    primals = (hidden_in.astype(jnp.float32), mixer_weight.astype(jnp.float32), output_weight.astype(jnp.float32), gate_up_weight.astype(jnp.float32), down_weight.astype(jnp.float32), mixer_norm_gain.astype(jnp.float32), head_group_gain.astype(jnp.float32), feedforward_gain.astype(jnp.float32), forget_floor.astype(jnp.float32))
    result, pullback = jax.vjp(layer, *primals)
    grads = pullback(out_grad.astype(jnp.float32))
    return (result.astype(jnp.bfloat16), grads[0].astype(jnp.bfloat16), grads[1], grads[2], grads[3], grads[4], grads[5], grads[6], grads[7], grads[8])
```

```python
import functools

import jax
import jax.numpy as jnp
from jax import lax
from jax.experimental import pallas as pl
from jax.experimental.pallas import tpu as pltpu
from jax.sharding import Mesh, PartitionSpec as P

D = 1024
HEADS = 8
HEAD_DIM = 128
FF = 2816
EPS = 1e-06

ROWS = 128
PARTS = 4
COLS = D // PARTS
UNITS = FF // PARTS
PAD = 768
LOCAL_HEADS = 2
STATES = PARTS * LOCAL_HEADS
HALF = STATES // 2
TAIL = 16
BF = jnp.bfloat16
F32 = jnp.float32
AXES = ("yh", "z", "x", "yl", "c")
VMEM = 56 * 1024 * 1024


def shift(value, axis, by):
    n = lax.axis_size(axis)
    return lax.ppermute(value, axis, [(i, (i + by) % n) for i in range(n)])


def gather_z(own):
    return (own, shift(own, "z", 1), shift(own, "z", -1), shift(own, "z", 2))


def scatter_z(parts):
    return (parts[0], shift(parts[1], "z", -1), shift(parts[2], "z", 1), shift(parts[3], "z", 2))


def transpose_xz(value):
    pairs = [(z * 4 + x, x * 4 + z) for z in range(4) for x in range(4)]
    return lax.ppermute(value, ("z", "x"), pairs)


def exchange(value, axes):
    return lax.all_to_all(value, axes, 0, 0)


def spread(value, axes, n):
    return lax.all_to_all(jnp.broadcast_to(value, (n,) + value.shape), axes, 0, 0)


def kernel_call(body, out_shape, *args, scratch=(), flops=0):
    in_specs = [
        pl.BlockSpec(memory_space=pltpu.SMEM) if a.dtype == jnp.int32 else pl.BlockSpec(memory_space=pltpu.VMEM)
        for a in args
    ]
    out_specs = jax.tree.map(lambda _: pl.BlockSpec(memory_space=pltpu.VMEM), out_shape)
    size = sum(a.size * a.dtype.itemsize for a in args)
    size += sum(a.size * a.dtype.itemsize for a in jax.tree.leaves(out_shape))
    return pl.pallas_call(
        body,
        out_shape=out_shape,
        in_specs=in_specs,
        out_specs=out_specs,
        scratch_shapes=list(scratch),
        compiler_params=pltpu.CompilerParams(vmem_limit_bytes=VMEM),
        cost_estimate=pl.CostEstimate(flops=flops, bytes_accessed=size, transcendentals=0),
    )(*args)


def shape(dims, dtype):
    return jax.ShapeDtypeStruct(dims, dtype)


def dot(a, b):
    return jnp.dot(a, b, preferred_element_type=F32)


def dot_t(a, b):
    return lax.dot_general(a, b, (((1,), (1,)), ((), ())), preferred_element_type=F32)


def t_dot(a, b):
    return lax.dot_general(a, b, (((0,), (0,)), ((), ())), preferred_element_type=F32)


def exact_dot(a, b):
    return jnp.dot(a, b, precision=lax.Precision.HIGHEST, preferred_element_type=F32)


def mean_scale(value):
    return lax.rsqrt(jnp.mean(value * value, axis=-1, keepdims=True) + EPS)


def triangle(strict, upper):
    row = lax.broadcasted_iota(jnp.int32, (ROWS, ROWS), 0)
    col = lax.broadcasted_iota(jnp.int32, (ROWS, ROWS), 1)
    if upper:
        row, col = col, row
    return row > col if strict else row >= col


def swish_slope(value, sigma):
    return sigma * (1.0 + value * (1.0 - sigma))


def norm_kernel(x_ref, out_ref):
    x = x_ref[...].astype(F32)
    out_ref[...] = (x * mean_scale(x)).astype(BF)


def gated(pre, floor):
    sigma = lax.logistic(pre)
    return sigma, floor + (1.0 - floor) * sigma


def project_kernel(x0, x1, x2, x3, w_ref, floor_ref, x_ref, pre_ref, cum_ref, local_ref, state_ref, total_ref):
    for b, part in enumerate((x0, x1, x2, x3)):
        x_ref[b * ROWS : (b + 1) * ROWS, :] = part[...]
    for j in range(4):
        pre_ref[:, j * COLS : (j + 1) * COLS] = dot(x_ref[...], w_ref[:, j * COLS : (j + 1) * COLS])
    causal = triangle(False, False)
    ones = causal.astype(F32)
    floor = floor_ref[...]
    for b in range(PARTS):
        rows = slice(b * ROWS, (b + 1) * ROWS)
        _, decay = gated(pre_ref[rows, COLS : 2 * COLS], floor)
        cum_all = exact_dot(ones, jnp.log(decay))
        cum_ref[rows, :] = cum_all
        q_pre = pre_ref[rows, :COLS]
        query = (q_pre * lax.logistic(q_pre)).astype(BF).astype(F32)
        key = (1.0 - decay).astype(BF).astype(F32)
        value_all = pre_ref[rows, 2 * COLS : 3 * COLS].astype(BF)
        for h in range(LOCAL_HEADS):
            cols = slice(h * HEAD_DIM, (h + 1) * HEAD_DIM)
            cum = cum_all[:, cols]
            total = cum[ROWS - 1 :, :]
            value = value_all[:, cols]
            q_in = (query[:, cols] * jnp.exp(cum)).astype(BF)
            k_in = (key[:, cols] * jnp.exp(-cum)).astype(BF)
            k_out = (key[:, cols] * jnp.exp(total - cum)).astype(BF)
            scores = jnp.where(causal, dot_t(q_in, k_in), 0.0).astype(BF)
            local_ref[rows, cols] = dot(scores, value)
            s = h * PARTS + b
            state_ref[s] = t_dot(k_out, value).astype(BF)
            total_ref[s : s + 1, :] = total


def chip_kernel(core_ref, mine_ref, other_ref, my_total_ref, other_total_ref, out_ref, total_ref, *, backward):
    core = core_ref[0]
    second = core == (0 if backward else 1)
    base = core * HALF
    for i in range(HALF):
        mine = mine_ref[base + i].astype(F32)
        other = other_ref[base + i].astype(F32)
        my_total = my_total_ref[pl.ds(base + i, 1), :]
        other_total = other_total_ref[pl.ds(base + i, 1), :]
        total_ref[i : i + 1, :] = my_total + other_total
        last = jnp.where(second, mine, other)
        first = jnp.where(second, other, mine)
        last_decay = jnp.exp(jnp.where(second, my_total, other_total))
        out_ref[i] = (jnp.transpose(last_decay) * first + last).astype(BF)


def carry_kernel(place_ref, all_ref, totals_ref, out_ref, *, backward):
    place = place_ref[0]
    for i in range(HALF):
        carried = jnp.zeros((HEAD_DIM, HEAD_DIM), F32)
        for step in range(8):
            j = 7 - step if backward else step
            reached = j > place if backward else j < place
            decay = jnp.transpose(jnp.exp(totals_ref[j, i : i + 1, :]))
            carried = jnp.where(reached, decay * carried + all_ref[j, i].astype(F32), carried)
        out_ref[i] = carried.astype(BF)


def enter_state(core, own_half, other_half, other_end, other_total, s, backward):
    h, b = divmod(s, PARTS)
    chip = jnp.where(core == h, own_half[b], other_half[b]).astype(F32)
    later = core == (0 if backward else 1)
    passed = jnp.transpose(jnp.exp(other_total[s : s + 1, :])) * chip + other_end[s].astype(F32)
    return jnp.where(later, passed, chip)


def mix_kernel(core_ref, pre_ref, cum_ref, local_ref, own_half, other_half, other_end, other_total, w_ref,
               out_ref, normed_ref, entered_ref, p0, p1, p2, p3):
    core = core_ref[0]
    for b, part in enumerate((p0, p1, p2, p3)):
        rows = slice(b * ROWS, (b + 1) * ROWS)
        for h in range(LOCAL_HEADS):
            cols = slice(h * HEAD_DIM, (h + 1) * HEAD_DIM)
            s = h * PARTS + b
            state = enter_state(core, own_half, other_half, other_end, other_total, s, False).astype(BF)
            entered_ref[s] = state
            q_pre = pre_ref[rows, cols]
            query = (q_pre * lax.logistic(q_pre)).astype(BF).astype(F32)
            q_in = (query * jnp.exp(cum_ref[rows, cols])).astype(BF)
            mixed = local_ref[rows, cols] + dot(q_in, state)
            out_ref[rows, cols] = mixed
            gate = pre_ref[rows, 3 * COLS + h * HEAD_DIM : 3 * COLS + (h + 1) * HEAD_DIM]
            normed_ref[rows, cols] = (mixed * mean_scale(mixed) * (gate * lax.logistic(gate))).astype(BF)
    product = dot(normed_ref[...], w_ref[...]).astype(BF)
    for b, part in enumerate((p0, p1, p2, p3)):
        part[...] = product[b * ROWS : (b + 1) * ROWS, :]


def middle_kernel(hidden_ref, p0, p1, p2, p3, middle_ref, normed_ref):
    middle = hidden_ref[...].astype(F32) + (
        (p0[...].astype(F32) + p1[...].astype(F32)) + (p2[...].astype(F32) + p3[...].astype(F32))
    )
    middle_ref[...] = middle
    normed_ref[...] = (middle * mean_scale(middle)).astype(BF)


def feed_kernel(x0, x1, x2, x3, g0, g1, g2, g3, up_ref, down_ref, x_ref, g_ref, act_ref, grad_ref, p0, p1, p2, p3):
    for b, part in enumerate((x0, x1, x2, x3)):
        x_ref[b * ROWS : (b + 1) * ROWS, :] = part[...]
    for b, part in enumerate((g0, g1, g2, g3)):
        g_ref[b * ROWS : (b + 1) * ROWS, :] = part[...]
    for j in range(3):
        lanes = slice(j * COLS, (j + 1) * COLS)
        ups = slice(PAD + j * COLS, PAD + (j + 1) * COLS)
        gate = dot(x_ref[...], up_ref[:, lanes])
        up = dot(x_ref[...], up_ref[:, ups])
        grad = dot_t(g_ref[...], down_ref[lanes, :])
        sigma = lax.logistic(gate)
        swish = gate * sigma
        act_ref[:, lanes] = (swish * up).astype(BF)
        grad_ref[:, lanes] = (grad * up * swish_slope(gate, sigma)).astype(BF)
        grad_ref[:, ups] = (grad * swish).astype(BF)
    product = dot_t(grad_ref[...], up_ref[...]).astype(BF)
    for b, part in enumerate((p0, p1, p2, p3)):
        part[...] = product[b * ROWS : (b + 1) * ROWS, :]


def down_kernel(act_ref, down_ref, p0, p1, p2, p3):
    product = dot(act_ref[...], down_ref[...]).astype(BF)
    for b, part in enumerate((p0, p1, p2, p3)):
        part[...] = product[b * ROWS : (b + 1) * ROWS, :]


def result_kernel(middle_ref, p0, p1, p2, p3, out_ref):
    out_ref[...] = (
        middle_ref[...]
        + ((p0[...].astype(F32) + p1[...].astype(F32)) + (p2[...].astype(F32) + p3[...].astype(F32)))
    ).astype(BF)


def norm_back_kernel(value_ref, base_ref, p0, p1, p2, p3, out_ref, low_ref):
    value = value_ref[...].astype(F32)
    scale = mean_scale(value)
    centered = value * scale
    u = (p0[...].astype(F32) + p1[...].astype(F32)) + (p2[...].astype(F32) + p3[...].astype(F32))
    back = scale * (u - centered * jnp.mean(u * centered, axis=-1, keepdims=True))
    total = base_ref[...].astype(F32) + back
    if out_ref is not None:
        out_ref[...] = total
    low_ref[...] = total.astype(BF)


def last_kernel(value_ref, base_ref, p0, p1, p2, p3, low_ref):
    norm_back_kernel(value_ref, base_ref, p0, p1, p2, p3, None, low_ref)


def head_back_kernel(b0, b1, b2, b3, w_ref, pre_ref, cum_ref, mixed_ref, branch_ref, gate_ref, out_grad_ref, state_ref):
    for b, part in enumerate((b0, b1, b2, b3)):
        branch_ref[b * ROWS : (b + 1) * ROWS, :] = part[...]
    grads = dot_t(branch_ref[...], w_ref[...])
    for b in range(PARTS):
        rows = slice(b * ROWS, (b + 1) * ROWS)
        for h in range(LOCAL_HEADS):
            cols = slice(h * HEAD_DIM, (h + 1) * HEAD_DIM)
            grad = grads[rows, cols]
            mixed = mixed_ref[rows, cols]
            scale = mean_scale(mixed)
            normed = mixed * scale
            gate = pre_ref[rows, 3 * COLS + h * HEAD_DIM : 3 * COLS + (h + 1) * HEAD_DIM]
            sigma = lax.logistic(gate)
            gate_ref[rows, cols] = (grad * normed * swish_slope(gate, sigma)).astype(BF)
            c = grad * (gate * sigma)
            mixer = (scale * (c - normed * jnp.mean(c * normed, axis=-1, keepdims=True))).astype(BF)
            out_grad_ref[rows, cols] = mixer
            q_pre = pre_ref[rows, cols]
            query = (q_pre * lax.logistic(q_pre)).astype(BF).astype(F32)
            q_in = (query * jnp.exp(cum_ref[rows, cols])).astype(BF)
            state_ref[h * PARTS + b] = t_dot(q_in, mixer).astype(BF)


def recur_back_kernel(core_ref, pre_ref, cum_ref, floor_ref, gate_ref, out_grad_ref, entered_ref, own_half, other_half,
                      other_end, other_total, w_ref, grad_ref, floor_grad_ref, p0, p1, p2, p3):
    core = core_ref[0]
    causal = triangle(False, False)
    suffix = triangle(False, True).astype(F32)
    before = triangle(True, False).astype(F32)
    for h in range(LOCAL_HEADS):
        cols = slice(h * HEAD_DIM, (h + 1) * HEAD_DIM)
        floor = floor_ref[:, cols]
        floor_sum = jnp.zeros((1, HEAD_DIM), F32)
        for b in range(PARTS):
            rows = slice(b * ROWS, (b + 1) * ROWS)
            s = h * PARTS + b
            after = enter_state(core, own_half, other_half, other_end, other_total, s, True)
            after_low = after.astype(BF)
            state = entered_ref[s]
            q_pre = pre_ref[rows, cols]
            q_sigma = lax.logistic(q_pre)
            query = (q_pre * q_sigma).astype(BF).astype(F32)
            sigma, decay = gated(pre_ref[rows, COLS + h * HEAD_DIM : COLS + (h + 1) * HEAD_DIM], floor)
            key = (1.0 - decay).astype(BF).astype(F32)
            value = pre_ref[rows, 2 * COLS + h * HEAD_DIM : 2 * COLS + (h + 1) * HEAD_DIM].astype(BF)
            cum = cum_ref[rows, cols]
            total = cum[ROWS - 1 :, :]
            grow = jnp.exp(cum)
            shrink = jnp.exp(-cum)
            to_end = jnp.exp(total - cum)
            q_in = (query * grow).astype(BF)
            k_in = (key * shrink).astype(BF)
            k_out = (key * to_end).astype(BF)
            out_grad = out_grad_ref[rows, cols]
            scores = jnp.where(causal, dot_t(q_in, k_in), 0.0).astype(BF)
            grad_scores = jnp.where(causal, dot_t(out_grad, value), 0.0).astype(BF)
            inner = dot(grad_scores, k_in) + dot_t(out_grad, state)
            back = t_dot(grad_scores, q_in)
            ahead = dot_t(value, after_low)
            grad_query = inner * grow
            grad_key = back * shrink + ahead * to_end
            grad_value = t_dot(scores, out_grad) + dot(k_out, after_low)
            near = q_in.astype(F32) * inner - k_in.astype(F32) * back
            far = k_out.astype(F32) * ahead
            edge = jnp.sum(after * state.astype(F32), axis=1, keepdims=True)
            grad_log = exact_dot(suffix, near) + exact_dot(before, far) + jnp.exp(total) * jnp.transpose(edge)
            grad_decay = grad_log / decay - grad_key
            floor_sum = floor_sum + jnp.sum(grad_decay * (1.0 - sigma), axis=0, keepdims=True)
            grad_ref[rows, cols] = (grad_query * swish_slope(q_pre, q_sigma)).astype(BF)
            grad_ref[rows, COLS + h * HEAD_DIM : COLS + (h + 1) * HEAD_DIM] = (
                grad_decay * (1.0 - floor) * sigma * (1.0 - sigma)
            ).astype(BF)
            grad_ref[rows, 2 * COLS + h * HEAD_DIM : 2 * COLS + (h + 1) * HEAD_DIM] = grad_value.astype(BF)
        floor_grad_ref[:, cols] = floor_sum
    grad_ref[:, 3 * COLS :] = gate_ref[...]
    product = dot_t(grad_ref[...], w_ref[...]).astype(BF)
    for b, part in enumerate((p0, p1, p2, p3)):
        part[...] = product[b * ROWS : (b + 1) * ROWS, :]


def split3(value):
    first = value.astype(BF)
    rest = value - first.astype(F32)
    second = rest.astype(BF)
    third = (rest - second.astype(F32)).astype(BF)
    return first, second, third


def columns_to_owners(partial, core, rider=None):
    n = partial.shape[1]
    blocks = partial.reshape(8, 2, 64, n)
    mine = lax.dynamic_index_in_dim(blocks, core, 1, keepdims=False)
    other = lax.dynamic_index_in_dim(blocks, 1 - core, 1, keepdims=False)
    both = (mine.astype(F32) + shift(other, "c", 1).astype(F32)).astype(BF)
    both = both.reshape(16, 32, n)
    if rider is None:
        arrived = exchange(both, ("x", "yl", "yh"))
        return spread(jnp.sum(arrived.astype(F32), axis=0).astype(BF), ("yh", "z"), 8)

    def packed(value):
        row = jnp.concatenate([*split3(value), jnp.zeros((1, n - 3 * COLS), BF)], axis=1)
        return jnp.pad(row, ((0, 7), (0, 0)))

    def unpacked(rows):
        value = rows[:, 0, : 3 * COLS].reshape(-1, 3, COLS).astype(F32)
        return (value[:, 0] + value[:, 1]) + value[:, 2]

    rider = packed(rider + shift(rider, "c", 1))
    both = jnp.concatenate([both, jnp.broadcast_to(rider, (16, 8, n))], axis=1)
    arrived = exchange(both, ("x", "yl", "yh"))
    rider = packed(jnp.sum(unpacked(arrived[:, 32:]), axis=0, keepdims=True))
    total = jnp.sum(arrived[:, :32].astype(F32), axis=0).astype(BF)
    arrived = spread(jnp.concatenate([total, rider], axis=0), ("yh", "z"), 8)
    return arrived[:, :32], unpacked(arrived[:PARTS, 32:]).reshape(D)


def body(hidden, mixer_weight, output_weight, gate_up_weight, down_weight, mixer_gain, group_gain, feed_gain,
         forget_floor, out_grad):
    z = lax.axis_index("z")
    c = lax.axis_index("c")
    yl = lax.axis_index("yl")
    x = lax.axis_index("x")
    core = c.reshape(1).astype(jnp.int32)
    place = (x * 2 + yl).reshape(1).astype(jnp.int32)
    gain_one = mixer_gain.astype(F32)[:, None]
    gain_group = group_gain.astype(F32)[:, None]
    gain_two = feed_gain.astype(F32)[:, None]
    floor = lax.dynamic_index_in_dim(forget_floor.reshape(PARTS, COLS), z, 0)

    mixer_cols = lax.dynamic_index_in_dim(mixer_weight.reshape(64, 4, PARTS, COLS), z, 2, keepdims=False)
    mixer_cols = (mixer_cols.reshape(64, 4 * COLS).astype(F32) * gain_one).astype(BF)
    halves = lax.dynamic_index_in_dim(gate_up_weight.reshape(64, 2, PARTS, UNITS), z, 2, keepdims=False)
    halves = (halves.astype(F32) * gain_two[:, :, None]).astype(BF)
    up_cols = jnp.pad(halves, ((0, 0), (0, 0), (0, PAD - UNITS))).reshape(64, 2 * PAD)
    row_block = jnp.concatenate([down_weight, (output_weight.astype(F32) * gain_group).astype(BF)], axis=0)

    normed_own = kernel_call(norm_kernel, shape((ROWS, D), BF), hidden)
    normed = gather_z(normed_own)
    w_mix = lax.all_gather(mixer_cols, ("x", "yl", "c"), axis=0, tiled=True)

    row_mine = transpose_xz(row_block)
    row_yl = shift(row_mine, "yl", 1)
    pair = jnp.stack([jnp.where(yl == 0, row_mine, row_yl), jnp.where(yl == 0, row_yl, row_mine)])
    pair_other = shift(pair, "c", 1)
    rows_all = jnp.stack([jnp.where(c == 0, pair, pair_other), jnp.where(c == 0, pair_other, pair)], axis=1)
    w_down = jnp.pad(rows_all[:, :, :176].reshape(UNITS, D), ((0, PAD - UNITS), (0, 0)))
    w_out = rows_all[:, :, 176:].reshape(COLS, D)
    w_up = lax.all_gather(up_cols, ("x", "yl", "c"), axis=0, tiled=True)
    grads_out = gather_z(out_grad)

    tokens = PARTS * ROWS
    x_all, pre, cum, local_out, end, total = kernel_call(
        project_kernel,
        (
            shape((tokens, D), BF),
            shape((tokens, D), F32),
            shape((tokens, COLS), F32),
            shape((tokens, COLS), F32),
            shape((STATES, HEAD_DIM, HEAD_DIM), BF),
            shape((STATES, HEAD_DIM), F32),
        ),
        *normed, w_mix, floor,
        flops=2 * tokens * D * D,
    )

    def pass_state(end_state, other_total, totals, backward):
        other_end = shift(end_state, "c", 1)
        chip_state, chip_total = kernel_call(
            functools.partial(chip_kernel, backward=backward),
            (shape((HALF, HEAD_DIM, HEAD_DIM), BF), shape((HALF, HEAD_DIM), F32)),
            core, end_state, other_end, total, other_total,
        )
        if totals is None:
            packed = jnp.concatenate([*split3(chip_total), jnp.zeros((TAIL - 3 * HALF, HEAD_DIM), BF)], axis=0)
            payload = jnp.concatenate([chip_state.reshape(HALF * HEAD_DIM, HEAD_DIM), packed], axis=0)
            arrived = spread(payload, ("x", "yl"), 8)
            states = arrived[:, : HALF * HEAD_DIM].reshape(8, HALF, HEAD_DIM, HEAD_DIM)
            packed = arrived[:, HALF * HEAD_DIM :].astype(F32)
            totals = packed[:, :HALF] + packed[:, HALF : 2 * HALF] + packed[:, 2 * HALF : 3 * HALF]
        else:
            states = spread(chip_state, ("x", "yl"), 8)
        own_half = kernel_call(
            functools.partial(carry_kernel, backward=backward),
            shape((HALF, HEAD_DIM, HEAD_DIM), BF),
            place, states, totals,
        )
        return own_half, shift(own_half, "c", 1), other_end, totals

    other_total = shift(total, "c", 1)
    own_half, other_half, other_end, totals = pass_state(end, other_total, None, False)
    mixed, normed_out, entered, *parts = kernel_call(
        mix_kernel,
        (
            shape((tokens, COLS), F32),
            shape((tokens, COLS), BF),
            shape((STATES, HEAD_DIM, HEAD_DIM), BF),
            *[shape((ROWS, D), BF)] * 4,
        ),
        core, pre, cum, local_out, own_half, other_half, other_end, other_total, w_out,
        flops=2 * tokens * COLS * D,
    )
    middle, feed_own = kernel_call(
        middle_kernel, (shape((ROWS, D), F32), shape((ROWS, D), BF)), hidden, *scatter_z(parts)
    )
    f_all, g_all, act, grad_up, *parts = kernel_call(
        feed_kernel,
        (
            shape((tokens, D), BF),
            shape((tokens, D), BF),
            shape((tokens, PAD), BF),
            shape((tokens, 2 * PAD), BF),
            *[shape((ROWS, D), BF)] * 4,
        ),
        *gather_z(feed_own), *grads_out, w_up, w_down,
        flops=2 * tokens * D * PAD * 5,
    )
    feed_back = scatter_z(parts)
    grad_middle, branch_own = kernel_call(
        norm_back_kernel, (shape((ROWS, D), F32), shape((ROWS, D), BF)), middle, out_grad, *feed_back
    )
    branch = gather_z(branch_own)
    branch_all, grad_gate, grad_mixed, end_grad = kernel_call(
        head_back_kernel,
        (
            shape((tokens, D), BF),
            shape((tokens, COLS), BF),
            shape((tokens, COLS), BF),
            shape((STATES, HEAD_DIM, HEAD_DIM), BF),
        ),
        *branch, w_out, pre, cum, mixed,
        flops=2 * tokens * COLS * D,
    )
    own_half, other_half, other_end, _ = pass_state(end_grad, other_total, totals, True)

    down_parts = kernel_call(
        down_kernel, tuple([shape((ROWS, D), BF)] * 4), act, w_down, flops=2 * tokens * D * PAD
    )
    result = kernel_call(result_kernel, shape((ROWS, D), BF), middle, *scatter_z(down_parts))
    up_sum = columns_to_owners(t_dot(f_all, grad_up).astype(BF), c)
    down_partial = t_dot(act, g_all).astype(BF)[:UNITS].reshape(2, 2, 176, D)
    out_partial = t_dot(normed_out, branch_all).astype(BF).reshape(2, 2, 64, D)
    row_partial = jnp.concatenate([down_partial, out_partial], axis=2)
    mine = lax.dynamic_index_in_dim(row_partial, c, 1, keepdims=False)
    other = lax.dynamic_index_in_dim(row_partial, 1 - c, 1, keepdims=False)
    both = (mine.astype(F32) + shift(other, "c", 1).astype(F32)).astype(BF)
    mine = lax.dynamic_index_in_dim(both, yl, 0, keepdims=False)
    other = lax.dynamic_index_in_dim(both, 1 - yl, 0, keepdims=False)
    both = (mine.astype(F32) + shift(other, "yl", 1).astype(F32)).astype(BF)
    both = transpose_xz(both)
    both = jnp.pad(both, ((0, 16), (0, 0))).reshape(8, 32, D)
    row_sum = jnp.sum(exchange(both, ("yh", "z")).astype(F32), axis=0).astype(BF)
    row_sum = spread(row_sum, ("yh", "z"), 8).reshape(256, D).astype(F32)

    grad_pre, floor_part, *parts = kernel_call(
        recur_back_kernel,
        (shape((tokens, D), BF), shape((1, COLS), F32), *[shape((ROWS, D), BF)] * 4),
        core, pre, cum, floor, grad_gate, grad_mixed, entered, own_half, other_half, other_end, other_total, w_mix,
        flops=2 * tokens * D * D,
    )
    grad_tokens = kernel_call(last_kernel, shape((ROWS, D), BF), hidden, grad_middle, *scatter_z(parts))
    mix_partial = t_dot(x_all, grad_pre).astype(BF)
    mix_sum, floor_grad = columns_to_owners(mix_partial, c, floor_part)

    def columns(gathered, width, valid):
        groups = gathered.shape[2] // width
        value = gathered.astype(F32).reshape(2, PARTS, 32, groups, width)[..., :valid]
        return jnp.transpose(value, (0, 2, 3, 1, 4)).reshape(64, groups * PARTS * valid)

    mix = columns(mix_sum, COLS, COLS)
    up = columns(up_sum, PAD, UNITS)
    down = row_sum[:176]
    out = row_sum[176:240]
    return (
        result,
        grad_tokens,
        mix * gain_one,
        out * gain_group,
        up * gain_two,
        down,
        jnp.sum(mix * mixer_weight.astype(F32), axis=1),
        jnp.sum(out * output_weight.astype(F32), axis=1),
        jnp.sum(up * gate_up_weight.astype(F32), axis=1),
        floor_grad,
    )


def solution(mesh):
    cut = Mesh(mesh.devices.reshape(2, 4, 4, 2, 2), AXES)
    seq = ("x", "yl", "c")
    rows, weight, vector = P(AXES, None), P(seq, None), P(seq)
    in_specs = (rows, weight, weight, weight, weight, vector, vector, vector, P(), rows)
    out_specs = (rows, rows, weight, weight, weight, weight, vector, vector, vector, P())
    return jax.shard_map(body, mesh=cut, in_specs=in_specs, out_specs=out_specs, check_vma=False)
```

```python
import functools

import jax
import jax.numpy as jnp
from jax import lax
from jax.experimental import pallas as pl
from jax.experimental.pallas import tpu as pltpu
from jax.sharding import Mesh, PartitionSpec as P

D = 1024
HEADS = 8
HEAD_DIM = 128
FF = 2816
EPS = 1e-06

ROWS = 128
PARTS = 4
COLS = D // PARTS
TOKENS = PARTS * ROWS
WIDE = 2 * COLS
PAD = 768
SLOT, TAKEN, OWNED = 48, 44, 176
SLOTS, UNITS = 8 * SLOT, 8 * OWNED
FEED_ROWS = 96
LOCAL_HEADS = 2
STATES = PARTS * LOCAL_HEADS
HALF = STATES // 2
TAIL = 16
BF = jnp.bfloat16
F32 = jnp.float32
AXES = ("yh", "z", "x", "yl", "c")
VMEM = 56 * 1024 * 1024


def shift(value, axis, by):
    n = lax.axis_size(axis)
    return lax.ppermute(value, axis, [(i, (i + by) % n) for i in range(n)])


def gather_z(own):
    return (own, shift(own, "z", 1), shift(own, "z", -1), shift(own, "z", 2))


def scatter_z(parts):
    return (parts[0], shift(parts[1], "z", -1), shift(parts[2], "z", 1), shift(parts[3], "z", 2))


def from_owner(value):
    x, z = lax.axis_index("x"), lax.axis_index("z")
    got = value
    for k in range(1, 4):
        pairs = [(i * 4 + i, i * 4 + (i + k) % 4) for i in range(4)]
        got = jnp.where(x == (z + k) % 4, lax.ppermute(value, ("z", "x"), pairs), got)
    return got


def four_rows(value):
    mine = from_owner(value)
    neighbour = shift(mine, "yl", 1)
    return mine, neighbour, shift(mine, "c", 1), shift(neighbour, "c", 1)


def transpose_xz(value):
    pairs = [(z * 4 + x, x * 4 + z) for z in range(4) for x in range(4)]
    return lax.ppermute(value, ("z", "x"), pairs)


def exchange(value, axes):
    return lax.all_to_all(value, axes, 0, 0)


def after(value, *others):
    return lax.optimization_barrier((value, *others))[0]


def kernel_call(body, out_shape, *args, scratch=(), flops=0, order=()):
    if order:
        args = after(args, *order)
    in_specs = [
        pl.BlockSpec(memory_space=pltpu.SMEM) if a.dtype == jnp.int32 else pl.BlockSpec(memory_space=pltpu.VMEM)
        for a in args
    ]
    out_specs = jax.tree.map(lambda _: pl.BlockSpec(memory_space=pltpu.VMEM), out_shape)
    size = sum(a.size * a.dtype.itemsize for a in args)
    size += sum(a.size * a.dtype.itemsize for a in jax.tree.leaves(out_shape))
    return pl.pallas_call(
        body,
        out_shape=out_shape,
        in_specs=in_specs,
        out_specs=out_specs,
        scratch_shapes=list(scratch),
        compiler_params=pltpu.CompilerParams(vmem_limit_bytes=VMEM),
        cost_estimate=pl.CostEstimate(flops=flops, bytes_accessed=size, transcendentals=0),
    )(*args)


def shape(dims, dtype):
    return jax.ShapeDtypeStruct(dims, dtype)


def dot(a, b):
    return jnp.dot(a, b, preferred_element_type=F32)


def dot_t(a, b):
    return lax.dot_general(a, b, (((1,), (1,)), ((), ())), preferred_element_type=F32)


def t_dot(a, b):
    return lax.dot_general(a, b, (((0,), (0,)), ((), ())), preferred_element_type=F32)


def exact_dot(a, b):
    return jnp.dot(a, b, precision=lax.Precision.HIGHEST, preferred_element_type=F32)


def mean_scale(value):
    return lax.rsqrt(jnp.mean(value * value, axis=-1, keepdims=True) + EPS)


def triangle(strict, upper):
    row = lax.broadcasted_iota(jnp.int32, (ROWS, ROWS), 0)
    col = lax.broadcasted_iota(jnp.int32, (ROWS, ROWS), 1)
    if upper:
        row, col = col, row
    return row > col if strict else row >= col


def swish_slope(value, sigma):
    return sigma * (1.0 + value * (1.0 - sigma))


def norm_kernel(x_ref, out_ref):
    x = x_ref[...].astype(F32)
    out_ref[...] = (x * mean_scale(x)).astype(BF)


def column(ref):
    return jnp.transpose(ref[...].astype(F32))


def row_sums(value):
    return jnp.sum(jnp.transpose(value), axis=0, keepdims=True)


def lane_blocks(value):
    total = value[:, :128]
    for j in range(128, value.shape[1], 128):
        total = total + value[:, j : j + 128]
    return total


def prepare_kernel(z_ref, w_ref, gain_ref, fv_ref, qg_ref):
    start = z_ref[0] * COLS
    gain = column(gain_ref)

    def block(j):
        cols = pl.ds(pl.multiple_of(j * D + start, 128), COLS)
        return (w_ref[:, cols].astype(F32) * gain).astype(BF)

    forget, value = block(1), block(2)
    for i in range(8):
        fv_ref[i, :, :COLS] = forget
        fv_ref[i, :, COLS:] = value
    qg_ref[:, :COLS] = block(0)
    qg_ref[:, COLS:] = block(3)


def selection(z, slots, units, slots_first):
    shape_ = (slots, units) if slots_first else (units, slots)
    line = (slots, 1) if slots_first else (1, slots)
    slot = lax.broadcasted_iota(jnp.int32, line, 0 if slots_first else 1)
    owner = jnp.zeros(line, jnp.int32)
    for i in range(1, slots // SLOT):
        owner = owner + (slot >= i * SLOT).astype(jnp.int32)
    place = slot - owner * SLOT
    unit = jnp.where(place < TAKEN, owner * OWNED + z * TAKEN + place, -1)
    return jnp.where(lax.broadcasted_iota(jnp.int32, shape_, 1 if slots_first else 0) == unit, 1.0, 0.0).astype(BF)


def prepare_feed_kernel(z_ref, up_ref, gain_ref, down_ref, out_ref):
    gain = column(gain_ref)
    chosen = selection(z_ref[0], SLOTS, UNITS, False)
    for i in range(4):
        picked = dot(up_ref[:, i * UNITS : (i + 1) * UNITS], chosen)
        out_ref[:64, i * SLOTS : (i + 1) * SLOTS] = (picked * gain).astype(BF)
    rows = dot(selection(z_ref[0], SLOT, OWNED, True), down_ref[...]).astype(BF)
    out_ref[64:, :D] = rows[:32]
    out_ref[64:80, D:] = rows[32:, :512]
    out_ref[80:, D:] = rows[32:, 512:]


def gated(pre, floor):
    sigma = lax.logistic(pre)
    return sigma, floor + (1.0 - floor) * sigma


def swish(value):
    return value * lax.logistic(value)


def head_cols(h):
    return slice(h * HEAD_DIM, (h + 1) * HEAD_DIM)


def part_rows(b):
    return slice(b * ROWS, (b + 1) * ROWS)


def first_kernel(core_ref, x0, x1, x2, x3, mine_ref, other_ref, floor_ref,
                 x_ref, w_ref, pre_ref, cum_ref, state_ref, total_ref):
    core = core_ref[0]
    w_ref[:, pl.ds(core, 1)] = mine_ref[...].reshape(8, 1, 64, WIDE)
    w_ref[:, pl.ds(1 - core, 1)] = other_ref[...].reshape(8, 1, 64, WIDE)
    for b, part in enumerate((x0, x1, x2, x3)):
        x_ref[part_rows(b), :] = part[...]
    pre_ref[...] = dot(x_ref[...], w_ref[...].reshape(D, WIDE))
    ones = triangle(False, False).astype(F32)
    floor = floor_ref[...]
    for b in range(PARTS):
        rows = part_rows(b)
        _, decay = gated(pre_ref[rows, :COLS], floor)
        cum_all = exact_dot(ones, jnp.log(decay))
        cum_ref[rows, :] = cum_all
        total_all = cum_all[ROWS - 1 :, :]
        k_out = ((1.0 - decay).astype(BF).astype(F32) * jnp.exp(total_all - cum_all)).astype(BF)
        for h in range(LOCAL_HEADS):
            value = pre_ref[rows, COLS + h * HEAD_DIM : COLS + (h + 1) * HEAD_DIM].astype(BF)
            s = h * PARTS + b
            state_ref[s] = t_dot(k_out[:, head_cols(h)], value).astype(BF)
            total_ref[s : s + 1, :] = total_all[:, head_cols(h)]


def second_kernel(x_ref, w_ref, fv_ref, cum_ref, floor_ref, pre_ref, q_ref, local_ref):
    pre_ref[...] = dot(x_ref[...], w_ref[...])
    causal = triangle(False, False)
    floor = floor_ref[...]
    for b in range(PARTS):
        rows = part_rows(b)
        _, decay = gated(fv_ref[rows, :COLS], floor)
        cum = cum_ref[rows, :]
        k_in = ((1.0 - decay).astype(BF).astype(F32) * jnp.exp(-cum)).astype(BF)
        q_in = (swish(pre_ref[rows, :COLS]).astype(BF).astype(F32) * jnp.exp(cum)).astype(BF)
        q_ref[rows, :] = q_in
        value = fv_ref[rows, COLS:].astype(BF)
        for h in range(LOCAL_HEADS):
            cols = head_cols(h)
            scores = jnp.where(causal, dot_t(q_in[:, cols], k_in[:, cols]), 0.0).astype(BF)
            local_ref[rows, cols] = dot(scores, value[:, cols])


def split3(value):
    first = value.astype(BF).astype(F32)
    second = (value - first).astype(BF).astype(F32)
    return first, second, value - first - second


def chip_kernel(core_ref, mine_ref, other_ref, my_total_ref, other_total_ref, out_ref, *, backward):
    core = core_ref[0]
    second = core == (0 if backward else 1)
    base = core * HALF
    my_total = my_total_ref[pl.ds(base, HALF), :]
    other_total = other_total_ref[pl.ds(base, HALF), :]
    last_decay = jnp.exp(jnp.where(second, my_total, other_total))
    for i in range(HALF):
        mine = mine_ref[base + i].astype(F32)
        other = other_ref[base + i].astype(F32)
        last = jnp.where(second, mine, other)
        first = jnp.where(second, other, mine)
        state = (jnp.transpose(last_decay[i : i + 1, :]) * first + last).astype(BF)
        for d in range(8):
            out_ref[d, i * HEAD_DIM : (i + 1) * HEAD_DIM, :] = state
    if not backward:
        pieces = split3(my_total + other_total)
        tail = jnp.concatenate([*pieces, jnp.zeros((HALF, HEAD_DIM), F32)], axis=0).astype(BF)
        for d in range(8):
            out_ref[d, HALF * HEAD_DIM :, :] = tail


def carry_kernel(place_ref, all_ref, *refs, backward):
    place = place_ref[0]
    if backward:
        totals_ref, out_ref = refs
    else:
        out_ref, totals_ref = refs
        for j in range(8):
            tail = all_ref[j, HALF * HEAD_DIM :, :].astype(F32)
            totals_ref[j] = (tail[:HALF] + tail[HALF : 2 * HALF]) + tail[2 * HALF : 3 * HALF]
    for i in range(HALF):
        carried = jnp.zeros((HEAD_DIM, HEAD_DIM), F32)
        decays = jnp.transpose(jnp.exp(jnp.concatenate([totals_ref[j, i : i + 1, :] for j in range(8)], axis=0)))
        for step in range(7):
            j = 7 - step if backward else step
            reached = j > place if backward else j < place
            block = all_ref[j, i * HEAD_DIM : (i + 1) * HEAD_DIM, :].astype(F32)
            carried = jnp.where(reached, decays[:, j : j + 1] * carried + block, carried)
        out_ref[i] = carried.astype(BF)


def enter_state(core, own_half, other_half, other_end, other_total, s, backward):
    h, b = divmod(s, PARTS)
    chip = jnp.where(core == h, own_half[b], other_half[b]).astype(F32)
    later = core == (0 if backward else 1)
    passed = jnp.transpose(jnp.exp(other_total[s : s + 1, :])) * chip + other_end[s].astype(F32)
    return jnp.where(later, passed, chip)


def gather_rows(core, yl, pieces, out_ref, rows):
    for i, piece in enumerate(pieces):
        at = (yl if i % 2 == 0 else 1 - yl) * 2 + (core if i < 2 else 1 - core)
        out_ref[pl.ds(at, 1)] = piece[...].reshape(1, rows, D)


def mix_kernel(core_ref, yl_ref, pre_ref, q_ref, local_ref, own_half, other_half, other_end, other_total,
               r0, r1, r2, r3, out_ref, normed_ref, entered_ref, w_ref, p0, p1, p2, p3):
    core = core_ref[0]
    gather_rows(core, yl_ref[0], (r0, r1, r2, r3), w_ref, 64)
    for b in range(PARTS):
        rows = part_rows(b)
        for h in range(LOCAL_HEADS):
            cols = head_cols(h)
            s = h * PARTS + b
            state = enter_state(core, own_half, other_half, other_end, other_total, s, False).astype(BF)
            entered_ref[s] = state
            mixed = local_ref[rows, cols] + dot(q_ref[rows, cols], state)
            out_ref[rows, cols] = mixed
            gate = pre_ref[rows, COLS + h * HEAD_DIM : COLS + (h + 1) * HEAD_DIM]
            normed_ref[rows, cols] = (mixed * mean_scale(mixed) * swish(gate)).astype(BF)
    product = dot(normed_ref[...], w_ref[...].reshape(COLS, D)).astype(BF)
    for b, part in enumerate((p0, p1, p2, p3)):
        part[...] = product[part_rows(b), :]


def sum_parts(p0, p1, p2, p3):
    return (p0[...].astype(F32) + p1[...].astype(F32)) + (p2[...].astype(F32) + p3[...].astype(F32))


def middle_kernel(hidden_ref, p0, p1, p2, p3, middle_ref, normed_ref):
    middle = hidden_ref[...].astype(F32) + sum_parts(p0, p1, p2, p3)
    middle_ref[...] = middle
    normed_ref[...] = (middle * mean_scale(middle)).astype(BF)


def feed_kernel(x0, x1, x2, x3, g0, g1, g2, g3, w_ref, x_ref, g_ref, act_ref, grad_ref, down_ref, p0, p1, p2, p3):
    for s in range(16):
        at = s * SLOT
        down_ref[at : at + 32, :] = w_ref[s, 64:, :D]
        down_ref[at + 32 : at + 48, :512] = w_ref[s, 64:80, D:]
        down_ref[at + 32 : at + 48, 512:] = w_ref[s, 80:, D:]
    for b, part in enumerate((x0, x1, x2, x3)):
        x_ref[part_rows(b), :] = part[...]
    for b, part in enumerate((g0, g1, g2, g3)):
        g_ref[part_rows(b), :] = part[...]
    for j in range(3):
        lanes = slice(j * COLS, (j + 1) * COLS)
        ups = slice(PAD + j * COLS, PAD + (j + 1) * COLS)
        gate = dot(x_ref[...], w_ref[:, :64, lanes].reshape(D, COLS))
        up = dot(x_ref[...], w_ref[:, :64, ups].reshape(D, COLS))
        grad = dot_t(g_ref[...], down_ref[lanes, :])
        sigma = lax.logistic(gate)
        active = gate * sigma
        act_ref[:, lanes] = (active * up).astype(BF)
        grad_ref[:, lanes] = (grad * up * swish_slope(gate, sigma)).astype(BF)
        grad_ref[:, ups] = (grad * active).astype(BF)
    product = dot_t(grad_ref[...], w_ref[:, :64, :].reshape(D, 2 * PAD)).astype(BF)
    for b, part in enumerate((p0, p1, p2, p3)):
        part[...] = product[part_rows(b), :]


def feed_grad_kernel(x_ref, grad_ref, act_ref, g_ref, out_ref):
    for j in range(0, 2 * PAD, 512):
        out_ref[:, :64, j : j + 512] = t_dot(x_ref[...], grad_ref[:, j : j + 512]).astype(BF).reshape(16, 64, 512)
    rows = t_dot(act_ref[...], g_ref[...]).astype(BF)
    for s in range(16):
        at = s * SLOT
        out_ref[s, 64:, :D] = rows[at : at + 32]
        out_ref[s, 64:80, D:] = rows[at + 32 : at + 48, :512]
        out_ref[s, 80:, D:] = rows[at + 32 : at + 48, 512:]


def add_kernel(a_ref, b_ref, out_ref):
    out_ref[...] = (a_ref[...].astype(F32) + b_ref[...].astype(F32)).astype(BF)


def down_kernel(act_ref, down_ref, p0, p1, p2, p3):
    product = dot(act_ref[...], down_ref[...]).astype(BF)
    for b, part in enumerate((p0, p1, p2, p3)):
        part[...] = product[part_rows(b), :]


def result_kernel(middle_ref, p0, p1, p2, p3, out_ref):
    out_ref[...] = (middle_ref[...] + sum_parts(p0, p1, p2, p3)).astype(BF)


def norm_back(value_ref, base_ref, parts):
    value = value_ref[...].astype(F32)
    scale = mean_scale(value)
    centered = value * scale
    u = sum_parts(*parts)
    back = scale * (u - centered * jnp.mean(u * centered, axis=-1, keepdims=True))
    return base_ref[...].astype(F32) + back


def branch_kernel(value_ref, base_ref, p0, p1, p2, p3, out_ref, low_ref):
    total = norm_back(value_ref, base_ref, (p0, p1, p2, p3))
    out_ref[...] = total
    low_ref[...] = total.astype(BF)


def last_kernel(value_ref, base_ref, p0, p1, p2, p3, low_ref):
    low_ref[...] = norm_back(value_ref, base_ref, (p0, p1, p2, p3)).astype(BF)


def head_back_kernel(b0, b1, b2, b3, w_ref, pre_ref, q_ref, mixed_ref, branch_ref, gate_ref, out_grad_ref, state_ref):
    for b, part in enumerate((b0, b1, b2, b3)):
        branch_ref[part_rows(b), :] = part[...]
    grads = dot_t(branch_ref[...], w_ref[...].reshape(COLS, D))
    for b in range(PARTS):
        rows = part_rows(b)
        for h in range(LOCAL_HEADS):
            cols = head_cols(h)
            grad = grads[rows, cols]
            mixed = mixed_ref[rows, cols]
            scale = mean_scale(mixed)
            normed = mixed * scale
            gate = pre_ref[rows, COLS + h * HEAD_DIM : COLS + (h + 1) * HEAD_DIM]
            sigma = lax.logistic(gate)
            gate_ref[rows, cols] = (grad * normed * swish_slope(gate, sigma)).astype(BF)
            c = grad * (gate * sigma)
            mixer = (scale * (c - normed * jnp.mean(c * normed, axis=-1, keepdims=True))).astype(BF)
            out_grad_ref[rows, cols] = mixer
            state_ref[h * PARTS + b] = t_dot(q_ref[rows, cols], mixer).astype(BF)


def near_back_kernel(qg_ref, fv_ref, cum_ref, floor_ref, q_ref, gate_ref, out_grad_ref, entered_ref,
                     grad_ref, log_ref, key_ref, value_ref):
    causal = triangle(False, False)
    suffix = triangle(False, True).astype(F32)
    floor = floor_ref[...]
    for b in range(PARTS):
        rows = part_rows(b)
        _, decay = gated(fv_ref[rows, :COLS], floor)
        cum = cum_ref[rows, :]
        grow_all = jnp.exp(cum)
        shrink_all = jnp.exp(-cum)
        k_all = ((1.0 - decay).astype(BF).astype(F32) * shrink_all).astype(BF)
        q_pre = qg_ref[rows, :COLS]
        slope_all = swish_slope(q_pre, lax.logistic(q_pre))
        for h in range(LOCAL_HEADS):
            cols = head_cols(h)
            value = fv_ref[rows, COLS + h * HEAD_DIM : COLS + (h + 1) * HEAD_DIM].astype(BF)
            q_in, k_in = q_ref[rows, cols], k_all[:, cols]
            out_grad = out_grad_ref[rows, cols]
            scores = jnp.where(causal, dot_t(q_in, k_in), 0.0).astype(BF)
            grad_scores = jnp.where(causal, dot_t(out_grad, value), 0.0).astype(BF)
            inner = dot(grad_scores, k_in) + dot_t(out_grad, entered_ref[h * PARTS + b])
            back = t_dot(grad_scores, q_in)
            near = q_in.astype(F32) * inner - k_in.astype(F32) * back
            log_ref[rows, cols] = exact_dot(suffix, near)
            key_ref[rows, cols] = back * shrink_all[:, cols]
            value_ref[rows, cols] = t_dot(scores, out_grad)
            grad_ref[rows, cols] = (inner * grow_all[:, cols] * slope_all[:, cols]).astype(BF)
    grad_ref[:, COLS:] = gate_ref[...]


def far_back_kernel(core_ref, fv_ref, cum_ref, floor_ref, log_ref, key_ref, value_ref, entered_ref, own_half, other_half,
                    other_end, other_total, qg_ref, w_fv_ref, w_qg_ref, grad_ref, floor_grad_ref, p0, p1, p2, p3):
    core = core_ref[0]
    before = triangle(True, False).astype(F32)
    floor = floor_ref[...]
    floor_sum = jnp.zeros((1, COLS), F32)
    for b in range(PARTS):
        rows = part_rows(b)
        sigma, decay = gated(fv_ref[rows, :COLS], floor)
        cum = cum_ref[rows, :]
        total = cum[ROWS - 1 :, :]
        to_end = jnp.exp(total - cum)
        k_all = ((1.0 - decay).astype(BF).astype(F32) * to_end).astype(BF)
        aheads, edges = [], []
        for h in range(LOCAL_HEADS):
            cols = head_cols(h)
            s = h * PARTS + b
            following = enter_state(core, own_half, other_half, other_end, other_total, s, True)
            low = following.astype(BF)
            value = fv_ref[rows, COLS + h * HEAD_DIM : COLS + (h + 1) * HEAD_DIM].astype(BF)
            aheads.append(dot_t(value, low))
            edges.append(jnp.transpose(jnp.sum(following * entered_ref[s].astype(F32), axis=1, keepdims=True)))
            grad_value = value_ref[rows, cols] + dot(k_all[:, cols], low)
            grad_ref[rows, COLS + h * HEAD_DIM : COLS + (h + 1) * HEAD_DIM] = grad_value.astype(BF)
        ahead = jnp.concatenate(aheads, axis=1)
        edge = jnp.concatenate(edges, axis=1)
        far = exact_dot(before, k_all.astype(F32) * ahead)
        grad_log = log_ref[rows, :] + far + jnp.exp(total) * edge
        grad_decay = grad_log / decay - (key_ref[rows, :] + ahead * to_end)
        floor_sum = floor_sum + jnp.sum(grad_decay * (1.0 - sigma), axis=0, keepdims=True)
        grad_ref[rows, :COLS] = (grad_decay * (1.0 - floor) * sigma * (1.0 - sigma)).astype(BF)
    floor_grad_ref[...] = floor_sum
    product = dot_t(grad_ref[...], w_fv_ref[...]) + dot_t(qg_ref[...], w_qg_ref[...])
    product = product.astype(BF)
    for b, part in enumerate((p0, p1, p2, p3)):
        part[...] = product[part_rows(b), :]


def column_grad_kernel(core_ref, a_ref, g_ref, mine_ref, other_ref, all_ref):
    core = core_ref[0]
    n = g_ref.shape[1]
    for j in range(0, n, 512):
        all_ref[:, :, :, j : j + 512] = t_dot(a_ref[...], g_ref[:, j : j + 512]).astype(BF).reshape(8, 2, 64, 512)
    mine_ref[...] = all_ref[:, pl.ds(core, 1)].reshape(8, 64, n)
    other_ref[...] = all_ref[:, pl.ds(1 - core, 1)].reshape(8, 64, n)


def row_grad_kernel(core_ref, a_ref, g_ref, mine_ref, other_ref, all_ref):
    core = core_ref[0]
    rows = mine_ref.shape[1]
    all_ref[...] = t_dot(a_ref[...], g_ref[...]).astype(BF)[: 4 * rows].reshape(2, 2, rows, D)
    mine_ref[...] = all_ref[:, pl.ds(core, 1)].reshape(2, rows, D)
    other_ref[...] = all_ref[:, pl.ds(1 - core, 1)].reshape(2, rows, D)


def pack_columns(mine_ref, other_ref, out_ref):
    lanes = mine_ref.shape[2] // 2
    for i in range(8):
        value = (mine_ref[i].astype(F32) + other_ref[i].astype(F32)).astype(BF)
        for half in range(2):
            for j in range(lanes // 128):
                at = half * lanes + j * 128
                out_ref[i * 2 + half, j * 64 : (j + 1) * 64, :] = value[:, at : at + 128]


def pack_rows(mine_ref, other_ref, out_ref, start):
    rows = mine_ref.shape[1]
    for yl in range(2):
        value = (mine_ref[yl].astype(F32) + other_ref[yl].astype(F32)).astype(BF)
        for p in range(8):
            to = (p // 2) * 4 + yl * 2 + p % 2
            out_ref[to, start : start + rows, :] = value[:, p * 128 : (p + 1) * 128]


def pack_kernel(mine_ref, other_ref, my_rows_ref, other_rows_ref, out_ref):
    pack_columns(mine_ref, other_ref, out_ref)
    pack_rows(my_rows_ref, other_rows_ref, out_ref, mine_ref.shape[2] // 4)


def rider_rows(value):
    rows = [piece[:, cols] for piece in split3(value) for cols in (slice(0, 128), slice(128, 256))]
    return jnp.concatenate([*rows, jnp.zeros((10, 128), F32)], axis=0).astype(BF)


def rider_value(rows):
    rows = rows.astype(F32)
    halves = [(rows[i : i + 1] + rows[i + 2 : i + 3]) + rows[i + 4 : i + 5] for i in range(2)]
    return jnp.concatenate(halves, axis=1)


def pack_last_kernel(mine_ref, other_ref, floor_ref, other_floor_ref, out_ref):
    pack_columns(mine_ref, other_ref, out_ref)
    rider = rider_rows(floor_ref[...] + other_floor_ref[...])
    for i in range(16):
        out_ref[i, 128:, :] = rider


def total_of(all_ref, rows):
    total = all_ref[0, rows, :].astype(F32)
    for i in range(1, 16):
        total = total + all_ref[i, rows, :].astype(F32)
    return total


def sum_kernel(all_ref, columns_ref, rows_ref):
    cut = columns_ref.shape[0]
    columns_ref[...] = total_of(all_ref, slice(0, cut)).astype(BF)
    rows_ref[...] = total_of(all_ref, slice(cut, all_ref.shape[1])).astype(BF)


def sum_last_kernel(all_ref, columns_ref, rows_ref, out_ref):
    total = total_of(all_ref, slice(0, 128)).astype(BF)
    floor = rider_value(all_ref[0, 128:, :])
    for i in range(1, 16):
        floor = floor + rider_value(all_ref[i, 128:, :])
    rider = rider_rows(floor)
    for i in range(8):
        out_ref[i, :128, :] = total
        out_ref[i, 128:144, :] = rider
        out_ref[i, 144:272, :] = columns_ref[...]
        out_ref[i, 272:, :] = rows_ref[...]


def feed_grads_kernel(z_ref, s0, s1, s2, s3, w_ref, gain_ref, up_ref, gain_grad_ref, down_ref):
    quarters = [lax.rem(z_ref[0] + by, 4) for by in (0, 3, 1, 2)]
    chosen = jnp.concatenate([selection(z, SLOTS, UNITS, True) for z in quarters], axis=0)
    gain = column(gain_ref)
    gain_grad = jnp.zeros((64, 128), F32)
    for i in range(4):
        lanes = slice(i * SLOTS, (i + 1) * SLOTS)
        value = dot(jnp.concatenate([ref[:64, lanes] for ref in (s0, s1, s2, s3)], axis=1), chosen)
        cols = slice(i * UNITS, (i + 1) * UNITS)
        up_ref[:, cols] = value * gain
        gain_grad = gain_grad + lane_blocks(value * w_ref[:, cols].astype(F32))
    gain_grad_ref[...] = row_sums(gain_grad)
    down = jnp.zeros((OWNED, D), F32)
    for z, ref in zip(quarters, (s0, s1, s2, s3)):
        last = jnp.concatenate([ref[64:80, D:], ref[80:, D:]], axis=1)
        rows = jnp.concatenate([ref[64:, :D], last], axis=0)
        down = down + dot(selection(z, SLOT, OWNED, False), rows)
    down_ref[...] = down


def mix_grads_kernel(all_ref, w_ref, gain_ref, out_w_ref, out_gain_ref,
                     mix_ref, gain_grad_ref, out_ref, out_gain_grad_ref, floor_ref):
    gain, out_gain = column(gain_ref), column(out_gain_ref)
    gain_grad = jnp.zeros((64, 128), F32)
    out_gain_grad = jnp.zeros((64, 128), F32)
    for yh in range(2):
        for z in range(4):
            i = yh * 4 + z
            for start, block in ((0, 2 if yh else 1), (144, 3 if yh else 0)):
                for j in range(2):
                    value = all_ref[i, start + j * 64 : start + (j + 1) * 64, :].astype(F32)
                    at = block * D + z * COLS + j * 128
                    mix_ref[:, at : at + 128] = value * gain
                    gain_grad = gain_grad + value * w_ref[:, at : at + 128].astype(F32)
            p = z * 2 + yh
            value = all_ref[i, 272:, :].astype(F32)
            cols = slice(p * 128, (p + 1) * 128)
            out_ref[:, cols] = value * out_gain
            out_gain_grad = out_gain_grad + value * out_w_ref[:, cols].astype(F32)
            if yh == 0:
                floor_ref[:, z * COLS : (z + 1) * COLS] = rider_value(all_ref[i, 128:144, :])
    gain_grad_ref[...] = row_sums(gain_grad)
    out_gain_grad_ref[...] = row_sums(out_gain_grad)


def scalar(value):
    return value.reshape(1).astype(jnp.int32)


def body(hidden, mixer_weight, output_weight, gate_up_weight, down_weight, mixer_gain, group_gain, feed_gain,
         forget_floor, out_grad):
    z = lax.axis_index("z")
    core, yl = scalar(lax.axis_index("c")), scalar(lax.axis_index("yl"))
    place = scalar(lax.axis_index("x") * 2 + lax.axis_index("yl"))
    gain_one, gain_group, gain_two = (g.reshape(1, 64) for g in (mixer_gain, group_gain, feed_gain))
    floor = lax.dynamic_index_in_dim(forget_floor.reshape(PARTS, COLS), z, 0)
    own = [shape((ROWS, D), BF)] * 4
    state_shape = shape((STATES, HEAD_DIM, HEAD_DIM), BF)

    normed_own = kernel_call(norm_kernel, shape((ROWS, D), BF), hidden)
    normed = gather_z(normed_own)
    fv_sent, qg_own = kernel_call(
        prepare_kernel,
        (shape((8, 64, WIDE), BF), shape((64, WIDE), BF)),
        scalar(z), mixer_weight, gain_one,
        order=(normed_own,),
    )
    fv_mine = exchange(fv_sent, ("x", "yl"))
    fv_other = shift(after(fv_mine, *normed), "c", 1)
    w_qg = lax.all_gather(qg_own, ("x", "yl", "c"), axis=0, tiled=True)
    out_own = (after(output_weight, fv_sent).astype(F32) * group_gain.astype(F32)[:, None]).astype(BF)
    out_rows = four_rows(out_own)
    feed_own_weights = kernel_call(
        prepare_feed_kernel, shape((FEED_ROWS, 2 * PAD), BF), scalar(z), gate_up_weight, gain_two, down_weight,
        order=(fv_sent,),
    )
    w_feed = lax.all_gather(feed_own_weights, ("x", "yl", "c"))

    x_all, w_fv, pre_fv, cum, end, total = kernel_call(
        first_kernel,
        (
            shape((TOKENS, D), BF),
            shape((8, 2, 64, WIDE), BF),
            shape((TOKENS, WIDE), F32),
            shape((TOKENS, COLS), F32),
            state_shape,
            shape((STATES, HEAD_DIM), F32),
        ),
        core, *normed, fv_mine, fv_other, floor,
        flops=2 * TOKENS * D * WIDE,
        order=(feed_own_weights, out_own),
    )
    w_fv = w_fv.reshape(D, WIDE)
    grads_out = gather_z(after(out_grad, end))

    def send_state(end_state, other_total, backward):
        other_end = shift(end_state, "c", 1)
        sent = kernel_call(
            functools.partial(chip_kernel, backward=backward),
            shape((8, HALF * HEAD_DIM + (0 if backward else TAIL), HEAD_DIM), BF),
            core, end_state, other_end, total, other_total,
        )
        return sent, exchange(sent, ("x", "yl")), other_end

    half_shape = shape((HALF, HEAD_DIM, HEAD_DIM), BF)
    other_total = shift(total, "c", 1)
    sent, arrived, other_end = send_state(end, other_total, False)
    pre_qg, q_in, local_out = kernel_call(
        second_kernel,
        (shape((TOKENS, WIDE), F32), shape((TOKENS, COLS), BF), shape((TOKENS, COLS), F32)),
        x_all, w_qg, pre_fv, cum, floor,
        flops=2 * TOKENS * D * WIDE,
        order=(sent,),
    )
    own_half, totals = kernel_call(
        functools.partial(carry_kernel, backward=False),
        (half_shape, shape((8, HALF, HEAD_DIM), F32)),
        place, arrived,
        order=(q_in,),
    )
    mixed, normed_out, entered, w_out, *parts = kernel_call(
        mix_kernel,
        (
            shape((TOKENS, COLS), F32),
            shape((TOKENS, COLS), BF),
            state_shape,
            shape((4, 64, D), BF),
            *own,
        ),
        core, yl, pre_qg, q_in, local_out, own_half, shift(own_half, "c", 1), other_end, other_total, *out_rows,
        flops=2 * TOKENS * COLS * D,
        order=grads_out,
    )
    middle, feed_own = kernel_call(
        middle_kernel, (shape((ROWS, D), F32), shape((ROWS, D), BF)), hidden, *scatter_z(parts)
    )
    f_all, g_all, act, grad_up, w_down, *parts = kernel_call(
        feed_kernel,
        (
            shape((TOKENS, D), BF),
            shape((TOKENS, D), BF),
            shape((TOKENS, PAD), BF),
            shape((TOKENS, 2 * PAD), BF),
            shape((PAD, D), BF),
            *own,
        ),
        *gather_z(feed_own), *grads_out, w_feed,
        flops=2 * TOKENS * D * PAD * 5,
    )
    feed_back = scatter_z(parts)

    def column_grad(a, g, order=()):
        n = g.shape[1]
        return kernel_call(
            column_grad_kernel,
            (shape((8, 64, n), BF), shape((8, 64, n), BF)),
            core, a, g,
            scratch=[pltpu.VMEM((8, 2, 64, n), BF)],
            flops=2 * TOKENS * D * n,
            order=order,
        )

    def row_grad(a, g, rows, order=()):
        return kernel_call(
            row_grad_kernel,
            (shape((2, rows, D), BF), shape((2, rows, D), BF)),
            core, a, g,
            scratch=[pltpu.VMEM((2, 2, rows, D), BF)],
            flops=2 * TOKENS * D * a.shape[1],
            order=order,
        )

    def pack(columns, other_columns, rows, other_rows, order):
        cut, high = columns.shape[2] // 4, rows.shape[1]
        return kernel_call(
            pack_kernel, shape((16, cut + high, 128), BF), columns, other_columns, rows, other_rows, order=order
        )

    def sums(packed, cut, high, order):
        arrived = exchange(packed, ("x", "yl", "yh"))
        columns, rows = kernel_call(
            sum_kernel, (shape((cut, 128), BF), shape((high, 128), BF)), arrived, order=order
        )
        return columns, transpose_xz(rows)

    feed_grad = kernel_call(
        feed_grad_kernel, shape((16, FEED_ROWS, 2 * PAD), BF), f_all, grad_up, act, g_all,
        flops=2 * TOKENS * D * PAD * 3,
        order=(parts[3],),
    )
    feed_sum = lax.psum_scatter(feed_grad, ("x", "yl", "c"), scatter_dimension=0)
    grad_middle, branch_own = kernel_call(
        branch_kernel, (shape((ROWS, D), F32), shape((ROWS, D), BF)), middle, out_grad, *feed_back,
        order=(feed_grad,),
    )
    branch = gather_z(branch_own)
    branch_all, grad_gate, grad_mixed, end_grad = kernel_call(
        head_back_kernel,
        (shape((TOKENS, D), BF), shape((TOKENS, COLS), BF), shape((TOKENS, COLS), BF), state_shape),
        *branch, w_out, pre_qg, q_in, mixed,
        flops=2 * TOKENS * COLS * D,
    )
    sent, arrived, other_end = send_state(end_grad, other_total, True)

    grad_qg, near_log, near_key, near_value = kernel_call(
        near_back_kernel,
        (shape((TOKENS, WIDE), BF), *[shape((TOKENS, COLS), F32)] * 3),
        pre_qg, pre_fv, cum, floor, q_in, grad_gate, grad_mixed, entered,
        flops=2 * TOKENS * HEAD_DIM * HEAD_DIM * 12,
        order=(sent,),
    )
    qg_mine, qg_other = column_grad(x_all, grad_qg)
    out_mine, out_other = row_grad(normed_out, branch_all, 64, order=(qg_other,))
    down_parts = kernel_call(
        down_kernel, tuple(own), act, w_down, flops=2 * TOKENS * D * PAD, order=(out_other,)
    )
    qg_packed = pack(qg_mine, shift(qg_other, "c", 1), out_mine, shift(out_other, "c", 1), (down_parts[3],))
    own_half = kernel_call(
        functools.partial(carry_kernel, backward=True), half_shape, place, arrived, totals, order=(qg_packed,)
    )
    grad_fv, floor_part, *parts = kernel_call(
        far_back_kernel,
        (shape((TOKENS, WIDE), BF), shape((1, COLS), F32), *own),
        core, pre_fv, cum, floor, near_log, near_key, near_value, entered, own_half, shift(own_half, "c", 1), other_end,
        other_total, grad_qg, w_fv, w_qg,
        flops=2 * TOKENS * D * D,
    )
    fv_mine, fv_other = column_grad(x_all, grad_fv)
    sent = kernel_call(
        pack_last_kernel, shape((16, 144, 128), BF), fv_mine, shift(fv_other, "c", 1), floor_part,
        shift(floor_part, "c", 1),
    )
    arrived = exchange(sent, ("x", "yl", "yh"))

    qg_columns, out_sums = sums(qg_packed, 128, 64, (sent,))
    feed_total = kernel_call(
        add_kernel, shape((FEED_ROWS, 2 * PAD), BF), feed_sum, shift(feed_sum, "yh", 1), order=(qg_columns,)
    )
    feed_totals = gather_z(feed_total)
    result = kernel_call(
        result_kernel, shape((ROWS, D), BF), middle, *scatter_z(down_parts), order=(feed_total,)
    )
    parts = scatter_z(after(parts, sent))
    last_copies = kernel_call(
        sum_last_kernel, shape((8, 336, 128), BF), arrived, qg_columns, out_sums, order=(result,)
    )
    last_sums = exchange(last_copies, ("yh", "z"))
    grad_tokens = kernel_call(
        last_kernel, shape((ROWS, D), BF), hidden, grad_middle, *parts, order=(last_copies,)
    )
    up_grad, feed_gain_grad, down_grad = kernel_call(
        feed_grads_kernel,
        (shape((64, 2 * FF), F32), shape((1, 64), F32), shape((OWNED, D), F32)),
        scalar(z), *feed_totals, gate_up_weight, gain_two,
        order=(grad_tokens,),
    )
    mix_grad, gain_grad, out_weight_grad, group_gain_grad, floor_grad = kernel_call(
        mix_grads_kernel,
        (
            shape((64, 4 * D), F32),
            shape((1, 64), F32),
            shape((64, D), F32),
            shape((1, 64), F32),
            shape((1, D), F32),
        ),
        last_sums, mixer_weight, gain_one, output_weight, gain_group,
        order=(up_grad,),
    )
    return (
        result,
        grad_tokens,
        mix_grad,
        out_weight_grad,
        up_grad,
        down_grad,
        gain_grad.reshape(64),
        group_gain_grad.reshape(64),
        feed_gain_grad.reshape(64),
        floor_grad.reshape(D),
    )


def solution(mesh):
    cut = Mesh(mesh.devices.reshape(2, 4, 4, 2, 2), AXES)
    seq = ("x", "yl", "c")
    rows, weight, vector = P(AXES, None), P(seq, None), P(seq)
    in_specs = (rows, weight, weight, weight, weight, vector, vector, vector, P(), rows)
    out_specs = (rows, rows, weight, weight, weight, weight, vector, vector, vector, P())
    return jax.shard_map(body, mesh=cut, in_specs=in_specs, out_specs=out_specs, check_vma=False)
```

```python
import functools

import jax
import jax.numpy as jnp
from jax import lax
from jax.experimental import pallas as pl
from jax.experimental.pallas import tpu as pltpu
from jax.sharding import Mesh, PartitionSpec as P

D = 1024
HEADS = 8
HEAD_DIM = 128
FF = 2816
EPS = 1e-06

ROWS = 128
PARTS = 4
COLS = D // PARTS
TOKENS = PARTS * ROWS
WIDE = 2 * COLS
PAD = 768
SLOT, TAKEN, OWNED = 48, 44, 176
SLOTS, UNITS = 8 * SLOT, 8 * OWNED
FEED_ROWS = 96
LOCAL_HEADS = 2
STATES = PARTS * LOCAL_HEADS
HALF = STATES // 2
TAIL = 16
BF = jnp.bfloat16
F32 = jnp.float32
AXES = ("yh", "z", "x", "yl", "c")
VMEM = 40 * 1024 * 1024


def shift(value, axis, by):
    n = lax.axis_size(axis)
    return lax.ppermute(value, axis, [(i, (i + by) % n) for i in range(n)])


def gather_z(own):
    return (own, shift(own, "z", 1), shift(own, "z", -1), shift(own, "z", 2))


def scatter_z(parts):
    return (parts[0], shift(parts[1], "z", -1), shift(parts[2], "z", 1), shift(parts[3], "z", 2))


def transpose_xz(value):
    pairs = [(z * 4 + x, x * 4 + z) for z in range(4) for x in range(4)]
    return lax.ppermute(value, ("z", "x"), pairs)


def quarters(z):
    return [lax.rem(z + by, 4) for by in (0, 3, 1, 2)]


def exchange(value, axes):
    return lax.all_to_all(value, axes, 0, 0)


def after(value, *others):
    return lax.optimization_barrier((value, *others))[0]


def kernel_call(body, out_shape, *args, scratch=(), flops=0, order=(), near=()):
    if order:
        args = after(args, *order)
    args = [
        a if a.dtype == jnp.int32 else pltpu.with_memory_space_constraint(a, pltpu.VMEM if i in near else pltpu.HBM)
        for i, a in enumerate(args)
    ]
    in_specs = [
        pl.BlockSpec(memory_space=pltpu.SMEM) if a.dtype == jnp.int32 else pl.BlockSpec(memory_space=pltpu.VMEM)
        for a in args
    ]
    out_specs = jax.tree.map(lambda _: pl.BlockSpec(memory_space=pltpu.VMEM), out_shape)
    return pl.pallas_call(
        body,
        out_shape=out_shape,
        in_specs=in_specs,
        out_specs=out_specs,
        scratch_shapes=list(scratch),
        compiler_params=pltpu.CompilerParams(vmem_limit_bytes=VMEM),
        cost_estimate=pl.CostEstimate(flops=1, bytes_accessed=1, transcendentals=0),
    )(*args)


def shape(dims, dtype):
    return pltpu.HBM(dims, dtype)


def near_shape(dims, dtype):
    return pltpu.VMEM(dims, dtype)


def dot(a, b):
    return jnp.dot(a, b, preferred_element_type=F32)


def dot_t(a, b):
    return lax.dot_general(a, b, (((1,), (1,)), ((), ())), preferred_element_type=F32)


def t_dot(a, b):
    return lax.dot_general(a, b, (((0,), (0,)), ((), ())), preferred_element_type=F32)


def exact_dot(a, b):
    return jnp.dot(a, b, precision=lax.Precision.HIGHEST, preferred_element_type=F32)


def mean_scale(value):
    return lax.rsqrt(jnp.mean(value * value, axis=-1, keepdims=True) + EPS)


def triangle(strict, upper):
    row = lax.broadcasted_iota(jnp.int32, (ROWS, ROWS), 0)
    col = lax.broadcasted_iota(jnp.int32, (ROWS, ROWS), 1)
    if upper:
        row, col = col, row
    return row > col if strict else row >= col


def swish_slope(value, sigma):
    return sigma * (1.0 + value * (1.0 - sigma))


def column(ref):
    return jnp.transpose(ref[...].astype(F32))


def row_sums(value):
    return jnp.sum(jnp.transpose(value), axis=0, keepdims=True)


def lane_blocks(value):
    total = value[:, :128]
    for j in range(128, value.shape[1], 128):
        total = total + value[:, j : j + 128]
    return total


def prepare_kernel(z_ref, w_ref, gain_ref, out_w_ref, out_gain_ref, sent_ref, out_ref):
    start = z_ref[0] * COLS
    gain = column(gain_ref)
    for to, j in enumerate((1, 2, 0, 3)):
        cols = pl.ds(pl.multiple_of(j * D + start, 128), COLS)
        block = (w_ref[:, cols].astype(F32) * gain).astype(BF)
        for i in range(8):
            sent_ref[i, :, to * COLS : (to + 1) * COLS] = block
    out_ref[...] = (out_w_ref[...].astype(F32) * column(out_gain_ref)).astype(BF)


def selection(z, slots, units, slots_first):
    shape_ = (slots, units) if slots_first else (units, slots)
    line = (slots, 1) if slots_first else (1, slots)
    slot = lax.broadcasted_iota(jnp.int32, line, 0 if slots_first else 1)
    owner = jnp.zeros(line, jnp.int32)
    for i in range(1, slots // SLOT):
        owner = owner + (slot >= i * SLOT).astype(jnp.int32)
    place = slot - owner * SLOT
    unit = jnp.where(place < TAKEN, owner * OWNED + z * TAKEN + place, -1)
    return jnp.where(lax.broadcasted_iota(jnp.int32, shape_, 1 if slots_first else 0) == unit, 1.0, 0.0).astype(BF)


def prepare_feed_kernel(z_ref, up_ref, gain_ref, down_ref, out_ref):
    gain = column(gain_ref)
    chosen = selection(z_ref[0], SLOTS, UNITS, False)
    for i in range(4):
        picked = dot(up_ref[:, i * UNITS : (i + 1) * UNITS], chosen)
        out_ref[:64, i * SLOTS : (i + 1) * SLOTS] = (picked * gain).astype(BF)
    rows = dot(selection(z_ref[0], SLOT, OWNED, True), down_ref[...]).astype(BF)
    out_ref[64:, :D] = rows[:32]
    out_ref[64:80, D:] = rows[32:, :512]
    out_ref[80:, D:] = rows[32:, 512:]


def gated(pre, floor):
    sigma = lax.logistic(pre)
    return sigma, floor + (1.0 - floor) * sigma


def swish(value):
    return value * lax.logistic(value)


def head_cols(h):
    return slice(h * HEAD_DIM, (h + 1) * HEAD_DIM)


def part_rows(b):
    return slice(b * ROWS, (b + 1) * ROWS)


def first_kernel(core_ref, x0, x1, x2, x3, mine_ref, other_ref, floor_ref,
                 x_ref, w_ref, pre_ref, cum_ref, state_ref, total_ref):
    core = core_ref[0]
    w_ref[:, pl.ds(core, 1)] = mine_ref[:, :, :WIDE].reshape(8, 1, 64, WIDE)
    w_ref[:, pl.ds(1 - core, 1)] = other_ref[:, :, :WIDE].reshape(8, 1, 64, WIDE)
    for b, part in enumerate((x0, x1, x2, x3)):
        value = part[...].astype(F32)
        x_ref[part_rows(b), :] = (value * mean_scale(value)).astype(BF)
    pre_ref[...] = dot(x_ref[...], w_ref[...].reshape(D, WIDE))
    ones = triangle(False, False).astype(F32)
    floor = floor_ref[...]
    for b in range(PARTS):
        rows = part_rows(b)
        _, decay = gated(pre_ref[rows, :COLS], floor)
        cum_all = exact_dot(ones, jnp.log(decay))
        cum_ref[rows, :] = cum_all
        total_all = cum_all[ROWS - 1 :, :]
        k_out = ((1.0 - decay).astype(BF).astype(F32) * jnp.exp(total_all - cum_all)).astype(BF)
        for h in range(LOCAL_HEADS):
            value = pre_ref[rows, COLS + h * HEAD_DIM : COLS + (h + 1) * HEAD_DIM].astype(BF)
            s = h * PARTS + b
            state_ref[s] = t_dot(k_out[:, head_cols(h)], value).astype(BF)
            total_ref[s : s + 1, :] = total_all[:, head_cols(h)]


def second_kernel(core_ref, x_ref, mine_ref, other_ref, fv_ref, cum_ref, floor_ref, w_ref, pre_ref, q_ref, local_ref):
    core = core_ref[0]
    w_ref[:, pl.ds(core, 1)] = mine_ref[:, :, WIDE:].reshape(8, 1, 64, WIDE)
    w_ref[:, pl.ds(1 - core, 1)] = other_ref[:, :, WIDE:].reshape(8, 1, 64, WIDE)
    pre_ref[...] = dot(x_ref[...], w_ref[...].reshape(D, WIDE))
    causal = triangle(False, False)
    floor = floor_ref[...]
    for b in range(PARTS):
        rows = part_rows(b)
        _, decay = gated(fv_ref[rows, :COLS], floor)
        cum = cum_ref[rows, :]
        k_in = ((1.0 - decay).astype(BF).astype(F32) * jnp.exp(-cum)).astype(BF)
        q_in = (swish(pre_ref[rows, :COLS]).astype(BF).astype(F32) * jnp.exp(cum)).astype(BF)
        q_ref[rows, :] = q_in
        value = fv_ref[rows, COLS:].astype(BF)
        for h in range(LOCAL_HEADS):
            cols = head_cols(h)
            scores = jnp.where(causal, dot_t(q_in[:, cols], k_in[:, cols]), 0.0).astype(BF)
            local_ref[rows, cols] = dot(scores, value[:, cols])


def split3(value):
    first = value.astype(BF).astype(F32)
    second = (value - first).astype(BF).astype(F32)
    return first, second, value - first - second


def chip_kernel(core_ref, mine_ref, other_ref, my_total_ref, other_total_ref, out_ref, *, backward):
    core = core_ref[0]
    second = core == (0 if backward else 1)
    base = core * HALF
    my_total = my_total_ref[pl.ds(base, HALF), :]
    other_total = other_total_ref[pl.ds(base, HALF), :]
    last_decay = jnp.exp(jnp.where(second, my_total, other_total))
    for i in range(HALF):
        mine = mine_ref[base + i].astype(F32)
        other = other_ref[base + i].astype(F32)
        last = jnp.where(second, mine, other)
        first = jnp.where(second, other, mine)
        state = (jnp.transpose(last_decay[i : i + 1, :]) * first + last).astype(BF)
        for d in range(8):
            out_ref[d, i * HEAD_DIM : (i + 1) * HEAD_DIM, :] = state
    if not backward:
        pieces = split3(my_total + other_total)
        tail = jnp.concatenate([*pieces, jnp.zeros((HALF, HEAD_DIM), F32)], axis=0).astype(BF)
        for d in range(8):
            out_ref[d, HALF * HEAD_DIM :, :] = tail


def carry_kernel(place_ref, all_ref, *refs, backward):
    place = place_ref[0]
    if backward:
        totals_ref, out_ref = refs
    else:
        out_ref, totals_ref = refs
        for j in range(8):
            tail = all_ref[j, HALF * HEAD_DIM :, :].astype(F32)
            totals_ref[j] = (tail[:HALF] + tail[HALF : 2 * HALF]) + tail[2 * HALF : 3 * HALF]
    for i in range(HALF):
        carried = jnp.zeros((HEAD_DIM, HEAD_DIM), F32)
        decays = jnp.transpose(jnp.exp(jnp.concatenate([totals_ref[j, i : i + 1, :] for j in range(8)], axis=0)))
        for step in range(7):
            j = 7 - step if backward else step
            reached = j > place if backward else j < place
            block = all_ref[j, i * HEAD_DIM : (i + 1) * HEAD_DIM, :].astype(F32)
            carried = jnp.where(reached, decays[:, j : j + 1] * carried + block, carried)
        out_ref[i] = carried.astype(BF)


def enter_state(core, own_half, other_half, other_end, other_total, s, backward):
    h, b = divmod(s, PARTS)
    chip = jnp.where(core == h, own_half[b], other_half[b]).astype(F32)
    later = core == (0 if backward else 1)
    passed = jnp.transpose(jnp.exp(other_total[s : s + 1, :])) * chip + other_end[s].astype(F32)
    return jnp.where(later, passed, chip)


def mix_kernel(core_ref, pre_ref, q_ref, local_ref, own_half, other_half, other_end, other_total, w_ref,
               out_ref, normed_ref, entered_ref, p0, p1, p2, p3):
    core = core_ref[0]
    for b in range(PARTS):
        rows = part_rows(b)
        for h in range(LOCAL_HEADS):
            cols = head_cols(h)
            s = h * PARTS + b
            state = enter_state(core, own_half, other_half, other_end, other_total, s, False).astype(BF)
            entered_ref[s] = state
            mixed = local_ref[rows, cols] + dot(q_ref[rows, cols], state)
            out_ref[rows, cols] = mixed
            gate = pre_ref[rows, COLS + h * HEAD_DIM : COLS + (h + 1) * HEAD_DIM]
            normed_ref[rows, cols] = (mixed * mean_scale(mixed) * swish(gate)).astype(BF)
    product = dot(normed_ref[...], w_ref[...]).astype(BF)
    for b, part in enumerate((p0, p1, p2, p3)):
        part[...] = product[part_rows(b), :]


def sum_parts(p0, p1, p2, p3):
    return (p0[...].astype(F32) + p1[...].astype(F32)) + (p2[...].astype(F32) + p3[...].astype(F32))


def middle_kernel(hidden_ref, p0, p1, p2, p3, middle_ref, normed_ref):
    middle = hidden_ref[...].astype(F32) + sum_parts(p0, p1, p2, p3)
    middle_ref[...] = middle
    normed_ref[...] = (middle * mean_scale(middle)).astype(BF)


def feed_kernel(z_ref, x0, x1, x2, x3, out_grad_ref, w_ref, x_ref, g_ref, act_ref, grad_ref, down_ref, out_ref):
    for s in range(16):
        at = s * SLOT
        down_ref[at : at + 32, :] = w_ref[s, 64:, :D]
        down_ref[at + 32 : at + 48, :512] = w_ref[s, 64:80, D:]
        down_ref[at + 32 : at + 48, 512:] = w_ref[s, 80:, D:]
    for b, part in enumerate((x0, x1, x2, x3)):
        x_ref[part_rows(b), :] = part[...]
    for b, z in enumerate(quarters(z_ref[0])):
        g_ref[part_rows(b), :] = out_grad_ref[pl.ds(z, 1)].reshape(ROWS, D)
    for j in range(3):
        lanes = slice(j * COLS, (j + 1) * COLS)
        ups = slice(PAD + j * COLS, PAD + (j + 1) * COLS)
        gate = dot(x_ref[...], w_ref[:, :64, lanes].reshape(D, COLS))
        up = dot(x_ref[...], w_ref[:, :64, ups].reshape(D, COLS))
        grad = dot_t(g_ref[...], down_ref[lanes, :])
        sigma = lax.logistic(gate)
        active = gate * sigma
        act_ref[:, lanes] = (active * up).astype(BF)
        grad_ref[:, lanes] = (grad * up * swish_slope(gate, sigma)).astype(BF)
        grad_ref[:, ups] = (grad * active).astype(BF)
    product = dot_t(grad_ref[...], w_ref[:, :64, :].reshape(D, 2 * PAD)).astype(BF)
    for b, z in enumerate(quarters(z_ref[0])):
        out_ref[pl.ds(z, 1)] = product[part_rows(b), :].reshape(1, ROWS, D)


def feed_grad_kernel(x_ref, grad_ref, act_ref, g_ref, down_ref, out_ref, p0, p1, p2, p3):
    product = dot(act_ref[...], down_ref[...]).astype(BF)
    for b, part in enumerate((p0, p1, p2, p3)):
        part[...] = product[part_rows(b), :]
    for j in range(0, 2 * PAD, 512):
        out_ref[:, :64, j : j + 512] = t_dot(x_ref[...], grad_ref[:, j : j + 512]).astype(BF).reshape(16, 64, 512)
    rows = t_dot(act_ref[...], g_ref[...]).astype(BF)
    for s in range(16):
        at = s * SLOT
        out_ref[s, 64:, :D] = rows[at : at + 32]
        out_ref[s, 64:80, D:] = rows[at + 32 : at + 48, :512]
        out_ref[s, 80:, D:] = rows[at + 32 : at + 48, 512:]


def add_kernel(a_ref, b_ref, out_ref):
    out_ref[...] = (a_ref[...].astype(F32) + b_ref[...].astype(F32)).astype(BF)


def result_kernel(middle_ref, p0, p1, p2, p3, out_ref):
    out_ref[...] = (middle_ref[...] + sum_parts(p0, p1, p2, p3)).astype(BF)


def norm_back(value_ref, base_ref, u):
    value = value_ref[...].astype(F32)
    scale = mean_scale(value)
    centered = value * scale
    back = scale * (u - centered * jnp.mean(u * centered, axis=-1, keepdims=True))
    return base_ref[...].astype(F32) + back


def branch_kernel(value_ref, base_ref, all_ref, out_ref, low_ref):
    total = norm_back(value_ref, base_ref, sum_parts(*(all_ref[i] for i in range(PARTS))))
    out_ref[...] = total
    low_ref[...] = total.astype(BF)


def last_kernel(value_ref, base_ref, p0, p1, p2, p3, low_ref):
    low_ref[...] = norm_back(value_ref, base_ref, sum_parts(p0, p1, p2, p3)).astype(BF)


def head_back_kernel(b0, b1, b2, b3, w_ref, pre_ref, q_ref, mixed_ref, branch_ref, gate_ref, out_grad_ref, state_ref):
    for b, part in enumerate((b0, b1, b2, b3)):
        branch_ref[part_rows(b), :] = part[...]
    grads = dot_t(branch_ref[...], w_ref[...])
    for b in range(PARTS):
        rows = part_rows(b)
        for h in range(LOCAL_HEADS):
            cols = head_cols(h)
            grad = grads[rows, cols]
            mixed = mixed_ref[rows, cols]
            scale = mean_scale(mixed)
            normed = mixed * scale
            gate = pre_ref[rows, COLS + h * HEAD_DIM : COLS + (h + 1) * HEAD_DIM]
            sigma = lax.logistic(gate)
            gate_ref[rows, cols] = (grad * normed * swish_slope(gate, sigma)).astype(BF)
            c = grad * (gate * sigma)
            mixer = (scale * (c - normed * jnp.mean(c * normed, axis=-1, keepdims=True))).astype(BF)
            out_grad_ref[rows, cols] = mixer
            state_ref[h * PARTS + b] = t_dot(q_ref[rows, cols], mixer).astype(BF)


def near_back_kernel(core_ref, x_ref, normed_ref, branch_ref, qg_ref, fv_ref, cum_ref, floor_ref, q_ref, gate_ref,
                     out_grad_ref, entered_ref, grad_ref, log_ref, key_ref, value_ref,
                     mine_ref, other_ref, my_rows_ref, other_rows_ref, all_ref, rows_ref):
    causal = triangle(False, False)
    suffix = triangle(False, True).astype(F32)
    floor = floor_ref[...]
    for b in range(PARTS):
        rows = part_rows(b)
        _, decay = gated(fv_ref[rows, :COLS], floor)
        cum = cum_ref[rows, :]
        grow_all = jnp.exp(cum)
        shrink_all = jnp.exp(-cum)
        k_all = ((1.0 - decay).astype(BF).astype(F32) * shrink_all).astype(BF)
        q_pre = qg_ref[rows, :COLS]
        slope_all = swish_slope(q_pre, lax.logistic(q_pre))
        for h in range(LOCAL_HEADS):
            cols = head_cols(h)
            value = fv_ref[rows, COLS + h * HEAD_DIM : COLS + (h + 1) * HEAD_DIM].astype(BF)
            q_in, k_in = q_ref[rows, cols], k_all[:, cols]
            out_grad = out_grad_ref[rows, cols]
            scores = jnp.where(causal, dot_t(q_in, k_in), 0.0).astype(BF)
            grad_scores = jnp.where(causal, dot_t(out_grad, value), 0.0).astype(BF)
            inner = dot(grad_scores, k_in) + dot_t(out_grad, entered_ref[h * PARTS + b])
            back = t_dot(grad_scores, q_in)
            near = q_in.astype(F32) * inner - k_in.astype(F32) * back
            log_ref[rows, cols] = exact_dot(suffix, near)
            key_ref[rows, cols] = back * shrink_all[:, cols]
            value_ref[rows, cols] = t_dot(scores, out_grad)
            grad_ref[rows, cols] = (inner * grow_all[:, cols] * slope_all[:, cols]).astype(BF)
    grad_ref[:, COLS:] = gate_ref[...]
    column_grad(core_ref[0], x_ref, grad_ref, mine_ref, other_ref, all_ref)
    row_grad(core_ref[0], normed_ref, branch_ref, my_rows_ref, other_rows_ref, rows_ref)


def far_back_kernel(core_ref, fv_ref, cum_ref, floor_ref, log_ref, key_ref, value_ref, entered_ref, own_half, other_half,
                    other_end, other_total, qg_ref, w_fv_ref, w_qg_ref, x_ref,
                    floor_grad_ref, mine_ref, other_ref, p0, p1, p2, p3, grad_ref, all_ref):
    core = core_ref[0]
    before = triangle(True, False).astype(F32)
    floor = floor_ref[...]
    floor_sum = jnp.zeros((1, COLS), F32)
    for b in range(PARTS):
        rows = part_rows(b)
        sigma, decay = gated(fv_ref[rows, :COLS], floor)
        cum = cum_ref[rows, :]
        total = cum[ROWS - 1 :, :]
        to_end = jnp.exp(total - cum)
        k_all = ((1.0 - decay).astype(BF).astype(F32) * to_end).astype(BF)
        aheads, edges = [], []
        for h in range(LOCAL_HEADS):
            cols = head_cols(h)
            s = h * PARTS + b
            following = enter_state(core, own_half, other_half, other_end, other_total, s, True)
            low = following.astype(BF)
            value = fv_ref[rows, COLS + h * HEAD_DIM : COLS + (h + 1) * HEAD_DIM].astype(BF)
            aheads.append(dot_t(value, low))
            edges.append(jnp.transpose(jnp.sum(following * entered_ref[s].astype(F32), axis=1, keepdims=True)))
            grad_value = value_ref[rows, cols] + dot(k_all[:, cols], low)
            grad_ref[rows, COLS + h * HEAD_DIM : COLS + (h + 1) * HEAD_DIM] = grad_value.astype(BF)
        ahead = jnp.concatenate(aheads, axis=1)
        edge = jnp.concatenate(edges, axis=1)
        far = exact_dot(before, k_all.astype(F32) * ahead)
        grad_log = log_ref[rows, :] + far + jnp.exp(total) * edge
        grad_decay = grad_log / decay - (key_ref[rows, :] + ahead * to_end)
        floor_sum = floor_sum + jnp.sum(grad_decay * (1.0 - sigma), axis=0, keepdims=True)
        grad_ref[rows, :COLS] = (grad_decay * (1.0 - floor) * sigma * (1.0 - sigma)).astype(BF)
    floor_grad_ref[...] = floor_sum
    column_grad(core, x_ref, grad_ref, mine_ref, other_ref, all_ref)
    product = dot_t(grad_ref[...], w_fv_ref[...].reshape(D, WIDE)) + dot_t(qg_ref[...], w_qg_ref[...].reshape(D, WIDE))
    product = product.astype(BF)
    for b, part in enumerate((p0, p1, p2, p3)):
        part[...] = product[part_rows(b), :]


def column_grad(core, a_ref, g_ref, mine_ref, other_ref, all_ref):
    n = g_ref.shape[1]
    all_ref[...] = t_dot(a_ref[...], g_ref[...]).astype(BF).reshape(8, 2, 64, n)
    mine_ref[...] = all_ref[:, pl.ds(core, 1)].reshape(8, 64, n)
    other_ref[...] = all_ref[:, pl.ds(1 - core, 1)].reshape(8, 64, n)


def row_grad(core, a_ref, g_ref, mine_ref, other_ref, all_ref):
    rows = mine_ref.shape[1]
    all_ref[...] = t_dot(a_ref[...], g_ref[...]).astype(BF).reshape(2, 2, rows, D)
    mine_ref[...] = all_ref[:, pl.ds(core, 1)].reshape(2, rows, D)
    other_ref[...] = all_ref[:, pl.ds(1 - core, 1)].reshape(2, rows, D)


def pack_columns(mine_ref, other_ref, out_ref):
    lanes = mine_ref.shape[2] // 2
    for i in range(8):
        value = (mine_ref[i].astype(F32) + other_ref[i].astype(F32)).astype(BF)
        for half in range(2):
            for j in range(lanes // 128):
                at = half * lanes + j * 128
                out_ref[i * 2 + half, j * 64 : (j + 1) * 64, :] = value[:, at : at + 128]


def pack_rows(mine_ref, other_ref, out_ref, start):
    rows = mine_ref.shape[1]
    for yl in range(2):
        value = (mine_ref[yl].astype(F32) + other_ref[yl].astype(F32)).astype(BF)
        for p in range(8):
            to = (p // 2) * 4 + yl * 2 + p % 2
            out_ref[to, start : start + rows, :] = value[:, p * 128 : (p + 1) * 128]


def pack_kernel(mine_ref, other_ref, my_rows_ref, other_rows_ref, out_ref):
    pack_columns(mine_ref, other_ref, out_ref)
    pack_rows(my_rows_ref, other_rows_ref, out_ref, mine_ref.shape[2] // 4)


def rider_rows(value):
    rows = [piece[:, cols] for piece in split3(value) for cols in (slice(0, 128), slice(128, 256))]
    return jnp.concatenate([*rows, jnp.zeros((10, 128), F32)], axis=0).astype(BF)


def rider_value(rows):
    rows = rows.astype(F32)
    halves = [(rows[i : i + 1] + rows[i + 2 : i + 3]) + rows[i + 4 : i + 5] for i in range(2)]
    return jnp.concatenate(halves, axis=1)


def pack_last_kernel(mine_ref, other_ref, floor_ref, other_floor_ref, out_ref):
    pack_columns(mine_ref, other_ref, out_ref)
    rider = rider_rows(floor_ref[...] + other_floor_ref[...])
    for i in range(16):
        out_ref[i, 128:, :] = rider


def total_of(all_ref, rows):
    total = all_ref[0, rows, :].astype(F32)
    for i in range(1, 16):
        total = total + all_ref[i, rows, :].astype(F32)
    return total


def sum_kernel(all_ref, columns_ref, rows_ref):
    cut = columns_ref.shape[0]
    columns_ref[...] = total_of(all_ref, slice(0, cut)).astype(BF)
    rows_ref[...] = total_of(all_ref, slice(cut, all_ref.shape[1])).astype(BF)


def sum_last_kernel(all_ref, columns_ref, rows_ref, out_ref):
    total = total_of(all_ref, slice(0, 128)).astype(BF)
    floor = rider_value(all_ref[0, 128:, :])
    for i in range(1, 16):
        floor = floor + rider_value(all_ref[i, 128:, :])
    rider = rider_rows(floor)
    for i in range(8):
        out_ref[i, :128, :] = total
        out_ref[i, 128:144, :] = rider
        out_ref[i, 144:272, :] = columns_ref[...]
        out_ref[i, 272:, :] = rows_ref[...]


def feed_grads_kernel(z_ref, s0, s1, s2, s3, w_ref, gain_ref, up_ref, gain_grad_ref, down_ref):
    chosen = jnp.concatenate([selection(z, SLOTS, UNITS, True) for z in quarters(z_ref[0])], axis=0)
    gain = column(gain_ref)
    gain_grad = jnp.zeros((64, 128), F32)
    for i in range(4):
        lanes = slice(i * SLOTS, (i + 1) * SLOTS)
        value = dot(jnp.concatenate([ref[:64, lanes] for ref in (s0, s1, s2, s3)], axis=1), chosen)
        cols = slice(i * UNITS, (i + 1) * UNITS)
        up_ref[:, cols] = value * gain
        gain_grad = gain_grad + lane_blocks(value * w_ref[:, cols].astype(F32))
    gain_grad_ref[...] = row_sums(gain_grad)
    down = jnp.zeros((OWNED, D), F32)
    for z, ref in zip(quarters(z_ref[0]), (s0, s1, s2, s3)):
        last = jnp.concatenate([ref[64:80, D:], ref[80:, D:]], axis=1)
        rows = jnp.concatenate([ref[64:, :D], last], axis=0)
        down = down + dot(selection(z, SLOT, OWNED, False), rows)
    down_ref[...] = down


def mix_grads_kernel(all_ref, w_ref, gain_ref, out_w_ref, out_gain_ref,
                     mix_ref, gain_grad_ref, out_ref, out_gain_grad_ref, floor_ref):
    gain, out_gain = column(gain_ref), column(out_gain_ref)
    gain_grad = jnp.zeros((64, 128), F32)
    out_gain_grad = jnp.zeros((64, 128), F32)
    for yh in range(2):
        for z in range(4):
            i = yh * 4 + z
            for start, block in ((0, 2 if yh else 1), (144, 3 if yh else 0)):
                for j in range(2):
                    value = all_ref[i, start + j * 64 : start + (j + 1) * 64, :].astype(F32)
                    at = block * D + z * COLS + j * 128
                    mix_ref[:, at : at + 128] = value * gain
                    gain_grad = gain_grad + value * w_ref[:, at : at + 128].astype(F32)
            p = z * 2 + yh
            value = all_ref[i, 272:, :].astype(F32)
            cols = slice(p * 128, (p + 1) * 128)
            out_ref[:, cols] = value * out_gain
            out_gain_grad = out_gain_grad + value * out_w_ref[:, cols].astype(F32)
            if yh == 0:
                floor_ref[:, z * COLS : (z + 1) * COLS] = rider_value(all_ref[i, 128:144, :])
    gain_grad_ref[...] = row_sums(gain_grad)
    out_gain_grad_ref[...] = row_sums(out_gain_grad)


def scalar(value):
    return value.reshape(1).astype(jnp.int32)


def body(hidden, mixer_weight, output_weight, gate_up_weight, down_weight, mixer_gain, group_gain, feed_gain,
         forget_floor, out_grad):
    z = lax.axis_index("z")
    z_of = scalar(z)
    core = scalar(lax.axis_index("c"))
    place = scalar(lax.axis_index("x") * 2 + lax.axis_index("yl"))
    gain_one, gain_group, gain_two = (g.reshape(1, 64) for g in (mixer_gain, group_gain, feed_gain))
    floor = lax.dynamic_index_in_dim(forget_floor.reshape(PARTS, COLS), z, 0)
    own = [near_shape((ROWS, D), BF)] * 4
    state_dims = (STATES, HEAD_DIM, HEAD_DIM)
    half_dims = (HALF, HEAD_DIM, HEAD_DIM)

    w_sent, out_own = kernel_call(
        prepare_kernel, (shape((8, 64, D), BF), shape((64, D), BF)),
        z_of, mixer_weight, gain_one, output_weight, gain_group,
    )
    tokens = gather_z(hidden)
    w_mine = exchange(w_sent, ("x", "yl"))
    grads_out = lax.all_gather(out_grad, "z")
    w_out = lax.all_gather(out_own, ("x", "yl", "c"))
    w_other = shift(after(w_mine, *tokens), "c", 1)
    x_all, w_fv, pre_fv, cum, end, total = kernel_call(
        first_kernel,
        (
            shape((TOKENS, D), BF),
            shape((8, 2, 64, WIDE), BF),
            shape((TOKENS, WIDE), F32),
            shape((TOKENS, COLS), F32),
            near_shape(state_dims, BF),
            shape((STATES, HEAD_DIM), F32),
        ),
        core, *tokens, w_mine, w_other, floor,
        flops=2 * TOKENS * D * WIDE,
    )

    def chip_state(end_state, other_total, backward, order=()):
        other_end = shift(end_state, "c", 1)
        sent = kernel_call(
            functools.partial(chip_kernel, backward=backward),
            shape((8, HALF * HEAD_DIM + (0 if backward else TAIL), HEAD_DIM), BF),
            core, end_state, other_end, total, other_total,
            order=order,
            near=(1,),
        )
        return sent, other_end

    other_total = shift(total, "c", 1)
    sent, other_end = chip_state(end, other_total, False)
    feed_own_weights = kernel_call(
        prepare_feed_kernel, shape((FEED_ROWS, 2 * PAD), BF), z_of, gate_up_weight, gain_two, down_weight,
        order=(sent,),
    )
    w_feed = lax.all_gather(feed_own_weights, ("x", "yl", "c"))
    arrived = exchange(sent, ("x", "yl"))
    w_qg, pre_qg, q_in, local_out = kernel_call(
        second_kernel,
        (
            shape((8, 2, 64, WIDE), BF),
            shape((TOKENS, WIDE), F32),
            shape((TOKENS, COLS), BF),
            shape((TOKENS, COLS), F32),
        ),
        core, x_all, w_mine, w_other, pre_fv, cum, floor,
        flops=2 * TOKENS * D * WIDE,
        order=(feed_own_weights,),
    )
    w_out = lax.dynamic_index_in_dim(w_out.reshape(PARTS, COLS, D), z, 0, keepdims=False)
    own_half, totals = kernel_call(
        functools.partial(carry_kernel, backward=False),
        (near_shape(half_dims, BF), shape((8, HALF, HEAD_DIM), F32)),
        place, arrived,
        order=(q_in, w_out),
    )
    mixed, normed_out, entered, *parts = kernel_call(
        mix_kernel,
        (shape((TOKENS, COLS), F32), shape((TOKENS, COLS), BF), shape(state_dims, BF), *own),
        core, pre_qg, q_in, local_out, own_half, shift(own_half, "c", 1), other_end, other_total, w_out,
        flops=2 * TOKENS * COLS * D,
        near=(4, 5),
    )
    middle, feed_own = kernel_call(
        middle_kernel, (shape((ROWS, D), F32), near_shape((ROWS, D), BF)), hidden, *scatter_z(parts),
        near=(1, 2, 3, 4),
    )
    f_all, g_all, act, grad_up, w_down, parts = kernel_call(
        feed_kernel,
        (
            shape((TOKENS, D), BF),
            shape((TOKENS, D), BF),
            shape((TOKENS, PAD), BF),
            shape((TOKENS, 2 * PAD), BF),
            shape((PAD, D), BF),
            shape((PARTS, ROWS, D), BF),
        ),
        z_of, *gather_z(feed_own), grads_out, w_feed,
        flops=2 * TOKENS * D * PAD * 5,
    )
    feed_back = exchange(parts, "z")
    feed_grad, *down_parts = kernel_call(
        feed_grad_kernel,
        (shape((16, FEED_ROWS, 2 * PAD), BF), *[shape((ROWS, D), BF)] * 4),
        f_all, grad_up, act, g_all, w_down,
        flops=2 * TOKENS * D * PAD * 3,
        order=(parts,),
    )
    grad_middle, branch_own = kernel_call(
        branch_kernel, (shape((ROWS, D), F32), near_shape((ROWS, D), BF)), middle, out_grad, feed_back,
        order=(feed_grad,),
    )
    feed_sum = lax.psum_scatter(after(feed_grad, feed_back), ("x", "yl", "c"), scatter_dimension=0)
    branch = gather_z(branch_own)
    branch_all, grad_gate, grad_mixed, end_grad = kernel_call(
        head_back_kernel,
        (
            shape((TOKENS, D), BF),
            shape((TOKENS, COLS), BF),
            shape((TOKENS, COLS), BF),
            near_shape(state_dims, BF),
        ),
        *branch, w_out, pre_qg, q_in, mixed,
        flops=2 * TOKENS * COLS * D,
        near=(0, 1, 2, 3),
    )

    sent, other_end = chip_state(end_grad, other_total, True)
    down_parts = scatter_z(after(down_parts, sent))
    arrived = exchange(sent, ("x", "yl"))
    grad_qg, near_log, near_key, near_value, qg_mine, qg_other, out_mine, out_other = kernel_call(
        near_back_kernel,
        (
            shape((TOKENS, WIDE), BF),
            *[shape((TOKENS, COLS), F32)] * 3,
            *[shape((8, 64, WIDE), BF)] * 2,
            *[shape((2, 64, D), BF)] * 2,
        ),
        core, x_all, normed_out, branch_all, pre_qg, pre_fv, cum, floor, q_in, grad_gate, grad_mixed, entered,
        scratch=[pltpu.VMEM((8, 2, 64, WIDE), BF), pltpu.VMEM((2, 2, 64, D), BF)],
        flops=2 * TOKENS * (HEAD_DIM * HEAD_DIM * 12 + D * WIDE),
        order=(sent,),
    )
    qg_packed = kernel_call(
        pack_kernel, shape((16, 192, 128), BF), qg_mine, shift(qg_other, "c", 1), out_mine, shift(out_other, "c", 1)
    )
    own_half = kernel_call(
        functools.partial(carry_kernel, backward=True), near_shape(half_dims, BF), place, arrived, totals,
        order=(qg_packed, *down_parts),
    )
    qg_arrived = exchange(after(qg_packed, own_half), ("x", "yl", "yh"))
    floor_part, fv_mine, fv_other, *parts = kernel_call(
        far_back_kernel,
        (shape((1, COLS), F32), *[shape((8, 64, WIDE), BF)] * 2, *[shape((ROWS, D), BF)] * 4),
        core, pre_fv, cum, floor, near_log, near_key, near_value, entered, own_half, shift(own_half, "c", 1), other_end,
        other_total, grad_qg, w_fv, w_qg, x_all,
        scratch=[pltpu.VMEM((TOKENS, WIDE), BF), pltpu.VMEM((8, 2, 64, WIDE), BF)],
        flops=2 * TOKENS * D * D * 2,
    )
    sent = kernel_call(
        pack_last_kernel, shape((16, 144, 128), BF), fv_mine, shift(fv_other, "c", 1), floor_part,
        shift(floor_part, "c", 1),
        order=(qg_arrived,),
    )

    arrived = exchange(sent, ("x", "yl", "yh"))
    feed_other = shift(after(feed_sum, sent), "yh", 1)
    parts = scatter_z(after(parts, sent))
    qg_columns, out_rows = kernel_call(
        sum_kernel, (shape((128, 128), BF), shape((64, 128), BF)), qg_arrived, order=(sent,)
    )
    feed_total = kernel_call(
        add_kernel, shape((FEED_ROWS, 2 * PAD), BF), feed_sum, feed_other, order=(qg_columns,)
    )
    grad_tokens = kernel_call(
        last_kernel, shape((ROWS, D), BF), hidden, grad_middle, *parts, order=(qg_columns,)
    )
    last_copies = kernel_call(
        sum_last_kernel, shape((8, 336, 128), BF), arrived, qg_columns, transpose_xz(out_rows), order=(grad_tokens, feed_total)
    )
    last_sums = exchange(last_copies, ("yh", "z"))
    feed_totals = gather_z(after(feed_total, last_copies))
    result = kernel_call(
        result_kernel, shape((ROWS, D), BF), middle, *down_parts, order=(last_copies,)
    )
    up_grad, feed_gain_grad, down_grad = kernel_call(
        feed_grads_kernel,
        (shape((64, 2 * FF), F32), shape((1, 64), F32), shape((OWNED, D), F32)),
        z_of, *feed_totals, gate_up_weight, gain_two,
        order=(result,),
    )
    mix_grad, gain_grad, out_weight_grad, group_gain_grad, floor_grad = kernel_call(
        mix_grads_kernel,
        (
            shape((64, 4 * D), F32),
            shape((1, 64), F32),
            shape((64, D), F32),
            shape((1, 64), F32),
            shape((1, D), F32),
        ),
        last_sums, mixer_weight, gain_one, output_weight, gain_group,
        order=(up_grad,),
    )
    return (
        result,
        grad_tokens,
        mix_grad,
        out_weight_grad,
        up_grad,
        down_grad,
        gain_grad.reshape(64),
        group_gain_grad.reshape(64),
        feed_gain_grad.reshape(64),
        floor_grad.reshape(D),
    )


def solution(mesh):
    cut = Mesh(mesh.devices.reshape(2, 4, 4, 2, 2), AXES)
    seq = ("x", "yl", "c")
    rows, weight, vector = P(AXES, None), P(seq, None), P(seq)
    in_specs = (rows, weight, weight, weight, weight, vector, vector, vector, P(), rows)
    out_specs = (rows, rows, weight, weight, weight, weight, vector, vector, vector, P())
    return jax.shard_map(body, mesh=cut, in_specs=in_specs, out_specs=out_specs, check_vma=False)
```

```python
import functools

import jax
import jax.numpy as jnp
from jax import lax
from jax.experimental import pallas as pl
from jax.experimental.pallas import tpu as pltpu
from jax.sharding import Mesh, PartitionSpec as P

D = 1024
HEADS = 8
HEAD_DIM = 128
FF = 2816
EPS = 1e-06

ROWS = 128
PARTS = 4
COLS = D // PARTS
TOKENS = PARTS * ROWS
WIDE = 2 * COLS
PAD = 768
SLOT, TAKEN, OWNED = 48, 44, 176
SLOTS, UNITS = 8 * SLOT, 8 * OWNED
FEED_ROWS = 96
LOCAL_HEADS = 2
STATES = PARTS * LOCAL_HEADS
HALF = STATES // 2
TAIL = 16
BF = jnp.bfloat16
F32 = jnp.float32
AXES = ("yh", "z", "x", "yl", "c")
VMEM = 40 * 1024 * 1024


def shift(value, axis, by):
    n = lax.axis_size(axis)
    return lax.ppermute(value, axis, [(i, (i + by) % n) for i in range(n)])


def gather_z(own):
    return (own, shift(own, "z", 1), shift(own, "z", -1), shift(own, "z", 2))


def scatter_z(parts):
    return (parts[0], shift(parts[1], "z", -1), shift(parts[2], "z", 1), shift(parts[3], "z", 2))


def transpose_xz(value):
    pairs = [(z * 4 + x, x * 4 + z) for z in range(4) for x in range(4)]
    return lax.ppermute(value, ("z", "x"), pairs)


def quarters(z):
    return [lax.rem(z + by, 4) for by in (0, 3, 1, 2)]


def exchange(value, axes):
    return lax.all_to_all(value, axes, 0, 0)


def after(value, *others):
    return lax.optimization_barrier((value, *others))[0]


def kernel_call(body, out_shape, *args, scratch=(), flops=0, order=(), near=()):
    if order:
        args = after(args, *order)
    args = [
        a if a.dtype == jnp.int32 else pltpu.with_memory_space_constraint(a, pltpu.VMEM if i in near else pltpu.HBM)
        for i, a in enumerate(args)
    ]
    in_specs = [
        pl.BlockSpec(memory_space=pltpu.SMEM) if a.dtype == jnp.int32 else pl.BlockSpec(memory_space=pltpu.VMEM)
        for a in args
    ]
    out_specs = jax.tree.map(lambda _: pl.BlockSpec(memory_space=pltpu.VMEM), out_shape)
    return pl.pallas_call(
        body,
        out_shape=out_shape,
        in_specs=in_specs,
        out_specs=out_specs,
        scratch_shapes=list(scratch),
        compiler_params=pltpu.CompilerParams(vmem_limit_bytes=VMEM),
        cost_estimate=pl.CostEstimate(flops=1, bytes_accessed=1, transcendentals=0),
    )(*args)


def shape(dims, dtype):
    return pltpu.HBM(dims, dtype)


def near_shape(dims, dtype):
    return pltpu.VMEM(dims, dtype)


def dot(a, b):
    return jnp.dot(a, b, preferred_element_type=F32)


def dot_t(a, b):
    return lax.dot_general(a, b, (((1,), (1,)), ((), ())), preferred_element_type=F32)


def t_dot(a, b):
    return lax.dot_general(a, b, (((0,), (0,)), ((), ())), preferred_element_type=F32)


def exact_dot(a, b):
    return jnp.dot(a, b, precision=lax.Precision.HIGHEST, preferred_element_type=F32)


def mean_scale(value):
    return lax.rsqrt(jnp.mean(value * value, axis=-1, keepdims=True) + EPS)


def triangle(strict, upper):
    row = lax.broadcasted_iota(jnp.int32, (ROWS, ROWS), 0)
    col = lax.broadcasted_iota(jnp.int32, (ROWS, ROWS), 1)
    if upper:
        row, col = col, row
    return row > col if strict else row >= col


def swish_slope(value, sigma):
    return sigma * (1.0 + value * (1.0 - sigma))


def column(ref):
    return jnp.transpose(ref[...].astype(F32))


def row_sums(value):
    return jnp.sum(jnp.transpose(value), axis=0, keepdims=True)


def lane_blocks(value):
    total = value[:, :128]
    for j in range(128, value.shape[1], 128):
        total = total + value[:, j : j + 128]
    return total


def prepare_kernel(z_ref, w_ref, gain_ref, out_w_ref, out_gain_ref, sent_ref, out_ref):
    start = z_ref[0] * COLS
    gain = column(gain_ref)
    for to, j in enumerate((1, 2, 0, 3)):
        cols = pl.ds(pl.multiple_of(j * D + start, 128), COLS)
        block = (w_ref[:, cols].astype(F32) * gain).astype(BF)
        for i in range(8):
            sent_ref[i, :, to * COLS : (to + 1) * COLS] = block
    out_ref[...] = (out_w_ref[...].astype(F32) * column(out_gain_ref)).astype(BF)


def selection(z, slots, units, slots_first):
    shape_ = (slots, units) if slots_first else (units, slots)
    line = (slots, 1) if slots_first else (1, slots)
    slot = lax.broadcasted_iota(jnp.int32, line, 0 if slots_first else 1)
    owner = jnp.zeros(line, jnp.int32)
    for i in range(1, slots // SLOT):
        owner = owner + (slot >= i * SLOT).astype(jnp.int32)
    place = slot - owner * SLOT
    unit = jnp.where(place < TAKEN, owner * OWNED + z * TAKEN + place, -1)
    return jnp.where(lax.broadcasted_iota(jnp.int32, shape_, 1 if slots_first else 0) == unit, 1.0, 0.0).astype(BF)


def prepare_feed_kernel(z_ref, up_ref, gain_ref, down_ref, out_ref):
    gain = column(gain_ref)
    chosen = selection(z_ref[0], SLOTS, UNITS, False)
    for i in range(4):
        picked = dot(up_ref[:, i * UNITS : (i + 1) * UNITS], chosen)
        out_ref[:64, i * SLOTS : (i + 1) * SLOTS] = (picked * gain).astype(BF)
    rows = dot(selection(z_ref[0], SLOT, OWNED, True), down_ref[...]).astype(BF)
    out_ref[64:, :D] = rows[:32]
    out_ref[64:80, D:] = rows[32:, :512]
    out_ref[80:, D:] = rows[32:, 512:]


def gated(pre, floor):
    sigma = lax.logistic(pre)
    return sigma, floor + (1.0 - floor) * sigma


def swish(value):
    return value * lax.logistic(value)


def head_cols(h):
    return slice(h * HEAD_DIM, (h + 1) * HEAD_DIM)


def part_rows(b):
    return slice(b * ROWS, (b + 1) * ROWS)


def first_kernel(core_ref, x0, x1, x2, x3, mine_ref, other_ref, floor_ref,
                 x_ref, w_ref, w_qg_ref, pre_ref, cum_ref, state_ref, total_ref):
    core = core_ref[0]
    for ref, lanes in ((w_ref, slice(0, WIDE)), (w_qg_ref, slice(WIDE, D))):
        ref[:, pl.ds(core, 1)] = mine_ref[:, :, lanes].reshape(8, 1, 64, WIDE)
        ref[:, pl.ds(1 - core, 1)] = other_ref[:, :, lanes].reshape(8, 1, 64, WIDE)
    for b, part in enumerate((x0, x1, x2, x3)):
        value = part[...].astype(F32)
        x_ref[part_rows(b), :] = (value * mean_scale(value)).astype(BF)
    pre_ref[...] = dot(x_ref[...], w_ref[...].reshape(D, WIDE))
    ones = triangle(False, False).astype(F32)
    floor = floor_ref[...]
    for b in range(PARTS):
        rows = part_rows(b)
        _, decay = gated(pre_ref[rows, :COLS], floor)
        cum_all = exact_dot(ones, jnp.log(decay))
        cum_ref[rows, :] = cum_all
        total_all = cum_all[ROWS - 1 :, :]
        k_out = ((1.0 - decay).astype(BF).astype(F32) * jnp.exp(total_all - cum_all)).astype(BF)
        for h in range(LOCAL_HEADS):
            value = pre_ref[rows, COLS + h * HEAD_DIM : COLS + (h + 1) * HEAD_DIM].astype(BF)
            s = h * PARTS + b
            state_ref[s] = t_dot(k_out[:, head_cols(h)], value).astype(BF)
            total_ref[s : s + 1, :] = total_all[:, head_cols(h)]


def second_kernel(x_ref, w_ref, fv_ref, cum_ref, floor_ref, pre_ref, q_ref, local_ref):
    pre_ref[...] = dot(x_ref[...], w_ref[...].reshape(D, WIDE))
    causal = triangle(False, False)
    floor = floor_ref[...]
    for b in range(PARTS):
        rows = part_rows(b)
        _, decay = gated(fv_ref[rows, :COLS], floor)
        cum = cum_ref[rows, :]
        k_in = ((1.0 - decay).astype(BF).astype(F32) * jnp.exp(-cum)).astype(BF)
        q_in = (swish(pre_ref[rows, :COLS]).astype(BF).astype(F32) * jnp.exp(cum)).astype(BF)
        q_ref[rows, :] = q_in
        value = fv_ref[rows, COLS:].astype(BF)
        for h in range(LOCAL_HEADS):
            cols = head_cols(h)
            scores = jnp.where(causal, dot_t(q_in[:, cols], k_in[:, cols]), 0.0).astype(BF)
            local_ref[rows, cols] = dot(scores, value[:, cols])


def split3(value):
    first = value.astype(BF).astype(F32)
    second = (value - first).astype(BF).astype(F32)
    return first, second, value - first - second


def chip_kernel(core_ref, mine_ref, other_ref, my_total_ref, other_total_ref, out_ref, *, backward):
    core = core_ref[0]
    second = core == (0 if backward else 1)
    base = core * HALF
    my_total = my_total_ref[pl.ds(base, HALF), :]
    other_total = other_total_ref[pl.ds(base, HALF), :]
    last_decay = jnp.exp(jnp.where(second, my_total, other_total))
    for i in range(HALF):
        mine = mine_ref[base + i].astype(F32)
        other = other_ref[base + i].astype(F32)
        last = jnp.where(second, mine, other)
        first = jnp.where(second, other, mine)
        state = (jnp.transpose(last_decay[i : i + 1, :]) * first + last).astype(BF)
        for d in range(8):
            out_ref[d, i * HEAD_DIM : (i + 1) * HEAD_DIM, :] = state
    if not backward:
        pieces = split3(my_total + other_total)
        tail = jnp.concatenate([*pieces, jnp.zeros((HALF, HEAD_DIM), F32)], axis=0).astype(BF)
        for d in range(8):
            out_ref[d, HALF * HEAD_DIM :, :] = tail


def carry_kernel(place_ref, all_ref, *refs, backward):
    place = place_ref[0]
    if backward:
        totals_ref, out_ref = refs
    else:
        out_ref, totals_ref = refs
        for j in range(8):
            tail = all_ref[j, HALF * HEAD_DIM :, :].astype(F32)
            totals_ref[j] = (tail[:HALF] + tail[HALF : 2 * HALF]) + tail[2 * HALF : 3 * HALF]
    for i in range(HALF):
        carried = jnp.zeros((HEAD_DIM, HEAD_DIM), F32)
        decays = jnp.transpose(jnp.exp(jnp.concatenate([totals_ref[j, i : i + 1, :] for j in range(8)], axis=0)))
        for step in range(7):
            j = 7 - step if backward else step
            reached = j > place if backward else j < place
            block = all_ref[j, i * HEAD_DIM : (i + 1) * HEAD_DIM, :].astype(F32)
            carried = jnp.where(reached, decays[:, j : j + 1] * carried + block, carried)
        out_ref[i] = carried.astype(BF)


def enter_state(core, own_half, other_half, other_end, other_total, s, backward):
    h, b = divmod(s, PARTS)
    chip = jnp.where(core == h, own_half[b], other_half[b]).astype(F32)
    later = core == (0 if backward else 1)
    passed = jnp.transpose(jnp.exp(other_total[s : s + 1, :])) * chip + other_end[s].astype(F32)
    return jnp.where(later, passed, chip)


def mix_kernel(core_ref, pre_ref, q_ref, local_ref, own_half, other_half, other_end, other_total, w_ref,
               out_ref, normed_ref, entered_ref, p0, p1, p2, p3):
    core = core_ref[0]
    for b in range(PARTS):
        rows = part_rows(b)
        for h in range(LOCAL_HEADS):
            cols = head_cols(h)
            s = h * PARTS + b
            state = enter_state(core, own_half, other_half, other_end, other_total, s, False).astype(BF)
            entered_ref[s] = state
            mixed = local_ref[rows, cols] + dot(q_ref[rows, cols], state)
            out_ref[rows, cols] = mixed
            gate = pre_ref[rows, COLS + h * HEAD_DIM : COLS + (h + 1) * HEAD_DIM]
            normed_ref[rows, cols] = (mixed * mean_scale(mixed) * swish(gate)).astype(BF)
    product = dot(normed_ref[...], w_ref[...]).astype(BF)
    for b, part in enumerate((p0, p1, p2, p3)):
        part[...] = product[part_rows(b), :]


def sum_parts(p0, p1, p2, p3):
    return (p0[...].astype(F32) + p1[...].astype(F32)) + (p2[...].astype(F32) + p3[...].astype(F32))


def middle_kernel(hidden_ref, p0, p1, p2, p3, middle_ref, normed_ref):
    middle = hidden_ref[...].astype(F32) + sum_parts(p0, p1, p2, p3)
    middle_ref[...] = middle
    normed_ref[...] = (middle * mean_scale(middle)).astype(BF)


def feed_inputs(parts, grads, w_ref, x_ref, g_ref, down_ref):
    for s in range(16):
        at = s * SLOT
        rows = w_ref[s, w_ref.shape[1] - 32 :, :]
        down_ref[at : at + 32, :] = rows[:, :D]
        down_ref[at + 32 : at + 48, :512] = rows[:16, D:]
        down_ref[at + 32 : at + 48, 512:] = rows[16:, D:]
    for b in range(PARTS):
        x_ref[part_rows(b), :] = parts[b][...]
        g_ref[part_rows(b), :] = grads[b][...]


def feed_kernel(x0, x1, x2, x3, g0, g1, g2, g3, w_ref, act_ref, grad_ref, p0, p1, p2, p3, x_ref, g_ref, down_ref):
    feed_inputs((x0, x1, x2, x3), (g0, g1, g2, g3), w_ref, x_ref, g_ref, down_ref)
    for j in range(3):
        lanes = slice(j * COLS, (j + 1) * COLS)
        ups = slice(PAD + j * COLS, PAD + (j + 1) * COLS)
        gate = dot(x_ref[...], w_ref[:, :64, lanes].reshape(D, COLS))
        up = dot(x_ref[...], w_ref[:, :64, ups].reshape(D, COLS))
        grad = dot_t(g_ref[...], down_ref[lanes, :])
        sigma = lax.logistic(gate)
        active = gate * sigma
        act_ref[:, lanes] = (active * up).astype(BF)
        grad_ref[:, lanes] = (grad * up * swish_slope(gate, sigma)).astype(BF)
        grad_ref[:, ups] = (grad * active).astype(BF)
    product = dot_t(grad_ref[...], w_ref[:, :64, :].reshape(D, 2 * PAD)).astype(BF)
    for b, part in enumerate((p0, p1, p2, p3)):
        part[...] = product[part_rows(b), :]


def feed_grad_kernel(x0, x1, x2, x3, g0, g1, g2, g3, w_ref, grad_ref, act_ref, out_ref, p0, p1, p2, p3,
                     x_ref, g_ref, down_ref):
    feed_inputs((x0, x1, x2, x3), (g0, g1, g2, g3), w_ref, x_ref, g_ref, down_ref)
    product = dot(act_ref[...], down_ref[...]).astype(BF)
    for b, part in enumerate((p0, p1, p2, p3)):
        part[...] = product[part_rows(b), :]
    for j in range(0, 2 * PAD, 512):
        out_ref[:, :64, j : j + 512] = t_dot(x_ref[...], grad_ref[:, j : j + 512]).astype(BF).reshape(16, 64, 512)
    rows = t_dot(act_ref[...], g_ref[...]).astype(BF)
    for s in range(16):
        at = s * SLOT
        out_ref[s, 64:, :D] = rows[at : at + 32]
        out_ref[s, 64:80, D:] = rows[at + 32 : at + 48, :512]
        out_ref[s, 80:, D:] = rows[at + 32 : at + 48, 512:]


def add_kernel(a_ref, b_ref, out_ref):
    out_ref[...] = (a_ref[...].astype(F32) + b_ref[...].astype(F32)).astype(BF)


def result_kernel(middle_ref, p0, p1, p2, p3, out_ref):
    out_ref[...] = (middle_ref[...] + sum_parts(p0, p1, p2, p3)).astype(BF)


def norm_back(value_ref, base_ref, u):
    value = value_ref[...].astype(F32)
    scale = mean_scale(value)
    centered = value * scale
    back = scale * (u - centered * jnp.mean(u * centered, axis=-1, keepdims=True))
    return base_ref[...].astype(F32) + back


def branch_kernel(value_ref, base_ref, p0, p1, p2, p3, out_ref, low_ref):
    total = norm_back(value_ref, base_ref, sum_parts(p0, p1, p2, p3))
    out_ref[...] = total
    low_ref[...] = total.astype(BF)


def last_kernel(value_ref, base_ref, p0, p1, p2, p3, low_ref):
    low_ref[...] = norm_back(value_ref, base_ref, sum_parts(p0, p1, p2, p3)).astype(BF)


def head_back_kernel(b0, b1, b2, b3, w_ref, pre_ref, q_ref, mixed_ref, branch_ref, gate_ref, out_grad_ref, state_ref):
    for b, part in enumerate((b0, b1, b2, b3)):
        branch_ref[part_rows(b), :] = part[...]
    grads = dot_t(branch_ref[...], w_ref[...])
    for b in range(PARTS):
        rows = part_rows(b)
        for h in range(LOCAL_HEADS):
            cols = head_cols(h)
            grad = grads[rows, cols]
            mixed = mixed_ref[rows, cols]
            scale = mean_scale(mixed)
            normed = mixed * scale
            gate = pre_ref[rows, COLS + h * HEAD_DIM : COLS + (h + 1) * HEAD_DIM]
            sigma = lax.logistic(gate)
            gate_ref[rows, cols] = (grad * normed * swish_slope(gate, sigma)).astype(BF)
            c = grad * (gate * sigma)
            mixer = (scale * (c - normed * jnp.mean(c * normed, axis=-1, keepdims=True))).astype(BF)
            out_grad_ref[rows, cols] = mixer
            state_ref[h * PARTS + b] = t_dot(q_ref[rows, cols], mixer).astype(BF)


def near_back_kernel(core_ref, x_ref, normed_ref, branch_ref, qg_ref, fv_ref, cum_ref, floor_ref, q_ref, gate_ref,
                     out_grad_ref, entered_ref, grad_ref, log_ref, key_ref, value_ref,
                     mine_ref, other_ref, my_rows_ref, other_rows_ref, all_ref, rows_ref):
    causal = triangle(False, False)
    suffix = triangle(False, True).astype(F32)
    floor = floor_ref[...]
    for b in range(PARTS):
        rows = part_rows(b)
        _, decay = gated(fv_ref[rows, :COLS], floor)
        cum = cum_ref[rows, :]
        grow_all = jnp.exp(cum)
        shrink_all = jnp.exp(-cum)
        k_all = ((1.0 - decay).astype(BF).astype(F32) * shrink_all).astype(BF)
        q_pre = qg_ref[rows, :COLS]
        slope_all = swish_slope(q_pre, lax.logistic(q_pre))
        for h in range(LOCAL_HEADS):
            cols = head_cols(h)
            value = fv_ref[rows, COLS + h * HEAD_DIM : COLS + (h + 1) * HEAD_DIM].astype(BF)
            q_in, k_in = q_ref[rows, cols], k_all[:, cols]
            out_grad = out_grad_ref[rows, cols]
            scores = jnp.where(causal, dot_t(q_in, k_in), 0.0).astype(BF)
            grad_scores = jnp.where(causal, dot_t(out_grad, value), 0.0).astype(BF)
            inner = dot(grad_scores, k_in) + dot_t(out_grad, entered_ref[h * PARTS + b])
            back = t_dot(grad_scores, q_in)
            near = q_in.astype(F32) * inner - k_in.astype(F32) * back
            log_ref[rows, cols] = exact_dot(suffix, near)
            key_ref[rows, cols] = back * shrink_all[:, cols]
            value_ref[rows, cols] = t_dot(scores, out_grad)
            grad_ref[rows, cols] = (inner * grow_all[:, cols] * slope_all[:, cols]).astype(BF)
    grad_ref[:, COLS:] = gate_ref[...]
    column_grad(core_ref[0], x_ref, grad_ref, mine_ref, other_ref, all_ref)
    row_grad(core_ref[0], normed_ref, branch_ref, my_rows_ref, other_rows_ref, rows_ref)


def far_back_kernel(core_ref, fv_ref, cum_ref, floor_ref, log_ref, key_ref, value_ref, entered_ref, own_half, other_half,
                    other_end, other_total, qg_ref, w_fv_ref, w_qg_ref, x_ref,
                    floor_grad_ref, mine_ref, other_ref, p0, p1, p2, p3, grad_ref, all_ref):
    core = core_ref[0]
    before = triangle(True, False).astype(F32)
    floor = floor_ref[...]
    floor_sum = jnp.zeros((1, COLS), F32)
    for b in range(PARTS):
        rows = part_rows(b)
        sigma, decay = gated(fv_ref[rows, :COLS], floor)
        cum = cum_ref[rows, :]
        total = cum[ROWS - 1 :, :]
        to_end = jnp.exp(total - cum)
        k_all = ((1.0 - decay).astype(BF).astype(F32) * to_end).astype(BF)
        aheads, edges = [], []
        for h in range(LOCAL_HEADS):
            cols = head_cols(h)
            s = h * PARTS + b
            following = enter_state(core, own_half, other_half, other_end, other_total, s, True)
            low = following.astype(BF)
            value = fv_ref[rows, COLS + h * HEAD_DIM : COLS + (h + 1) * HEAD_DIM].astype(BF)
            aheads.append(dot_t(value, low))
            edges.append(jnp.transpose(jnp.sum(following * entered_ref[s].astype(F32), axis=1, keepdims=True)))
            grad_value = value_ref[rows, cols] + dot(k_all[:, cols], low)
            grad_ref[rows, COLS + h * HEAD_DIM : COLS + (h + 1) * HEAD_DIM] = grad_value.astype(BF)
        ahead = jnp.concatenate(aheads, axis=1)
        edge = jnp.concatenate(edges, axis=1)
        far = exact_dot(before, k_all.astype(F32) * ahead)
        grad_log = log_ref[rows, :] + far + jnp.exp(total) * edge
        grad_decay = grad_log / decay - (key_ref[rows, :] + ahead * to_end)
        floor_sum = floor_sum + jnp.sum(grad_decay * (1.0 - sigma), axis=0, keepdims=True)
        grad_ref[rows, :COLS] = (grad_decay * (1.0 - floor) * sigma * (1.0 - sigma)).astype(BF)
    floor_grad_ref[...] = floor_sum
    column_grad(core, x_ref, grad_ref, mine_ref, other_ref, all_ref)
    product = dot_t(grad_ref[...], w_fv_ref[...].reshape(D, WIDE)) + dot_t(qg_ref[...], w_qg_ref[...].reshape(D, WIDE))
    product = product.astype(BF)
    for b, part in enumerate((p0, p1, p2, p3)):
        part[...] = product[part_rows(b), :]


def column_grad(core, a_ref, g_ref, mine_ref, other_ref, all_ref):
    n = g_ref.shape[1]
    all_ref[...] = t_dot(a_ref[...], g_ref[...]).astype(BF).reshape(8, 2, 64, n)
    mine_ref[...] = all_ref[:, pl.ds(core, 1)].reshape(8, 64, n)
    other_ref[...] = all_ref[:, pl.ds(1 - core, 1)].reshape(8, 64, n)


def row_grad(core, a_ref, g_ref, mine_ref, other_ref, all_ref):
    rows = mine_ref.shape[1]
    all_ref[...] = t_dot(a_ref[...], g_ref[...]).astype(BF).reshape(2, 2, rows, D)
    mine_ref[...] = all_ref[:, pl.ds(core, 1)].reshape(2, rows, D)
    other_ref[...] = all_ref[:, pl.ds(1 - core, 1)].reshape(2, rows, D)


def pack_columns(mine_ref, other_ref, out_ref, start):
    lanes = mine_ref.shape[2] // 2
    for i in range(8):
        value = (mine_ref[i].astype(F32) + other_ref[i].astype(F32)).astype(BF)
        for half in range(2):
            for j in range(lanes // 128):
                at = half * lanes + j * 128
                out_ref[i * 2 + half, start + j * 64 : start + (j + 1) * 64, :] = value[:, at : at + 128]


def pack_rows(mine_ref, other_ref, out_ref, start):
    rows = mine_ref.shape[1]
    for yl in range(2):
        value = (mine_ref[yl].astype(F32) + other_ref[yl].astype(F32)).astype(BF)
        for p in range(8):
            to = (p // 2) * 4 + yl * 2 + p % 2
            out_ref[to, start : start + rows, :] = value[:, p * 128 : (p + 1) * 128]


def rider_rows(value):
    rows = [piece[:, cols] for piece in split3(value) for cols in (slice(0, 128), slice(128, 256))]
    return jnp.concatenate([*rows, jnp.zeros((10, 128), F32)], axis=0).astype(BF)


def rider_value(rows):
    rows = rows.astype(F32)
    halves = [(rows[i : i + 1] + rows[i + 2 : i + 3]) + rows[i + 4 : i + 5] for i in range(2)]
    return jnp.concatenate(halves, axis=1)


def pack_kernel(mine_ref, other_ref, floor_ref, other_floor_ref, my_qg_ref, other_qg_ref, my_rows_ref, other_rows_ref, out_ref):
    pack_columns(mine_ref, other_ref, out_ref, 0)
    rider = rider_rows(floor_ref[...] + other_floor_ref[...])
    for i in range(16):
        out_ref[i, 128:144, :] = rider
    pack_columns(my_qg_ref, other_qg_ref, out_ref, 144)
    pack_rows(my_rows_ref, other_rows_ref, out_ref, 272)


def total_of(all_ref, rows):
    total = all_ref[0, rows, :].astype(F32)
    for i in range(1, 16):
        total = total + all_ref[i, rows, :].astype(F32)
    return total


def sum_kernel(all_ref, columns_ref, rows_ref):
    columns_ref[:128, :] = total_of(all_ref, slice(0, 128)).astype(BF)
    floor = rider_value(all_ref[0, 128:144, :])
    for i in range(1, 16):
        floor = floor + rider_value(all_ref[i, 128:144, :])
    columns_ref[128:144, :] = rider_rows(floor)
    columns_ref[144:, :] = total_of(all_ref, slice(144, 272)).astype(BF)
    rows_ref[...] = total_of(all_ref, slice(272, 336)).astype(BF)


def copies_kernel(columns_ref, rows_ref, out_ref):
    for i in range(8):
        out_ref[i, :272, :] = columns_ref[...]
        out_ref[i, 272:, :] = rows_ref[...]


def feed_grads_kernel(z_ref, s0, s1, s2, s3, w_ref, gain_ref, up_ref, gain_grad_ref, down_ref):
    chosen = jnp.concatenate([selection(z, SLOTS, UNITS, True) for z in quarters(z_ref[0])], axis=0)
    gain = column(gain_ref)
    gain_grad = jnp.zeros((64, 128), F32)
    taken = jnp.concatenate(
        [
            jnp.concatenate([ref[:64, i * SLOTS : (i + 1) * SLOTS] for ref in (s0, s1, s2, s3)], axis=1)
            for i in range(4)
        ],
        axis=0,
    )
    values = dot(taken, chosen)
    for i in range(4):
        value = values[i * 64 : (i + 1) * 64]
        cols = slice(i * UNITS, (i + 1) * UNITS)
        up_ref[:, cols] = value * gain
        gain_grad = gain_grad + lane_blocks(value * w_ref[:, cols].astype(F32))
    gain_grad_ref[...] = row_sums(gain_grad)
    down = jnp.zeros((OWNED, D), F32)
    for z, ref in zip(quarters(z_ref[0]), (s0, s1, s2, s3)):
        last = jnp.concatenate([ref[64:80, D:], ref[80:, D:]], axis=1)
        rows = jnp.concatenate([ref[64:, :D], last], axis=0)
        down = down + dot(selection(z, SLOT, OWNED, False), rows)
    down_ref[...] = down


def mix_grads_kernel(all_ref, w_ref, gain_ref, out_w_ref, out_gain_ref,
                     mix_ref, gain_grad_ref, out_ref, out_gain_grad_ref, floor_ref):
    gain, out_gain = column(gain_ref), column(out_gain_ref)
    gain_grad = jnp.zeros((64, 128), F32)
    out_gain_grad = jnp.zeros((64, 128), F32)
    for yh in range(2):
        for z in range(4):
            i = yh * 4 + z
            for start, block in ((0, 2 if yh else 1), (144, 3 if yh else 0)):
                for j in range(2):
                    value = all_ref[i, start + j * 64 : start + (j + 1) * 64, :].astype(F32)
                    at = block * D + z * COLS + j * 128
                    mix_ref[:, at : at + 128] = value * gain
                    gain_grad = gain_grad + value * w_ref[:, at : at + 128].astype(F32)
            p = z * 2 + yh
            value = all_ref[i, 272:, :].astype(F32)
            cols = slice(p * 128, (p + 1) * 128)
            out_ref[:, cols] = value * out_gain
            out_gain_grad = out_gain_grad + value * out_w_ref[:, cols].astype(F32)
            if yh == 0:
                floor_ref[:, z * COLS : (z + 1) * COLS] = rider_value(all_ref[i, 128:144, :])
    gain_grad_ref[...] = row_sums(gain_grad)
    out_gain_grad_ref[...] = row_sums(out_gain_grad)


def scalar(value):
    return value.reshape(1).astype(jnp.int32)


def body(hidden, mixer_weight, output_weight, gate_up_weight, down_weight, mixer_gain, group_gain, feed_gain,
         forget_floor, out_grad):
    z = lax.axis_index("z")
    z_of = scalar(z)
    core = scalar(lax.axis_index("c"))
    place = scalar(lax.axis_index("x") * 2 + lax.axis_index("yl"))
    gain_one, gain_group, gain_two = (g.reshape(1, 64) for g in (mixer_gain, group_gain, feed_gain))
    floor = lax.dynamic_index_in_dim(forget_floor.reshape(PARTS, COLS), z, 0)
    own = [near_shape((ROWS, D), BF)] * 4
    state_dims = (STATES, HEAD_DIM, HEAD_DIM)
    half_dims = (HALF, HEAD_DIM, HEAD_DIM)

    w_sent, out_own = kernel_call(
        prepare_kernel, (shape((8, 64, D), BF), shape((64, D), BF)),
        z_of, mixer_weight, gain_one, output_weight, gain_group,
    )
    tokens = gather_z(hidden)
    w_mine = exchange(w_sent, ("x", "yl"))
    w_out = lax.all_gather(out_own, ("x", "yl", "c"))
    w_other = shift(after(w_mine, *tokens), "c", 1)
    x_all, w_fv, w_qg, pre_fv, cum, end, total = kernel_call(
        first_kernel,
        (
            shape((TOKENS, D), BF),
            shape((8, 2, 64, WIDE), BF),
            shape((8, 2, 64, WIDE), BF),
            shape((TOKENS, WIDE), F32),
            shape((TOKENS, COLS), F32),
            near_shape(state_dims, BF),
            shape((STATES, HEAD_DIM), F32),
        ),
        core, *tokens, w_mine, w_other, floor,
        flops=2 * TOKENS * D * WIDE,
        near=(5, 6),
    )

    def chip_state(end_state, other_total, backward, order=()):
        other_end = shift(end_state, "c", 1)
        sent = kernel_call(
            functools.partial(chip_kernel, backward=backward),
            shape((8, HALF * HEAD_DIM + (0 if backward else TAIL), HEAD_DIM), BF),
            core, end_state, other_end, total, other_total,
            order=order,
            near=(1, 2),
        )
        return sent, other_end

    other_total = shift(total, "c", 1)
    sent, other_end = chip_state(end, other_total, False)
    arrived = exchange(sent, ("x", "yl"))
    grads_out = gather_z(after(out_grad, sent))
    pre_qg, q_in, local_out = kernel_call(
        second_kernel,
        (shape((TOKENS, WIDE), F32), shape((TOKENS, COLS), BF), shape((TOKENS, COLS), F32)),
        x_all, w_qg, pre_fv, cum, floor,
        flops=2 * TOKENS * D * WIDE,
        order=(sent,),
    )
    w_out = lax.dynamic_index_in_dim(w_out.reshape(PARTS, COLS, D), z, 0, keepdims=False)
    feed_own_weights = kernel_call(
        prepare_feed_kernel, shape((FEED_ROWS, 2 * PAD), BF), z_of, gate_up_weight, gain_two, down_weight,
        order=(q_in, w_out),
    )
    w_feed = lax.all_gather(after(feed_own_weights, arrived, *grads_out), ("x", "yl", "c"))
    own_half, totals = kernel_call(
        functools.partial(carry_kernel, backward=False),
        (near_shape(half_dims, BF), shape((8, HALF, HEAD_DIM), F32)),
        place, arrived,
        order=(feed_own_weights, w_out, *grads_out),
        near=(1,),
    )
    mixed, normed_out, entered, *parts = kernel_call(
        mix_kernel,
        (shape((TOKENS, COLS), F32), shape((TOKENS, COLS), BF), shape(state_dims, BF), *own),
        core, pre_qg, q_in, local_out, own_half, shift(own_half, "c", 1), other_end, other_total, w_out,
        flops=2 * TOKENS * COLS * D,
        near=(4, 5),
    )
    middle, feed_own = kernel_call(
        middle_kernel, (shape((ROWS, D), F32), near_shape((ROWS, D), BF)), hidden, *scatter_z(parts),
        near=(1, 2, 3, 4),
    )
    feed_in = (*gather_z(feed_own), *grads_out, w_feed)
    feed_scratch = [pltpu.VMEM((TOKENS, D), BF), pltpu.VMEM((TOKENS, D), BF), pltpu.VMEM((PAD, D), BF)]
    act, grad_up, *parts = kernel_call(
        feed_kernel,
        (shape((TOKENS, PAD), BF), shape((TOKENS, 2 * PAD), BF), *own),
        *feed_in,
        scratch=feed_scratch,
        flops=2 * TOKENS * D * PAD * 5,
    )
    feed_back = scatter_z(parts)
    feed_grad, *down_parts = kernel_call(
        feed_grad_kernel,
        (shape((16, FEED_ROWS, 2 * PAD), BF), *[shape((ROWS, D), BF)] * 4),
        *feed_in, grad_up, act,
        scratch=feed_scratch,
        flops=2 * TOKENS * D * PAD * 3,
        order=(parts[3],),
    )
    grad_middle, branch_own = kernel_call(
        branch_kernel, (shape((ROWS, D), F32), near_shape((ROWS, D), BF)), middle, out_grad, *feed_back,
        order=(feed_grad,),
        near=(2, 3, 4, 5),
    )
    feed_sum = lax.psum_scatter(after(feed_grad, *feed_back), ("x", "yl", "c"), scatter_dimension=0)
    branch = gather_z(branch_own)
    branch_all, grad_gate, grad_mixed, end_grad = kernel_call(
        head_back_kernel,
        (
            shape((TOKENS, D), BF),
            shape((TOKENS, COLS), BF),
            shape((TOKENS, COLS), BF),
            near_shape(state_dims, BF),
        ),
        *branch, w_out, pre_qg, q_in, mixed,
        flops=2 * TOKENS * COLS * D,
        near=(0, 1, 2, 3),
    )

    sent, other_end = chip_state(end_grad, other_total, True)
    down_parts = scatter_z(after(down_parts, sent))
    arrived = exchange(sent, ("x", "yl"))
    grad_qg, near_log, near_key, near_value, qg_mine, qg_other, out_mine, out_other = kernel_call(
        near_back_kernel,
        (
            shape((TOKENS, WIDE), BF),
            *[shape((TOKENS, COLS), F32)] * 3,
            *[shape((8, 64, WIDE), BF)] * 2,
            *[shape((2, 64, D), BF)] * 2,
        ),
        core, x_all, normed_out, branch_all, pre_qg, pre_fv, cum, floor, q_in, grad_gate, grad_mixed, entered,
        scratch=[pltpu.VMEM((8, 2, 64, WIDE), BF), pltpu.VMEM((2, 2, 64, D), BF)],
        flops=2 * TOKENS * (HEAD_DIM * HEAD_DIM * 12 + D * WIDE),
        order=(sent,),
    )
    own_half = kernel_call(
        functools.partial(carry_kernel, backward=True), near_shape(half_dims, BF), place, arrived, totals,
        order=(grad_qg, *down_parts),
        near=(1,),
    )
    qg_other, out_other = after((qg_other, out_other), own_half)
    floor_part, fv_mine, fv_other, *parts = kernel_call(
        far_back_kernel,
        (shape((1, COLS), F32), *[shape((8, 64, WIDE), BF)] * 2, *[shape((ROWS, D), BF)] * 4),
        core, pre_fv, cum, floor, near_log, near_key, near_value, entered, own_half, shift(own_half, "c", 1), other_end,
        other_total, grad_qg, w_fv, w_qg, x_all,
        scratch=[pltpu.VMEM((TOKENS, WIDE), BF), pltpu.VMEM((8, 2, 64, WIDE), BF)],
        flops=2 * TOKENS * D * D * 2,
    )
    sent = kernel_call(
        pack_kernel, shape((16, 336, 128), BF), fv_mine, shift(fv_other, "c", 1), floor_part,
        shift(floor_part, "c", 1), qg_mine, shift(qg_other, "c", 1), out_mine, shift(out_other, "c", 1),
    )

    arrived = exchange(sent, ("x", "yl", "yh"))
    parts = scatter_z(after(parts, sent))
    feed_other = shift(after(feed_sum, *parts), "yh", 1)
    grad_tokens = kernel_call(last_kernel, shape((ROWS, D), BF), hidden, grad_middle, *parts, order=(sent,))
    columns, rows = kernel_call(
        sum_kernel, (shape((272, 128), BF), shape((64, 128), BF)), arrived, order=(feed_other, grad_tokens), near=(0,)
    )
    feed_total = kernel_call(
        add_kernel, shape((FEED_ROWS, 2 * PAD), BF), feed_sum, feed_other, order=(columns,)
    )
    feed_totals = gather_z(feed_total)
    last_sums = exchange(
        kernel_call(
            copies_kernel, shape((8, 336, 128), BF), columns, transpose_xz(rows), order=(feed_total,)
        ),
        ("yh", "z"),
    )
    result = kernel_call(
        result_kernel, shape((ROWS, D), BF), middle, *down_parts, order=(columns,)
    )
    mix_grad, gain_grad, out_weight_grad, group_gain_grad, floor_grad = kernel_call(
        mix_grads_kernel,
        (
            shape((64, 4 * D), F32),
            shape((1, 64), F32),
            shape((64, D), F32),
            shape((1, 64), F32),
            shape((1, D), F32),
        ),
        last_sums, mixer_weight, gain_one, output_weight, gain_group,
        order=(result,),
        near=(0,),
    )
    up_grad, feed_gain_grad, down_grad = kernel_call(
        feed_grads_kernel,
        (shape((64, 2 * FF), F32), shape((1, 64), F32), shape((OWNED, D), F32)),
        z_of, *feed_totals, gate_up_weight, gain_two,
        order=(mix_grad,),
    )
    return (
        result,
        grad_tokens,
        mix_grad,
        out_weight_grad,
        up_grad,
        down_grad,
        gain_grad.reshape(64),
        group_gain_grad.reshape(64),
        feed_gain_grad.reshape(64),
        floor_grad.reshape(D),
    )


def solution(mesh):
    cut = Mesh(mesh.devices.reshape(2, 4, 4, 2, 2), AXES)
    seq = ("x", "yl", "c")
    rows, weight, vector = P(AXES, None), P(seq, None), P(seq)
    in_specs = (rows, weight, weight, weight, weight, vector, vector, vector, P(), rows)
    out_specs = (rows, rows, weight, weight, weight, weight, vector, vector, vector, P())
    return jax.shard_map(body, mesh=cut, in_specs=in_specs, out_specs=out_specs, check_vma=False)
```

```python
import functools

import jax
import jax.numpy as jnp
from jax import lax
from jax.experimental import pallas as pl
from jax.experimental.pallas import tpu as pltpu
from jax.sharding import Mesh, PartitionSpec as P

D = 1024
HEADS = 8
HEAD_DIM = 128
FF = 2816
EPS = 1e-06

ROWS = 128
PARTS = 4
COLS = D // PARTS
TOKENS = PARTS * ROWS
WIDE = 2 * COLS
PAD = 768
SLOT, TAKEN, OWNED = 48, 44, 176
SLOTS, UNITS = 8 * SLOT, 8 * OWNED
FEED_ROWS = 96
LOCAL_HEADS = 2
STATES = PARTS * LOCAL_HEADS
HALF = STATES // 2
TAIL = 16
BF = jnp.bfloat16
F32 = jnp.float32
AXES = ("yh", "z", "x", "yl", "c")
VMEM = 40 * 1024 * 1024


def shift(value, axis, by):
    n = lax.axis_size(axis)
    return lax.ppermute(value, axis, [(i, (i + by) % n) for i in range(n)])


def gather_z(own):
    return (own, shift(own, "z", 1), shift(own, "z", -1), shift(own, "z", 2))


def scatter_z(parts):
    return (parts[0], shift(parts[1], "z", -1), shift(parts[2], "z", 1), shift(parts[3], "z", 2))


def transpose_xz(value, flip):
    pairs = [
        ((yh * 4 + z) * 4 + x, ((yh ^ flip) * 4 + x) * 4 + z) for yh in range(2) for z in range(4) for x in range(4)
    ]
    return lax.ppermute(value, ("yh", "z", "x"), pairs)


def quarters(z):
    return [lax.rem(z + by, 4) for by in (0, 3, 1, 2)]


def exchange(value, axes):
    return lax.all_to_all(value, axes, 0, 0)


def after(value, *others):
    return lax.optimization_barrier((value, *others))[0]


def kernel_call(body, out_shape, *args, scratch=(), flops=0, order=(), near=()):
    if order:
        args = after(args, *order)
    args = [
        a if a.dtype == jnp.int32 else pltpu.with_memory_space_constraint(a, pltpu.VMEM if i in near else pltpu.HBM)
        for i, a in enumerate(args)
    ]
    in_specs = [
        pl.BlockSpec(memory_space=pltpu.SMEM) if a.dtype == jnp.int32 else pl.BlockSpec(memory_space=pltpu.VMEM)
        for a in args
    ]
    out_specs = jax.tree.map(lambda _: pl.BlockSpec(memory_space=pltpu.VMEM), out_shape)
    return pl.pallas_call(
        body,
        out_shape=out_shape,
        in_specs=in_specs,
        out_specs=out_specs,
        scratch_shapes=list(scratch),
        compiler_params=pltpu.CompilerParams(vmem_limit_bytes=VMEM),
        cost_estimate=pl.CostEstimate(flops=1, bytes_accessed=1, transcendentals=0),
    )(*args)


def shape(dims, dtype):
    return pltpu.HBM(dims, dtype)


def near_shape(dims, dtype):
    return pltpu.VMEM(dims, dtype)


def dot(a, b):
    return jnp.dot(a, b, preferred_element_type=F32)


def dot_t(a, b):
    return lax.dot_general(a, b, (((1,), (1,)), ((), ())), preferred_element_type=F32)


def t_dot(a, b):
    return lax.dot_general(a, b, (((0,), (0,)), ((), ())), preferred_element_type=F32)


def exact_dot(a, b):
    return jnp.dot(a, b, precision=lax.Precision.HIGHEST, preferred_element_type=F32)


def mean_scale(value):
    return lax.rsqrt(jnp.mean(value * value, axis=-1, keepdims=True) + EPS)


def triangle(strict, upper):
    row = lax.broadcasted_iota(jnp.int32, (ROWS, ROWS), 0)
    col = lax.broadcasted_iota(jnp.int32, (ROWS, ROWS), 1)
    if upper:
        row, col = col, row
    return row > col if strict else row >= col


def swish_slope(value, sigma):
    return sigma * (1.0 + value * (1.0 - sigma))


def column(ref):
    return jnp.transpose(ref[...].astype(F32))


def row_sums(value):
    return jnp.sum(jnp.transpose(value), axis=0, keepdims=True)


def lane_blocks(value):
    total = value[:, :128]
    for j in range(128, value.shape[1], 128):
        total = total + value[:, j : j + 128]
    return total


def prepare_kernel(z_ref, w_ref, gain_ref, out_w_ref, out_gain_ref, sent_ref, out_ref):
    start = z_ref[0] * COLS
    gain = column(gain_ref)
    for to, j in enumerate((1, 2, 0, 3)):
        cols = pl.ds(pl.multiple_of(j * D + start, 128), COLS)
        block = (w_ref[:, cols].astype(F32) * gain).astype(BF)
        for i in range(8):
            sent_ref[i, :, to * COLS : (to + 1) * COLS] = block
    out_ref[...] = (out_w_ref[...].astype(F32) * column(out_gain_ref)).astype(BF)


def selection(z, slots, units, slots_first):
    shape_ = (slots, units) if slots_first else (units, slots)
    line = (slots, 1) if slots_first else (1, slots)
    slot = lax.broadcasted_iota(jnp.int32, line, 0 if slots_first else 1)
    owner = jnp.zeros(line, jnp.int32)
    for i in range(1, slots // SLOT):
        owner = owner + (slot >= i * SLOT).astype(jnp.int32)
    place = slot - owner * SLOT
    unit = jnp.where(place < TAKEN, owner * OWNED + z * TAKEN + place, -1)
    return jnp.where(lax.broadcasted_iota(jnp.int32, shape_, 1 if slots_first else 0) == unit, 1.0, 0.0).astype(BF)


def prepare_feed_kernel(z_ref, up_ref, gain_ref, down_ref, out_ref):
    gain = column(gain_ref)
    chosen = selection(z_ref[0], SLOTS, UNITS, False)
    for i in range(4):
        picked = dot(up_ref[:, i * UNITS : (i + 1) * UNITS], chosen)
        out_ref[:64, i * SLOTS : (i + 1) * SLOTS] = (picked * gain).astype(BF)
    rows = dot(selection(z_ref[0], SLOT, OWNED, True), down_ref[...]).astype(BF)
    out_ref[64:, :D] = rows[:32]
    out_ref[64:80, D:] = rows[32:, :512]
    out_ref[80:, D:] = rows[32:, 512:]


def gated(pre, floor):
    sigma = lax.logistic(pre)
    return sigma, floor + (1.0 - floor) * sigma


def swish(value):
    return value * lax.logistic(value)


def head_cols(h):
    return slice(h * HEAD_DIM, (h + 1) * HEAD_DIM)


def part_rows(b):
    return slice(b * ROWS, (b + 1) * ROWS)


def first_kernel(core_ref, x0, x1, x2, x3, mine_ref, other_ref, floor_ref,
                 x_ref, w_ref, w_qg_ref, pre_ref, cum_ref, state_ref, total_ref):
    core = core_ref[0]
    for ref, lanes in ((w_ref, slice(0, WIDE)), (w_qg_ref, slice(WIDE, D))):
        ref[:, pl.ds(core, 1)] = mine_ref[:, :, lanes].reshape(8, 1, 64, WIDE)
        ref[:, pl.ds(1 - core, 1)] = other_ref[:, :, lanes].reshape(8, 1, 64, WIDE)
    for b, part in enumerate((x0, x1, x2, x3)):
        value = part[...].astype(F32)
        x_ref[part_rows(b), :] = (value * mean_scale(value)).astype(BF)
    pre_ref[...] = dot(x_ref[...], w_ref[...].reshape(D, WIDE))
    ones = triangle(False, False).astype(F32)
    floor = floor_ref[...]
    for b in range(PARTS):
        rows = part_rows(b)
        _, decay = gated(pre_ref[rows, :COLS], floor)
        cum_all = exact_dot(ones, jnp.log(decay))
        cum_ref[rows, :] = cum_all
        total_all = cum_all[ROWS - 1 :, :]
        k_out = ((1.0 - decay).astype(BF).astype(F32) * jnp.exp(total_all - cum_all)).astype(BF)
        for h in range(LOCAL_HEADS):
            value = pre_ref[rows, COLS + h * HEAD_DIM : COLS + (h + 1) * HEAD_DIM].astype(BF)
            s = h * PARTS + b
            state_ref[s] = t_dot(k_out[:, head_cols(h)], value).astype(BF)
            total_ref[s : s + 1, :] = total_all[:, head_cols(h)]


def second_kernel(x_ref, w_ref, fv_ref, cum_ref, floor_ref, pre_ref, q_ref, local_ref):
    pre_ref[...] = dot(x_ref[...], w_ref[...].reshape(D, WIDE))
    causal = triangle(False, False)
    floor = floor_ref[...]
    for b in range(PARTS):
        rows = part_rows(b)
        _, decay = gated(fv_ref[rows, :COLS], floor)
        cum = cum_ref[rows, :]
        k_in = ((1.0 - decay).astype(BF).astype(F32) * jnp.exp(-cum)).astype(BF)
        q_in = (swish(pre_ref[rows, :COLS]).astype(BF).astype(F32) * jnp.exp(cum)).astype(BF)
        q_ref[rows, :] = q_in
        value = fv_ref[rows, COLS:].astype(BF)
        for h in range(LOCAL_HEADS):
            cols = head_cols(h)
            scores = jnp.where(causal, dot_t(q_in[:, cols], k_in[:, cols]), 0.0).astype(BF)
            local_ref[rows, cols] = dot(scores, value[:, cols])


def split3(value):
    first = value.astype(BF).astype(F32)
    second = (value - first).astype(BF).astype(F32)
    return first, second, value - first - second


def chip_kernel(core_ref, mine_ref, other_ref, my_total_ref, other_total_ref, out_ref, *, backward):
    core = core_ref[0]
    second = core == (0 if backward else 1)
    base = core * HALF
    my_total = my_total_ref[pl.ds(base, HALF), :]
    other_total = other_total_ref[pl.ds(base, HALF), :]
    last_decay = jnp.exp(jnp.where(second, my_total, other_total))
    for i in range(HALF):
        mine = mine_ref[base + i].astype(F32)
        other = other_ref[base + i].astype(F32)
        last = jnp.where(second, mine, other)
        first = jnp.where(second, other, mine)
        state = (jnp.transpose(last_decay[i : i + 1, :]) * first + last).astype(BF)
        for d in range(8):
            out_ref[d, i * HEAD_DIM : (i + 1) * HEAD_DIM, :] = state
    if not backward:
        pieces = split3(my_total + other_total)
        tail = jnp.concatenate([*pieces, jnp.zeros((HALF, HEAD_DIM), F32)], axis=0).astype(BF)
        for d in range(8):
            out_ref[d, HALF * HEAD_DIM :, :] = tail


def carry_kernel(place_ref, all_ref, *refs, backward):
    place = place_ref[0]
    if backward:
        totals_ref, out_ref = refs
    else:
        out_ref, totals_ref = refs
        for j in range(8):
            tail = all_ref[j, HALF * HEAD_DIM :, :].astype(F32)
            totals_ref[j] = (tail[:HALF] + tail[HALF : 2 * HALF]) + tail[2 * HALF : 3 * HALF]
    for i in range(HALF):
        carried = jnp.zeros((HEAD_DIM, HEAD_DIM), F32)
        decays = jnp.transpose(jnp.exp(jnp.concatenate([totals_ref[j, i : i + 1, :] for j in range(8)], axis=0)))
        for step in range(7):
            j = 7 - step if backward else step
            reached = j > place if backward else j < place
            block = all_ref[j, i * HEAD_DIM : (i + 1) * HEAD_DIM, :].astype(F32)
            carried = jnp.where(reached, decays[:, j : j + 1] * carried + block, carried)
        out_ref[i] = carried.astype(BF)


def enter_state(core, own_half, other_half, other_end, other_total, s, backward):
    h, b = divmod(s, PARTS)
    chip = jnp.where(core == h, own_half[b], other_half[b]).astype(F32)
    later = core == (0 if backward else 1)
    passed = jnp.transpose(jnp.exp(other_total[s : s + 1, :])) * chip + other_end[s].astype(F32)
    return jnp.where(later, passed, chip)


def mix_kernel(core_ref, pre_ref, q_ref, local_ref, own_half, other_half, other_end, other_total, w_ref,
               out_ref, normed_ref, entered_ref, p0, p1, p2, p3):
    core = core_ref[0]
    for b in range(PARTS):
        rows = part_rows(b)
        for h in range(LOCAL_HEADS):
            cols = head_cols(h)
            s = h * PARTS + b
            state = enter_state(core, own_half, other_half, other_end, other_total, s, False).astype(BF)
            entered_ref[s] = state
            mixed = local_ref[rows, cols] + dot(q_ref[rows, cols], state)
            out_ref[rows, cols] = mixed
            gate = pre_ref[rows, COLS + h * HEAD_DIM : COLS + (h + 1) * HEAD_DIM]
            normed_ref[rows, cols] = (mixed * mean_scale(mixed) * swish(gate)).astype(BF)
    product = dot(normed_ref[...], w_ref[...]).astype(BF)
    for b, part in enumerate((p0, p1, p2, p3)):
        part[...] = product[part_rows(b), :]


def sum_parts(p0, p1, p2, p3):
    return (p0[...].astype(F32) + p1[...].astype(F32)) + (p2[...].astype(F32) + p3[...].astype(F32))


def middle_kernel(hidden_ref, p0, p1, p2, p3, middle_ref, normed_ref):
    middle = hidden_ref[...].astype(F32) + sum_parts(p0, p1, p2, p3)
    middle_ref[...] = middle
    normed_ref[...] = (middle * mean_scale(middle)).astype(BF)


def feed_inputs(parts, grads, w_ref, x_ref, g_ref, down_ref):
    for s in range(16):
        at = s * SLOT
        rows = w_ref[s, w_ref.shape[1] - 32 :, :]
        down_ref[at : at + 32, :] = rows[:, :D]
        down_ref[at + 32 : at + 48, :512] = rows[:16, D:]
        down_ref[at + 32 : at + 48, 512:] = rows[16:, D:]
    for b in range(PARTS):
        x_ref[part_rows(b), :] = parts[b][...]
        g_ref[part_rows(b), :] = grads[b][...]


def feed_kernel(x0, x1, x2, x3, g0, g1, g2, g3, w_ref, act_ref, grad_ref, p0, p1, p2, p3, x_ref, g_ref, down_ref):
    feed_inputs((x0, x1, x2, x3), (g0, g1, g2, g3), w_ref, x_ref, g_ref, down_ref)
    for j in range(3):
        lanes = slice(j * COLS, (j + 1) * COLS)
        ups = slice(PAD + j * COLS, PAD + (j + 1) * COLS)
        gate = dot(x_ref[...], w_ref[:, :64, lanes].reshape(D, COLS))
        up = dot(x_ref[...], w_ref[:, :64, ups].reshape(D, COLS))
        grad = dot_t(g_ref[...], down_ref[lanes, :])
        sigma = lax.logistic(gate)
        active = gate * sigma
        act_ref[:, lanes] = (active * up).astype(BF)
        grad_ref[:, lanes] = (grad * up * swish_slope(gate, sigma)).astype(BF)
        grad_ref[:, ups] = (grad * active).astype(BF)
    product = dot_t(grad_ref[...], w_ref[:, :64, :].reshape(D, 2 * PAD)).astype(BF)
    for b, part in enumerate((p0, p1, p2, p3)):
        part[...] = product[part_rows(b), :]


def feed_grad_kernel(x0, x1, x2, x3, g0, g1, g2, g3, w_ref, grad_ref, act_ref, out_ref, p0, p1, p2, p3,
                     x_ref, g_ref, down_ref):
    feed_inputs((x0, x1, x2, x3), (g0, g1, g2, g3), w_ref, x_ref, g_ref, down_ref)
    product = dot(act_ref[...], down_ref[...]).astype(BF)
    for b, part in enumerate((p0, p1, p2, p3)):
        part[...] = product[part_rows(b), :]
    for j in range(0, 2 * PAD, 512):
        out_ref[:, :64, j : j + 512] = t_dot(x_ref[...], grad_ref[:, j : j + 512]).astype(BF).reshape(16, 64, 512)
    rows = t_dot(act_ref[...], g_ref[...]).astype(BF)
    for s in range(16):
        at = s * SLOT
        out_ref[s, 64:, :D] = rows[at : at + 32]
        out_ref[s, 64:80, D:] = rows[at + 32 : at + 48, :512]
        out_ref[s, 80:, D:] = rows[at + 32 : at + 48, 512:]


def add_kernel(a_ref, b_ref, out_ref):
    out_ref[...] = (a_ref[...].astype(F32) + b_ref[...].astype(F32)).astype(BF)


def result_kernel(middle_ref, p0, p1, p2, p3, out_ref):
    out_ref[...] = (middle_ref[...] + sum_parts(p0, p1, p2, p3)).astype(BF)


def norm_back(value_ref, base_ref, u):
    value = value_ref[...].astype(F32)
    scale = mean_scale(value)
    centered = value * scale
    back = scale * (u - centered * jnp.mean(u * centered, axis=-1, keepdims=True))
    return base_ref[...].astype(F32) + back


def branch_kernel(value_ref, base_ref, p0, p1, p2, p3, out_ref, low_ref):
    total = norm_back(value_ref, base_ref, sum_parts(p0, p1, p2, p3))
    out_ref[...] = total
    low_ref[...] = total.astype(BF)


def last_kernel(value_ref, base_ref, p0, p1, p2, p3, low_ref):
    low_ref[...] = norm_back(value_ref, base_ref, sum_parts(p0, p1, p2, p3)).astype(BF)


def head_back_kernel(b0, b1, b2, b3, w_ref, pre_ref, q_ref, mixed_ref, branch_ref, gate_ref, out_grad_ref, state_ref):
    for b, part in enumerate((b0, b1, b2, b3)):
        branch_ref[part_rows(b), :] = part[...]
    grads = dot_t(branch_ref[...], w_ref[...])
    for b in range(PARTS):
        rows = part_rows(b)
        for h in range(LOCAL_HEADS):
            cols = head_cols(h)
            grad = grads[rows, cols]
            mixed = mixed_ref[rows, cols]
            scale = mean_scale(mixed)
            normed = mixed * scale
            gate = pre_ref[rows, COLS + h * HEAD_DIM : COLS + (h + 1) * HEAD_DIM]
            sigma = lax.logistic(gate)
            gate_ref[rows, cols] = (grad * normed * swish_slope(gate, sigma)).astype(BF)
            c = grad * (gate * sigma)
            mixer = (scale * (c - normed * jnp.mean(c * normed, axis=-1, keepdims=True))).astype(BF)
            out_grad_ref[rows, cols] = mixer
            state_ref[h * PARTS + b] = t_dot(q_ref[rows, cols], mixer).astype(BF)


def near_back_kernel(core_ref, x_ref, normed_ref, branch_ref, qg_ref, fv_ref, cum_ref, floor_ref, q_ref, gate_ref,
                     out_grad_ref, entered_ref, grad_ref, log_ref, key_ref, value_ref,
                     mine_ref, other_ref, my_rows_ref, other_rows_ref, all_ref, rows_ref):
    causal = triangle(False, False)
    suffix = triangle(False, True).astype(F32)
    floor = floor_ref[...]
    for b in range(PARTS):
        rows = part_rows(b)
        _, decay = gated(fv_ref[rows, :COLS], floor)
        cum = cum_ref[rows, :]
        grow_all = jnp.exp(cum)
        shrink_all = jnp.exp(-cum)
        k_all = ((1.0 - decay).astype(BF).astype(F32) * shrink_all).astype(BF)
        q_pre = qg_ref[rows, :COLS]
        slope_all = swish_slope(q_pre, lax.logistic(q_pre))
        for h in range(LOCAL_HEADS):
            cols = head_cols(h)
            value = fv_ref[rows, COLS + h * HEAD_DIM : COLS + (h + 1) * HEAD_DIM].astype(BF)
            q_in, k_in = q_ref[rows, cols], k_all[:, cols]
            out_grad = out_grad_ref[rows, cols]
            scores = jnp.where(causal, dot_t(q_in, k_in), 0.0).astype(BF)
            grad_scores = jnp.where(causal, dot_t(out_grad, value), 0.0).astype(BF)
            inner = dot(grad_scores, k_in) + dot_t(out_grad, entered_ref[h * PARTS + b])
            back = t_dot(grad_scores, q_in)
            near = q_in.astype(F32) * inner - k_in.astype(F32) * back
            log_ref[rows, cols] = exact_dot(suffix, near)
            key_ref[rows, cols] = back * shrink_all[:, cols]
            value_ref[rows, cols] = t_dot(scores, out_grad)
            grad_ref[rows, cols] = (inner * grow_all[:, cols] * slope_all[:, cols]).astype(BF)
    grad_ref[:, COLS:] = gate_ref[...]
    column_grad(core_ref[0], x_ref, grad_ref, mine_ref, other_ref, all_ref)
    row_grad(core_ref[0], normed_ref, branch_ref, my_rows_ref, other_rows_ref, rows_ref)


def far_back_kernel(core_ref, fv_ref, cum_ref, floor_ref, log_ref, key_ref, value_ref, entered_ref, own_half, other_half,
                    other_end, other_total, qg_ref, w_fv_ref, w_qg_ref, x_ref,
                    floor_grad_ref, mine_ref, other_ref, p0, p1, p2, p3, grad_ref, all_ref):
    core = core_ref[0]
    before = triangle(True, False).astype(F32)
    floor = floor_ref[...]
    floor_sum = jnp.zeros((1, COLS), F32)
    for b in range(PARTS):
        rows = part_rows(b)
        sigma, decay = gated(fv_ref[rows, :COLS], floor)
        cum = cum_ref[rows, :]
        total = cum[ROWS - 1 :, :]
        to_end = jnp.exp(total - cum)
        k_all = ((1.0 - decay).astype(BF).astype(F32) * to_end).astype(BF)
        aheads, edges = [], []
        for h in range(LOCAL_HEADS):
            cols = head_cols(h)
            s = h * PARTS + b
            following = enter_state(core, own_half, other_half, other_end, other_total, s, True)
            low = following.astype(BF)
            value = fv_ref[rows, COLS + h * HEAD_DIM : COLS + (h + 1) * HEAD_DIM].astype(BF)
            aheads.append(dot_t(value, low))
            edges.append(jnp.transpose(jnp.sum(following * entered_ref[s].astype(F32), axis=1, keepdims=True)))
            grad_value = value_ref[rows, cols] + dot(k_all[:, cols], low)
            grad_ref[rows, COLS + h * HEAD_DIM : COLS + (h + 1) * HEAD_DIM] = grad_value.astype(BF)
        ahead = jnp.concatenate(aheads, axis=1)
        edge = jnp.concatenate(edges, axis=1)
        far = exact_dot(before, k_all.astype(F32) * ahead)
        grad_log = log_ref[rows, :] + far + jnp.exp(total) * edge
        grad_decay = grad_log / decay - (key_ref[rows, :] + ahead * to_end)
        floor_sum = floor_sum + jnp.sum(grad_decay * (1.0 - sigma), axis=0, keepdims=True)
        grad_ref[rows, :COLS] = (grad_decay * (1.0 - floor) * sigma * (1.0 - sigma)).astype(BF)
    floor_grad_ref[...] = floor_sum
    column_grad(core, x_ref, grad_ref, mine_ref, other_ref, all_ref)
    product = dot_t(grad_ref[...], w_fv_ref[...].reshape(D, WIDE)) + dot_t(qg_ref[...], w_qg_ref[...].reshape(D, WIDE))
    product = product.astype(BF)
    for b, part in enumerate((p0, p1, p2, p3)):
        part[...] = product[part_rows(b), :]


def column_grad(core, a_ref, g_ref, mine_ref, other_ref, all_ref):
    n = g_ref.shape[1]
    all_ref[...] = t_dot(a_ref[...], g_ref[...]).astype(BF).reshape(8, 2, 64, n)
    mine_ref[...] = all_ref[:, pl.ds(core, 1)].reshape(8, 64, n)
    other_ref[...] = all_ref[:, pl.ds(1 - core, 1)].reshape(8, 64, n)


def row_grad(core, a_ref, g_ref, mine_ref, other_ref, all_ref):
    rows = mine_ref.shape[1]
    all_ref[...] = t_dot(a_ref[...], g_ref[...]).astype(BF).reshape(2, 2, rows, D)
    mine_ref[...] = all_ref[:, pl.ds(core, 1)].reshape(2, rows, D)
    other_ref[...] = all_ref[:, pl.ds(1 - core, 1)].reshape(2, rows, D)


def pack_columns(mine_ref, other_ref, out_ref, start):
    lanes = mine_ref.shape[2] // 2
    for i in range(8):
        value = (mine_ref[i].astype(F32) + other_ref[i].astype(F32)).astype(BF)
        for half in range(2):
            for j in range(lanes // 128):
                at = half * lanes + j * 128
                out_ref[i * 2 + half, start + j * 64 : start + (j + 1) * 64, :] = value[:, at : at + 128]


def pack_rows(mine_ref, other_ref, out_ref, start):
    rows = mine_ref.shape[1]
    for yl in range(2):
        value = (mine_ref[yl].astype(F32) + other_ref[yl].astype(F32)).astype(BF)
        for p in range(8):
            to = (p // 2) * 4 + yl * 2 + p % 2
            out_ref[to, start : start + rows, :] = value[:, p * 128 : (p + 1) * 128]


def rider_rows(value):
    rows = [piece[:, cols] for piece in split3(value) for cols in (slice(0, 128), slice(128, 256))]
    return jnp.concatenate([*rows, jnp.zeros((10, 128), F32)], axis=0).astype(BF)


def rider_value(rows):
    rows = rows.astype(F32)
    halves = [(rows[i : i + 1] + rows[i + 2 : i + 3]) + rows[i + 4 : i + 5] for i in range(2)]
    return jnp.concatenate(halves, axis=1)


def pack_kernel(mine_ref, other_ref, floor_ref, other_floor_ref, my_qg_ref, other_qg_ref, my_rows_ref, other_rows_ref, out_ref):
    pack_columns(mine_ref, other_ref, out_ref, 0)
    rider = rider_rows(floor_ref[...] + other_floor_ref[...])
    for i in range(16):
        out_ref[i, 128:144, :] = rider
    pack_columns(my_qg_ref, other_qg_ref, out_ref, 144)
    pack_rows(my_rows_ref, other_rows_ref, out_ref, 272)


def total_of(all_ref, rows):
    total = all_ref[0, rows, :].astype(F32)
    for i in range(1, 16):
        total = total + all_ref[i, rows, :].astype(F32)
    return total


def sum_kernel(all_ref, out_ref, rows_ref):
    first = total_of(all_ref, slice(0, 128)).astype(BF)
    floor = rider_value(all_ref[0, 128:144, :])
    for i in range(1, 16):
        floor = floor + rider_value(all_ref[i, 128:144, :])
    rider = rider_rows(floor)
    second = total_of(all_ref, slice(144, 272)).astype(BF)
    for i in range(8):
        out_ref[i, :128, :] = first
        out_ref[i, 128:144, :] = rider
        out_ref[i, 144:, :] = second
    rows_ref[...] = total_of(all_ref, slice(272, 336)).astype(BF)


def feed_grads_kernel(z_ref, s0, s1, s2, s3, w_ref, gain_ref, up_ref, gain_grad_ref, down_ref):
    chosen = jnp.concatenate([selection(z, SLOTS, UNITS, True) for z in quarters(z_ref[0])], axis=0)
    gain = column(gain_ref)
    gain_grad = jnp.zeros((64, 128), F32)
    taken = jnp.concatenate(
        [
            jnp.concatenate([ref[:64, i * SLOTS : (i + 1) * SLOTS] for ref in (s0, s1, s2, s3)], axis=1)
            for i in range(4)
        ],
        axis=0,
    )
    values = dot(taken, chosen)
    for i in range(4):
        value = values[i * 64 : (i + 1) * 64]
        cols = slice(i * UNITS, (i + 1) * UNITS)
        up_ref[:, cols] = value * gain
        gain_grad = gain_grad + lane_blocks(value * w_ref[:, cols].astype(F32))
    gain_grad_ref[...] = row_sums(gain_grad)
    down = jnp.zeros((OWNED, D), F32)
    for z, ref in zip(quarters(z_ref[0]), (s0, s1, s2, s3)):
        last = jnp.concatenate([ref[64:80, D:], ref[80:, D:]], axis=1)
        rows = jnp.concatenate([ref[64:, :D], last], axis=0)
        down = down + dot(selection(z, SLOT, OWNED, False), rows)
    down_ref[...] = down


def mix_grads_kernel(z_ref, yh_ref, all_ref, o0, o1, o2, o3, w_ref, gain_ref, out_w_ref, out_gain_ref,
                     mix_ref, gain_grad_ref, out_ref, out_gain_grad_ref, floor_ref):
    gain, out_gain = column(gain_ref), column(out_gain_ref)
    gain_grad = jnp.zeros((64, 128), F32)
    out_gain_grad = jnp.zeros((64, 128), F32)
    for yh in range(2):
        for z in range(4):
            i = yh * 4 + z
            for start, block in ((0, 2 if yh else 1), (144, 3 if yh else 0)):
                for j in range(2):
                    value = all_ref[i, start + j * 64 : start + (j + 1) * 64, :].astype(F32)
                    at = block * D + z * COLS + j * 128
                    mix_ref[:, at : at + 128] = value * gain
                    gain_grad = gain_grad + value * w_ref[:, at : at + 128].astype(F32)
            if yh == 0:
                floor_ref[:, z * COLS : (z + 1) * COLS] = rider_value(all_ref[i, 128:144, :])
    for z, ref in zip(quarters(z_ref[0]), (o0, o1, o2, o3)):
        for k in range(2):
            yh = yh_ref[0] if k == 0 else 1 - yh_ref[0]
            cols = pl.ds(pl.multiple_of((z * 2 + yh) * 128, 128), 128)
            value = ref[k * 64 : (k + 1) * 64, :].astype(F32)
            out_ref[:, cols] = value * out_gain
            out_gain_grad = out_gain_grad + value * out_w_ref[:, cols].astype(F32)
    gain_grad_ref[...] = row_sums(gain_grad)
    out_gain_grad_ref[...] = row_sums(out_gain_grad)


def scalar(value):
    return value.reshape(1).astype(jnp.int32)


def body(hidden, mixer_weight, output_weight, gate_up_weight, down_weight, mixer_gain, group_gain, feed_gain,
         forget_floor, out_grad):
    z = lax.axis_index("z")
    z_of, yh_of = scalar(z), scalar(lax.axis_index("yh"))
    core = scalar(lax.axis_index("c"))
    place = scalar(lax.axis_index("x") * 2 + lax.axis_index("yl"))
    gain_one, gain_group, gain_two = (g.reshape(1, 64) for g in (mixer_gain, group_gain, feed_gain))
    floor = lax.dynamic_index_in_dim(forget_floor.reshape(PARTS, COLS), z, 0)
    own = [near_shape((ROWS, D), BF)] * 4
    state_dims = (STATES, HEAD_DIM, HEAD_DIM)
    half_dims = (HALF, HEAD_DIM, HEAD_DIM)

    w_sent, out_own = kernel_call(
        prepare_kernel, (shape((8, 64, D), BF), shape((64, D), BF)),
        z_of, mixer_weight, gain_one, output_weight, gain_group,
    )
    tokens = gather_z(hidden)
    w_mine = exchange(w_sent, ("x", "yl"))
    w_out = lax.all_gather(out_own, ("x", "yl", "c"))
    w_other = shift(after(w_mine, *tokens), "c", 1)
    x_all, w_fv, w_qg, pre_fv, cum, end, total = kernel_call(
        first_kernel,
        (
            shape((TOKENS, D), BF),
            shape((8, 2, 64, WIDE), BF),
            shape((8, 2, 64, WIDE), BF),
            shape((TOKENS, WIDE), F32),
            shape((TOKENS, COLS), F32),
            near_shape(state_dims, BF),
            shape((STATES, HEAD_DIM), F32),
        ),
        core, *tokens, w_mine, w_other, floor,
        flops=2 * TOKENS * D * WIDE,
        near=(5, 6),
    )

    def chip_state(end_state, other_total, backward, order=()):
        other_end = shift(end_state, "c", 1)
        sent = kernel_call(
            functools.partial(chip_kernel, backward=backward),
            shape((8, HALF * HEAD_DIM + (0 if backward else TAIL), HEAD_DIM), BF),
            core, end_state, other_end, total, other_total,
            order=order,
            near=(1, 2),
        )
        return sent, other_end

    other_total = shift(total, "c", 1)
    sent, other_end = chip_state(end, other_total, False)
    arrived = exchange(sent, ("x", "yl"))
    grads_out = gather_z(after(out_grad, sent))
    pre_qg, q_in, local_out = kernel_call(
        second_kernel,
        (shape((TOKENS, WIDE), F32), shape((TOKENS, COLS), BF), shape((TOKENS, COLS), F32)),
        x_all, w_qg, pre_fv, cum, floor,
        flops=2 * TOKENS * D * WIDE,
        order=(sent,),
    )
    w_out = lax.dynamic_index_in_dim(w_out.reshape(PARTS, COLS, D), z, 0, keepdims=False)
    feed_own_weights = kernel_call(
        prepare_feed_kernel, shape((FEED_ROWS, 2 * PAD), BF), z_of, gate_up_weight, gain_two, down_weight,
        order=(q_in, w_out),
    )
    w_feed = lax.all_gather(after(feed_own_weights, arrived, *grads_out), ("x", "yl", "c"))
    own_half, totals = kernel_call(
        functools.partial(carry_kernel, backward=False),
        (near_shape(half_dims, BF), shape((8, HALF, HEAD_DIM), F32)),
        place, arrived,
        order=(feed_own_weights, w_out, *grads_out),
        near=(1,),
    )
    mixed, normed_out, entered, *parts = kernel_call(
        mix_kernel,
        (shape((TOKENS, COLS), F32), shape((TOKENS, COLS), BF), shape(state_dims, BF), *own),
        core, pre_qg, q_in, local_out, own_half, shift(own_half, "c", 1), other_end, other_total, w_out,
        flops=2 * TOKENS * COLS * D,
        near=(4, 5),
    )
    middle, feed_own = kernel_call(
        middle_kernel, (shape((ROWS, D), F32), near_shape((ROWS, D), BF)), hidden, *scatter_z(parts),
        near=(1, 2, 3, 4),
    )
    feed_in = (*gather_z(feed_own), *grads_out, w_feed)
    feed_scratch = [pltpu.VMEM((TOKENS, D), BF), pltpu.VMEM((TOKENS, D), BF), pltpu.VMEM((PAD, D), BF)]
    act, grad_up, *parts = kernel_call(
        feed_kernel,
        (shape((TOKENS, PAD), BF), shape((TOKENS, 2 * PAD), BF), *own),
        *feed_in,
        scratch=feed_scratch,
        flops=2 * TOKENS * D * PAD * 5,
    )
    feed_back = scatter_z(parts)
    feed_grad, *down_parts = kernel_call(
        feed_grad_kernel,
        (shape((16, FEED_ROWS, 2 * PAD), BF), *[shape((ROWS, D), BF)] * 4),
        *feed_in, grad_up, act,
        scratch=feed_scratch,
        flops=2 * TOKENS * D * PAD * 3,
        order=(parts[3],),
    )
    grad_middle, branch_own = kernel_call(
        branch_kernel, (shape((ROWS, D), F32), near_shape((ROWS, D), BF)), middle, out_grad, *feed_back,
        order=(feed_grad,),
        near=(2, 3, 4, 5),
    )
    feed_sum = lax.psum_scatter(after(feed_grad, *feed_back), ("x", "yl", "c"), scatter_dimension=0)
    branch = gather_z(branch_own)
    branch_all, grad_gate, grad_mixed, end_grad = kernel_call(
        head_back_kernel,
        (
            shape((TOKENS, D), BF),
            shape((TOKENS, COLS), BF),
            shape((TOKENS, COLS), BF),
            near_shape(state_dims, BF),
        ),
        *branch, w_out, pre_qg, q_in, mixed,
        flops=2 * TOKENS * COLS * D,
        near=(0, 1, 2, 3),
    )

    sent, other_end = chip_state(end_grad, other_total, True)
    down_parts = scatter_z(after(down_parts, sent))
    arrived = exchange(sent, ("x", "yl"))
    grad_qg, near_log, near_key, near_value, qg_mine, qg_other, out_mine, out_other = kernel_call(
        near_back_kernel,
        (
            shape((TOKENS, WIDE), BF),
            *[shape((TOKENS, COLS), F32)] * 3,
            *[shape((8, 64, WIDE), BF)] * 2,
            *[shape((2, 64, D), BF)] * 2,
        ),
        core, x_all, normed_out, branch_all, pre_qg, pre_fv, cum, floor, q_in, grad_gate, grad_mixed, entered,
        scratch=[pltpu.VMEM((8, 2, 64, WIDE), BF), pltpu.VMEM((2, 2, 64, D), BF)],
        flops=2 * TOKENS * (HEAD_DIM * HEAD_DIM * 12 + D * WIDE),
        order=(sent,),
    )
    own_half = kernel_call(
        functools.partial(carry_kernel, backward=True), near_shape(half_dims, BF), place, arrived, totals,
        order=(grad_qg, *down_parts),
        near=(1,),
    )
    qg_other, out_other = after((qg_other, out_other), own_half)
    floor_part, fv_mine, fv_other, *parts = kernel_call(
        far_back_kernel,
        (shape((1, COLS), F32), *[shape((8, 64, WIDE), BF)] * 2, *[shape((ROWS, D), BF)] * 4),
        core, pre_fv, cum, floor, near_log, near_key, near_value, entered, own_half, shift(own_half, "c", 1), other_end,
        other_total, grad_qg, w_fv, w_qg, x_all,
        scratch=[pltpu.VMEM((TOKENS, WIDE), BF), pltpu.VMEM((8, 2, 64, WIDE), BF)],
        flops=2 * TOKENS * D * D * 2,
    )
    sent = kernel_call(
        pack_kernel, shape((16, 336, 128), BF), fv_mine, shift(fv_other, "c", 1), floor_part,
        shift(floor_part, "c", 1), qg_mine, shift(qg_other, "c", 1), out_mine, shift(out_other, "c", 1),
    )

    arrived = exchange(sent, ("x", "yl", "yh"))
    parts = scatter_z(after(parts, sent))
    feed_other = shift(after(feed_sum, *parts), "yh", 1)
    grad_tokens = kernel_call(last_kernel, shape((ROWS, D), BF), hidden, grad_middle, *parts, order=(sent,))
    copies, rows = kernel_call(
        sum_kernel, (shape((8, 272, 128), BF), shape((64, 128), BF)), arrived, order=(feed_other, grad_tokens), near=(0,)
    )
    last_sums = exchange(copies, ("yh", "z"))
    out_sums = gather_z(jnp.concatenate([transpose_xz(rows, 0), transpose_xz(rows, 1)], axis=0))
    feed_total = kernel_call(
        add_kernel, shape((FEED_ROWS, 2 * PAD), BF), feed_sum, feed_other, order=(copies,)
    )
    feed_totals = gather_z(feed_total)
    result = kernel_call(
        result_kernel, shape((ROWS, D), BF), middle, *down_parts, order=(copies,)
    )
    up_grad, feed_gain_grad, down_grad = kernel_call(
        feed_grads_kernel,
        (shape((64, 2 * FF), F32), shape((1, 64), F32), shape((OWNED, D), F32)),
        z_of, *feed_totals, gate_up_weight, gain_two,
        order=(result,),
    )
    mix_grad, gain_grad, out_weight_grad, group_gain_grad, floor_grad = kernel_call(
        mix_grads_kernel,
        (
            shape((64, 4 * D), F32),
            shape((1, 64), F32),
            shape((64, D), F32),
            shape((1, 64), F32),
            shape((1, D), F32),
        ),
        z_of, yh_of, last_sums, *out_sums, mixer_weight, gain_one, output_weight, gain_group,
        order=(up_grad,),
        near=(2,),
    )
    return (
        result,
        grad_tokens,
        mix_grad,
        out_weight_grad,
        up_grad,
        down_grad,
        gain_grad.reshape(64),
        group_gain_grad.reshape(64),
        feed_gain_grad.reshape(64),
        floor_grad.reshape(D),
    )


def solution(mesh):
    cut = Mesh(mesh.devices.reshape(2, 4, 4, 2, 2), AXES)
    seq = ("x", "yl", "c")
    rows, weight, vector = P(AXES, None), P(seq, None), P(seq)
    in_specs = (rows, weight, weight, weight, weight, vector, vector, vector, P(), rows)
    out_specs = (rows, rows, weight, weight, weight, weight, vector, vector, vector, P())
    return jax.shard_map(body, mesh=cut, in_specs=in_specs, out_specs=out_specs, check_vma=False)
```

```python
import functools

import jax
import jax.numpy as jnp
from jax import lax
from jax.experimental import pallas as pl
from jax.experimental.pallas import tpu as pltpu
from jax.sharding import Mesh, PartitionSpec as P

D = 1024
HEADS = 8
HEAD_DIM = 128
FF = 2816
EPS = 1e-06

ROWS = 128
PARTS = 4
COLS = D // PARTS
TOKENS = PARTS * ROWS
WIDE = 2 * COLS
PAD = 768
SLOT, TAKEN, OWNED = 48, 44, 176
SLOTS, UNITS = 8 * SLOT, 8 * OWNED
FEED_ROWS = 96
LOCAL_HEADS = 2
STATES = PARTS * LOCAL_HEADS
HALF = STATES // 2
TAIL = 16
BF = jnp.bfloat16
F32 = jnp.float32
AXES = ("yh", "z", "x", "yl", "c")
VMEM = 40 * 1024 * 1024


def shift(value, axis, by):
    n = lax.axis_size(axis)
    return lax.ppermute(value, axis, [(i, (i + by) % n) for i in range(n)])


def gather_z(own):
    return (own, shift(own, "z", 1), shift(own, "z", -1), shift(own, "z", 2))


def scatter_z(parts):
    return (parts[0], shift(parts[1], "z", -1), shift(parts[2], "z", 1), shift(parts[3], "z", 2))


def transpose_xz(value, flip):
    pairs = [
        ((yh * 4 + z) * 4 + x, ((yh ^ flip) * 4 + x) * 4 + z) for yh in range(2) for z in range(4) for x in range(4)
    ]
    return lax.ppermute(value, ("yh", "z", "x"), pairs)


def quarters(z):
    return [lax.rem(z + by, 4) for by in (0, 3, 1, 2)]


def exchange(value, axes):
    return lax.all_to_all(value, axes, 0, 0)


def after(value, *others):
    return lax.optimization_barrier((value, *others))[0]


def kernel_call(body, out_shape, *args, scratch=(), flops=0, order=(), near=()):
    if order:
        args = after(args, *order)
    args = [
        a if a.dtype == jnp.int32 else pltpu.with_memory_space_constraint(a, pltpu.VMEM if i in near else pltpu.HBM)
        for i, a in enumerate(args)
    ]
    in_specs = [
        pl.BlockSpec(memory_space=pltpu.SMEM) if a.dtype == jnp.int32 else pl.BlockSpec(memory_space=pltpu.VMEM)
        for a in args
    ]
    out_specs = jax.tree.map(lambda _: pl.BlockSpec(memory_space=pltpu.VMEM), out_shape)
    return pl.pallas_call(
        body,
        out_shape=out_shape,
        in_specs=in_specs,
        out_specs=out_specs,
        scratch_shapes=list(scratch),
        compiler_params=pltpu.CompilerParams(vmem_limit_bytes=VMEM),
        cost_estimate=pl.CostEstimate(flops=1, bytes_accessed=1, transcendentals=0),
    )(*args)


def shape(dims, dtype):
    return pltpu.HBM(dims, dtype)


def near_shape(dims, dtype):
    return pltpu.VMEM(dims, dtype)


def dot(a, b):
    return jnp.dot(a, b, preferred_element_type=F32)


def dot_t(a, b):
    return lax.dot_general(a, b, (((1,), (1,)), ((), ())), preferred_element_type=F32)


def t_dot(a, b):
    return lax.dot_general(a, b, (((0,), (0,)), ((), ())), preferred_element_type=F32)


def exact_dot(a, b):
    return jnp.dot(a, b, precision=lax.Precision.HIGHEST, preferred_element_type=F32)


def mean_scale(value):
    return lax.rsqrt(jnp.mean(value * value, axis=-1, keepdims=True) + EPS)


def triangle(strict, upper):
    row = lax.broadcasted_iota(jnp.int32, (ROWS, ROWS), 0)
    col = lax.broadcasted_iota(jnp.int32, (ROWS, ROWS), 1)
    if upper:
        row, col = col, row
    return row > col if strict else row >= col


def swish_slope(value, sigma):
    return sigma * (1.0 + value * (1.0 - sigma))


def column(ref):
    return jnp.transpose(ref[...].astype(F32))


def row_sums(value):
    return jnp.sum(jnp.transpose(value), axis=0, keepdims=True)


def lane_blocks(value):
    total = value[:, :128]
    for j in range(128, value.shape[1], 128):
        total = total + value[:, j : j + 128]
    return total


def prepare_kernel(z_ref, w_ref, gain_ref, out_w_ref, out_gain_ref, sent_ref, out_ref):
    start = z_ref[0] * COLS
    gain = column(gain_ref)
    for to, j in enumerate((1, 2, 0, 3)):
        cols = pl.ds(pl.multiple_of(j * D + start, 128), COLS)
        block = (w_ref[:, cols].astype(F32) * gain).astype(BF)
        for i in range(8):
            sent_ref[i, :, to * COLS : (to + 1) * COLS] = block
    out_ref[...] = (out_w_ref[...].astype(F32) * column(out_gain_ref)).astype(BF)


def selection(z, slots, units, slots_first):
    shape_ = (slots, units) if slots_first else (units, slots)
    line = (slots, 1) if slots_first else (1, slots)
    slot = lax.broadcasted_iota(jnp.int32, line, 0 if slots_first else 1)
    owner = jnp.zeros(line, jnp.int32)
    for i in range(1, slots // SLOT):
        owner = owner + (slot >= i * SLOT).astype(jnp.int32)
    place = slot - owner * SLOT
    unit = jnp.where(place < TAKEN, owner * OWNED + z * TAKEN + place, -1)
    return jnp.where(lax.broadcasted_iota(jnp.int32, shape_, 1 if slots_first else 0) == unit, 1.0, 0.0).astype(BF)


def prepare_feed_kernel(z_ref, up_ref, gain_ref, down_ref, out_ref):
    gain = column(gain_ref)
    chosen = selection(z_ref[0], SLOTS, UNITS, False)
    for i in range(4):
        picked = dot(up_ref[:, i * UNITS : (i + 1) * UNITS], chosen)
        out_ref[:64, i * SLOTS : (i + 1) * SLOTS] = (picked * gain).astype(BF)
    rows = dot(selection(z_ref[0], SLOT, OWNED, True), down_ref[...]).astype(BF)
    out_ref[64:, :D] = rows[:32]
    out_ref[64:80, D:] = rows[32:, :512]
    out_ref[80:, D:] = rows[32:, 512:]


def gated(pre, floor):
    sigma = lax.logistic(pre)
    return sigma, floor + (1.0 - floor) * sigma


def swish(value):
    return value * lax.logistic(value)


def head_cols(h):
    return slice(h * HEAD_DIM, (h + 1) * HEAD_DIM)


def part_rows(b):
    return slice(b * ROWS, (b + 1) * ROWS)


def first_kernel(core_ref, x0, x1, x2, x3, mine_ref, other_ref, floor_ref,
                 x_ref, w_ref, w_qg_ref, pre_ref, cum_ref, state_ref, total_ref):
    core = core_ref[0]
    for ref, lanes in ((w_ref, slice(0, WIDE)), (w_qg_ref, slice(WIDE, D))):
        ref[:, pl.ds(core, 1)] = mine_ref[:, :, lanes].reshape(8, 1, 64, WIDE)
        ref[:, pl.ds(1 - core, 1)] = other_ref[:, :, lanes].reshape(8, 1, 64, WIDE)
    for b, part in enumerate((x0, x1, x2, x3)):
        value = part[...].astype(F32)
        x_ref[part_rows(b), :] = (value * mean_scale(value)).astype(BF)
    pre_ref[...] = dot(x_ref[...], w_ref[...].reshape(D, WIDE))
    ones = triangle(False, False).astype(F32)
    floor = floor_ref[...]
    for b in range(PARTS):
        rows = part_rows(b)
        _, decay = gated(pre_ref[rows, :COLS], floor)
        cum_all = exact_dot(ones, jnp.log(decay))
        cum_ref[rows, :] = cum_all
        total_all = cum_all[ROWS - 1 :, :]
        k_out = ((1.0 - decay).astype(BF).astype(F32) * jnp.exp(total_all - cum_all)).astype(BF)
        for h in range(LOCAL_HEADS):
            value = pre_ref[rows, COLS + h * HEAD_DIM : COLS + (h + 1) * HEAD_DIM].astype(BF)
            s = h * PARTS + b
            state_ref[s] = t_dot(k_out[:, head_cols(h)], value).astype(BF)
            total_ref[s : s + 1, :] = total_all[:, head_cols(h)]


def second_kernel(x_ref, w_ref, fv_ref, cum_ref, floor_ref, pre_ref, q_ref, local_ref):
    pre_ref[...] = dot(x_ref[...], w_ref[...].reshape(D, WIDE))
    causal = triangle(False, False)
    floor = floor_ref[...]
    for b in range(PARTS):
        rows = part_rows(b)
        _, decay = gated(fv_ref[rows, :COLS], floor)
        cum = cum_ref[rows, :]
        k_in = ((1.0 - decay).astype(BF).astype(F32) * jnp.exp(-cum)).astype(BF)
        q_in = (swish(pre_ref[rows, :COLS]).astype(BF).astype(F32) * jnp.exp(cum)).astype(BF)
        q_ref[rows, :] = q_in
        value = fv_ref[rows, COLS:].astype(BF)
        for h in range(LOCAL_HEADS):
            cols = head_cols(h)
            scores = jnp.where(causal, dot_t(q_in[:, cols], k_in[:, cols]), 0.0).astype(BF)
            local_ref[rows, cols] = dot(scores, value[:, cols])


def split3(value):
    first = value.astype(BF).astype(F32)
    second = (value - first).astype(BF).astype(F32)
    return first, second, value - first - second


def chip_kernel(core_ref, mine_ref, other_ref, my_total_ref, other_total_ref, out_ref, *, backward):
    core = core_ref[0]
    second = core == (0 if backward else 1)
    base = core * HALF
    my_total = my_total_ref[pl.ds(base, HALF), :]
    other_total = other_total_ref[pl.ds(base, HALF), :]
    last_decay = jnp.exp(jnp.where(second, my_total, other_total))
    for i in range(HALF):
        mine = mine_ref[base + i].astype(F32)
        other = other_ref[base + i].astype(F32)
        last = jnp.where(second, mine, other)
        first = jnp.where(second, other, mine)
        state = (jnp.transpose(last_decay[i : i + 1, :]) * first + last).astype(BF)
        for d in range(8):
            out_ref[d, i * HEAD_DIM : (i + 1) * HEAD_DIM, :] = state
    if not backward:
        pieces = split3(my_total + other_total)
        tail = jnp.concatenate([*pieces, jnp.zeros((HALF, HEAD_DIM), F32)], axis=0).astype(BF)
        for d in range(8):
            out_ref[d, HALF * HEAD_DIM :, :] = tail


def carry_kernel(place_ref, all_ref, *refs, backward):
    place = place_ref[0]
    if backward:
        totals_ref, out_ref = refs
    else:
        out_ref, totals_ref = refs
        for j in range(8):
            tail = all_ref[j, HALF * HEAD_DIM :, :].astype(F32)
            totals_ref[j] = (tail[:HALF] + tail[HALF : 2 * HALF]) + tail[2 * HALF : 3 * HALF]
    for i in range(HALF):
        carried = jnp.zeros((HEAD_DIM, HEAD_DIM), F32)
        decays = jnp.transpose(jnp.exp(jnp.concatenate([totals_ref[j, i : i + 1, :] for j in range(8)], axis=0)))
        for step in range(7):
            j = 7 - step if backward else step
            reached = j > place if backward else j < place
            block = all_ref[j, i * HEAD_DIM : (i + 1) * HEAD_DIM, :].astype(F32)
            carried = jnp.where(reached, decays[:, j : j + 1] * carried + block, carried)
        out_ref[i] = carried.astype(BF)


def enter_state(core, own_half, other_half, other_end, other_total, s, backward):
    h, b = divmod(s, PARTS)
    chip = jnp.where(core == h, own_half[b], other_half[b]).astype(F32)
    later = core == (0 if backward else 1)
    passed = jnp.transpose(jnp.exp(other_total[s : s + 1, :])) * chip + other_end[s].astype(F32)
    return jnp.where(later, passed, chip)


def mix_kernel(core_ref, pre_ref, q_ref, local_ref, own_half, other_half, other_end, other_total, w_ref,
               out_ref, normed_ref, entered_ref, p0, p1, p2, p3):
    core = core_ref[0]
    for b in range(PARTS):
        rows = part_rows(b)
        for h in range(LOCAL_HEADS):
            cols = head_cols(h)
            s = h * PARTS + b
            state = enter_state(core, own_half, other_half, other_end, other_total, s, False).astype(BF)
            entered_ref[s] = state
            mixed = local_ref[rows, cols] + dot(q_ref[rows, cols], state)
            out_ref[rows, cols] = mixed
            gate = pre_ref[rows, COLS + h * HEAD_DIM : COLS + (h + 1) * HEAD_DIM]
            normed_ref[rows, cols] = (mixed * mean_scale(mixed) * swish(gate)).astype(BF)
    product = dot(normed_ref[...], w_ref[...]).astype(BF)
    for b, part in enumerate((p0, p1, p2, p3)):
        part[...] = product[part_rows(b), :]


def sum_parts(p0, p1, p2, p3):
    return (p0[...].astype(F32) + p1[...].astype(F32)) + (p2[...].astype(F32) + p3[...].astype(F32))


def middle_kernel(hidden_ref, p0, p1, p2, p3, middle_ref, normed_ref):
    middle = hidden_ref[...].astype(F32) + sum_parts(p0, p1, p2, p3)
    middle_ref[...] = middle
    normed_ref[...] = (middle * mean_scale(middle)).astype(BF)


def feed_inputs(parts, grads, w_ref, x_ref, g_ref, down_ref):
    for s in range(16):
        at = s * SLOT
        rows = w_ref[s, w_ref.shape[1] - 32 :, :]
        down_ref[at : at + 32, :] = rows[:, :D]
        down_ref[at + 32 : at + 48, :512] = rows[:16, D:]
        down_ref[at + 32 : at + 48, 512:] = rows[16:, D:]
    for b in range(PARTS):
        x_ref[part_rows(b), :] = parts[b][...]
        g_ref[part_rows(b), :] = grads[b][...]


def feed_kernel(x0, x1, x2, x3, g0, g1, g2, g3, w_ref, act_ref, grad_ref, p0, p1, p2, p3, x_ref, g_ref, down_ref):
    feed_inputs((x0, x1, x2, x3), (g0, g1, g2, g3), w_ref, x_ref, g_ref, down_ref)
    for j in range(3):
        lanes = slice(j * COLS, (j + 1) * COLS)
        ups = slice(PAD + j * COLS, PAD + (j + 1) * COLS)
        gate = dot(x_ref[...], w_ref[:, :64, lanes].reshape(D, COLS))
        up = dot(x_ref[...], w_ref[:, :64, ups].reshape(D, COLS))
        grad = dot_t(g_ref[...], down_ref[lanes, :])
        sigma = lax.logistic(gate)
        active = gate * sigma
        act_ref[:, lanes] = (active * up).astype(BF)
        grad_ref[:, lanes] = (grad * up * swish_slope(gate, sigma)).astype(BF)
        grad_ref[:, ups] = (grad * active).astype(BF)
    product = dot_t(grad_ref[...], w_ref[:, :64, :].reshape(D, 2 * PAD)).astype(BF)
    for b, part in enumerate((p0, p1, p2, p3)):
        part[...] = product[part_rows(b), :]


def feed_grad_kernel(x0, x1, x2, x3, g0, g1, g2, g3, w_ref, grad_ref, act_ref, out_ref, p0, p1, p2, p3,
                     x_ref, g_ref, down_ref):
    feed_inputs((x0, x1, x2, x3), (g0, g1, g2, g3), w_ref, x_ref, g_ref, down_ref)
    product = dot(act_ref[...], down_ref[...]).astype(BF)
    for b, part in enumerate((p0, p1, p2, p3)):
        part[...] = product[part_rows(b), :]
    for j in range(0, 2 * PAD, 512):
        out_ref[:, :64, j : j + 512] = t_dot(x_ref[...], grad_ref[:, j : j + 512]).astype(BF).reshape(16, 64, 512)
    rows = t_dot(act_ref[...], g_ref[...]).astype(BF)
    for s in range(16):
        at = s * SLOT
        out_ref[s, 64:, :D] = rows[at : at + 32]
        out_ref[s, 64:80, D:] = rows[at + 32 : at + 48, :512]
        out_ref[s, 80:, D:] = rows[at + 32 : at + 48, 512:]


def add_kernel(a_ref, b_ref, out_ref):
    out_ref[...] = (a_ref[...].astype(F32) + b_ref[...].astype(F32)).astype(BF)


def result_kernel(middle_ref, p0, p1, p2, p3, out_ref):
    out_ref[...] = (middle_ref[...] + sum_parts(p0, p1, p2, p3)).astype(BF)


def norm_back(value_ref, base_ref, u):
    value = value_ref[...].astype(F32)
    scale = mean_scale(value)
    centered = value * scale
    back = scale * (u - centered * jnp.mean(u * centered, axis=-1, keepdims=True))
    return base_ref[...].astype(F32) + back


def branch_kernel(value_ref, base_ref, p0, p1, p2, p3, out_ref, low_ref):
    total = norm_back(value_ref, base_ref, sum_parts(p0, p1, p2, p3))
    out_ref[...] = total
    low_ref[...] = total.astype(BF)


def last_kernel(value_ref, base_ref, p0, p1, p2, p3, low_ref):
    low_ref[...] = norm_back(value_ref, base_ref, sum_parts(p0, p1, p2, p3)).astype(BF)


def head_back_kernel(b0, b1, b2, b3, w_ref, pre_ref, q_ref, mixed_ref, branch_ref, gate_ref, out_grad_ref, state_ref):
    for b, part in enumerate((b0, b1, b2, b3)):
        branch_ref[part_rows(b), :] = part[...]
    grads = dot_t(branch_ref[...], w_ref[...])
    for b in range(PARTS):
        rows = part_rows(b)
        for h in range(LOCAL_HEADS):
            cols = head_cols(h)
            grad = grads[rows, cols]
            mixed = mixed_ref[rows, cols]
            scale = mean_scale(mixed)
            normed = mixed * scale
            gate = pre_ref[rows, COLS + h * HEAD_DIM : COLS + (h + 1) * HEAD_DIM]
            sigma = lax.logistic(gate)
            gate_ref[rows, cols] = (grad * normed * swish_slope(gate, sigma)).astype(BF)
            c = grad * (gate * sigma)
            mixer = (scale * (c - normed * jnp.mean(c * normed, axis=-1, keepdims=True))).astype(BF)
            out_grad_ref[rows, cols] = mixer
            state_ref[h * PARTS + b] = t_dot(q_ref[rows, cols], mixer).astype(BF)


def near_back_kernel(core_ref, x_ref, normed_ref, branch_ref, qg_ref, fv_ref, cum_ref, floor_ref, q_ref, gate_ref,
                     out_grad_ref, entered_ref, grad_ref, log_ref, key_ref, value_ref,
                     mine_ref, other_ref, my_rows_ref, other_rows_ref, all_ref, rows_ref):
    causal = triangle(False, False)
    suffix = triangle(False, True).astype(F32)
    floor = floor_ref[...]
    for b in range(PARTS):
        rows = part_rows(b)
        _, decay = gated(fv_ref[rows, :COLS], floor)
        cum = cum_ref[rows, :]
        grow_all = jnp.exp(cum)
        shrink_all = jnp.exp(-cum)
        k_all = ((1.0 - decay).astype(BF).astype(F32) * shrink_all).astype(BF)
        q_pre = qg_ref[rows, :COLS]
        slope_all = swish_slope(q_pre, lax.logistic(q_pre))
        for h in range(LOCAL_HEADS):
            cols = head_cols(h)
            value = fv_ref[rows, COLS + h * HEAD_DIM : COLS + (h + 1) * HEAD_DIM].astype(BF)
            q_in, k_in = q_ref[rows, cols], k_all[:, cols]
            out_grad = out_grad_ref[rows, cols]
            scores = jnp.where(causal, dot_t(q_in, k_in), 0.0).astype(BF)
            grad_scores = jnp.where(causal, dot_t(out_grad, value), 0.0).astype(BF)
            inner = dot(grad_scores, k_in) + dot_t(out_grad, entered_ref[h * PARTS + b])
            back = t_dot(grad_scores, q_in)
            near = q_in.astype(F32) * inner - k_in.astype(F32) * back
            log_ref[rows, cols] = exact_dot(suffix, near)
            key_ref[rows, cols] = back * shrink_all[:, cols]
            value_ref[rows, cols] = t_dot(scores, out_grad)
            grad_ref[rows, cols] = (inner * grow_all[:, cols] * slope_all[:, cols]).astype(BF)
    grad_ref[:, COLS:] = gate_ref[...]
    column_grad(core_ref[0], x_ref, grad_ref, mine_ref, other_ref, all_ref)
    row_grad(core_ref[0], normed_ref, branch_ref, my_rows_ref, other_rows_ref, rows_ref)


def far_back_kernel(core_ref, fv_ref, cum_ref, floor_ref, log_ref, key_ref, value_ref, entered_ref, own_half, other_half,
                    other_end, other_total, qg_ref, w_fv_ref, w_qg_ref, x_ref,
                    floor_grad_ref, mine_ref, other_ref, p0, p1, p2, p3, grad_ref, all_ref):
    core = core_ref[0]
    before = triangle(True, False).astype(F32)
    floor = floor_ref[...]
    floor_sum = jnp.zeros((1, COLS), F32)
    for b in range(PARTS):
        rows = part_rows(b)
        sigma, decay = gated(fv_ref[rows, :COLS], floor)
        cum = cum_ref[rows, :]
        total = cum[ROWS - 1 :, :]
        to_end = jnp.exp(total - cum)
        k_all = ((1.0 - decay).astype(BF).astype(F32) * to_end).astype(BF)
        aheads, edges = [], []
        for h in range(LOCAL_HEADS):
            cols = head_cols(h)
            s = h * PARTS + b
            following = enter_state(core, own_half, other_half, other_end, other_total, s, True)
            low = following.astype(BF)
            value = fv_ref[rows, COLS + h * HEAD_DIM : COLS + (h + 1) * HEAD_DIM].astype(BF)
            aheads.append(dot_t(value, low))
            edges.append(jnp.transpose(jnp.sum(following * entered_ref[s].astype(F32), axis=1, keepdims=True)))
            grad_value = value_ref[rows, cols] + dot(k_all[:, cols], low)
            grad_ref[rows, COLS + h * HEAD_DIM : COLS + (h + 1) * HEAD_DIM] = grad_value.astype(BF)
        ahead = jnp.concatenate(aheads, axis=1)
        edge = jnp.concatenate(edges, axis=1)
        far = exact_dot(before, k_all.astype(F32) * ahead)
        grad_log = log_ref[rows, :] + far + jnp.exp(total) * edge
        grad_decay = grad_log / decay - (key_ref[rows, :] + ahead * to_end)
        floor_sum = floor_sum + jnp.sum(grad_decay * (1.0 - sigma), axis=0, keepdims=True)
        grad_ref[rows, :COLS] = (grad_decay * (1.0 - floor) * sigma * (1.0 - sigma)).astype(BF)
    floor_grad_ref[...] = floor_sum
    column_grad(core, x_ref, grad_ref, mine_ref, other_ref, all_ref)
    product = dot_t(grad_ref[...], w_fv_ref[...].reshape(D, WIDE)) + dot_t(qg_ref[...], w_qg_ref[...].reshape(D, WIDE))
    product = product.astype(BF)
    for b, part in enumerate((p0, p1, p2, p3)):
        part[...] = product[part_rows(b), :]


def column_grad(core, a_ref, g_ref, mine_ref, other_ref, all_ref):
    n = g_ref.shape[1]
    all_ref[...] = t_dot(a_ref[...], g_ref[...]).astype(BF).reshape(8, 2, 64, n)
    mine_ref[...] = all_ref[:, pl.ds(core, 1)].reshape(8, 64, n)
    other_ref[...] = all_ref[:, pl.ds(1 - core, 1)].reshape(8, 64, n)


def row_grad(core, a_ref, g_ref, mine_ref, other_ref, all_ref):
    rows = mine_ref.shape[1]
    all_ref[...] = t_dot(a_ref[...], g_ref[...]).astype(BF).reshape(2, 2, rows, D)
    mine_ref[...] = all_ref[:, pl.ds(core, 1)].reshape(2, rows, D)
    other_ref[...] = all_ref[:, pl.ds(1 - core, 1)].reshape(2, rows, D)


def pack_columns(mine_ref, other_ref, out_ref, start):
    lanes = mine_ref.shape[2] // 2
    for i in range(8):
        value = (mine_ref[i].astype(F32) + other_ref[i].astype(F32)).astype(BF)
        for half in range(2):
            for j in range(lanes // 128):
                at = half * lanes + j * 128
                out_ref[i * 2 + half, start + j * 64 : start + (j + 1) * 64, :] = value[:, at : at + 128]


def pack_rows(mine_ref, other_ref, out_ref, start):
    rows = mine_ref.shape[1]
    for yl in range(2):
        value = (mine_ref[yl].astype(F32) + other_ref[yl].astype(F32)).astype(BF)
        for p in range(8):
            to = (p // 2) * 4 + yl * 2 + p % 2
            out_ref[to, start : start + rows, :] = value[:, p * 128 : (p + 1) * 128]


def rider_rows(value):
    rows = [piece[:, cols] for piece in split3(value) for cols in (slice(0, 128), slice(128, 256))]
    return jnp.concatenate([*rows, jnp.zeros((10, 128), F32)], axis=0).astype(BF)


def rider_value(rows):
    rows = rows.astype(F32)
    halves = [(rows[i : i + 1] + rows[i + 2 : i + 3]) + rows[i + 4 : i + 5] for i in range(2)]
    return jnp.concatenate(halves, axis=1)


def pack_kernel(mine_ref, other_ref, floor_ref, other_floor_ref, my_qg_ref, other_qg_ref, my_rows_ref, other_rows_ref, out_ref):
    pack_columns(mine_ref, other_ref, out_ref, 0)
    rider = rider_rows(floor_ref[...] + other_floor_ref[...])
    for i in range(16):
        out_ref[i, 128:144, :] = rider
    pack_columns(my_qg_ref, other_qg_ref, out_ref, 144)
    pack_rows(my_rows_ref, other_rows_ref, out_ref, 272)


def total_of(all_ref, rows):
    total = all_ref[0, rows, :].astype(F32)
    for i in range(1, 16):
        total = total + all_ref[i, rows, :].astype(F32)
    return total


def sum_kernel(all_ref, out_ref, rows_ref):
    first = total_of(all_ref, slice(0, 128)).astype(BF)
    floor = rider_value(all_ref[0, 128:144, :])
    for i in range(1, 16):
        floor = floor + rider_value(all_ref[i, 128:144, :])
    rider = rider_rows(floor)
    second = total_of(all_ref, slice(144, 272)).astype(BF)
    for i in range(8):
        out_ref[i, :128, :] = first
        out_ref[i, 128:144, :] = rider
        out_ref[i, 144:, :] = second
    rows_ref[...] = total_of(all_ref, slice(272, 336)).astype(BF)


def feed_grads_kernel(z_ref, s0, s1, s2, s3, w_ref, gain_ref, up_ref, gain_grad_ref, down_ref):
    chosen = jnp.concatenate([selection(z, SLOTS, UNITS, True) for z in quarters(z_ref[0])], axis=0)
    gain = column(gain_ref)
    gain_grad = jnp.zeros((64, 128), F32)
    taken = jnp.concatenate(
        [
            jnp.concatenate([ref[:64, i * SLOTS : (i + 1) * SLOTS] for ref in (s0, s1, s2, s3)], axis=1)
            for i in range(4)
        ],
        axis=0,
    )
    values = dot(taken, chosen)
    for i in range(4):
        value = values[i * 64 : (i + 1) * 64]
        cols = slice(i * UNITS, (i + 1) * UNITS)
        up_ref[:, cols] = value * gain
        gain_grad = gain_grad + lane_blocks(value * w_ref[:, cols].astype(F32))
    gain_grad_ref[...] = row_sums(gain_grad)
    down = jnp.zeros((OWNED, D), F32)
    for z, ref in zip(quarters(z_ref[0]), (s0, s1, s2, s3)):
        last = jnp.concatenate([ref[64:80, D:], ref[80:, D:]], axis=1)
        rows = jnp.concatenate([ref[64:, :D], last], axis=0)
        down = down + dot(selection(z, SLOT, OWNED, False), rows)
    down_ref[...] = down


def mix_grads_kernel(z_ref, yh_ref, all_ref, o0, o1, o2, o3, w_ref, gain_ref, out_w_ref, out_gain_ref,
                     mix_ref, gain_grad_ref, out_ref, out_gain_grad_ref, floor_ref):
    gain, out_gain = column(gain_ref), column(out_gain_ref)
    gain_grad = jnp.zeros((64, 128), F32)
    out_gain_grad = jnp.zeros((64, 128), F32)
    for yh in range(2):
        for z in range(4):
            i = yh * 4 + z
            for start, block in ((0, 2 if yh else 1), (144, 3 if yh else 0)):
                for j in range(2):
                    value = all_ref[i, start + j * 64 : start + (j + 1) * 64, :].astype(F32)
                    at = block * D + z * COLS + j * 128
                    mix_ref[:, at : at + 128] = value * gain
                    gain_grad = gain_grad + value * w_ref[:, at : at + 128].astype(F32)
            if yh == 0:
                floor_ref[:, z * COLS : (z + 1) * COLS] = rider_value(all_ref[i, 128:144, :])
    for z, ref in zip(quarters(z_ref[0]), (o0, o1, o2, o3)):
        for k in range(2):
            yh = yh_ref[0] if k == 0 else 1 - yh_ref[0]
            cols = pl.ds(pl.multiple_of((z * 2 + yh) * 128, 128), 128)
            value = ref[k * 64 : (k + 1) * 64, :].astype(F32)
            out_ref[:, cols] = value * out_gain
            out_gain_grad = out_gain_grad + value * out_w_ref[:, cols].astype(F32)
    gain_grad_ref[...] = row_sums(gain_grad)
    out_gain_grad_ref[...] = row_sums(out_gain_grad)


def scalar(value):
    return value.reshape(1).astype(jnp.int32)


def body(hidden, mixer_weight, output_weight, gate_up_weight, down_weight, mixer_gain, group_gain, feed_gain,
         forget_floor, out_grad):
    z = lax.axis_index("z")
    z_of, yh_of = scalar(z), scalar(lax.axis_index("yh"))
    core = scalar(lax.axis_index("c"))
    place = scalar(lax.axis_index("x") * 2 + lax.axis_index("yl"))
    gain_one, gain_group, gain_two = (g.reshape(1, 64) for g in (mixer_gain, group_gain, feed_gain))
    floor = lax.dynamic_index_in_dim(forget_floor.reshape(PARTS, COLS), z, 0)
    own = [near_shape((ROWS, D), BF)] * 4
    state_dims = (STATES, HEAD_DIM, HEAD_DIM)
    half_dims = (HALF, HEAD_DIM, HEAD_DIM)

    w_sent, out_own = kernel_call(
        prepare_kernel, (shape((8, 64, D), BF), shape((64, D), BF)),
        z_of, mixer_weight, gain_one, output_weight, gain_group,
    )
    tokens = gather_z(hidden)
    w_mine = exchange(w_sent, ("x", "yl"))
    w_out = lax.all_gather(out_own, ("x", "yl", "c"))
    w_other = shift(after(w_mine, *tokens), "c", 1)
    x_all, w_fv, w_qg, pre_fv, cum, end, total = kernel_call(
        first_kernel,
        (
            shape((TOKENS, D), BF),
            shape((8, 2, 64, WIDE), BF),
            shape((8, 2, 64, WIDE), BF),
            shape((TOKENS, WIDE), F32),
            shape((TOKENS, COLS), F32),
            near_shape(state_dims, BF),
            shape((STATES, HEAD_DIM), F32),
        ),
        core, *tokens, w_mine, w_other, floor,
        flops=2 * TOKENS * D * WIDE,
        near=(5, 6),
    )

    def chip_state(end_state, other_total, backward, order=()):
        other_end = shift(end_state, "c", 1)
        sent = kernel_call(
            functools.partial(chip_kernel, backward=backward),
            shape((8, HALF * HEAD_DIM + (0 if backward else TAIL), HEAD_DIM), BF),
            core, end_state, other_end, total, other_total,
            order=order,
            near=(1, 2),
        )
        return sent, other_end

    other_total = shift(total, "c", 1)
    sent, other_end = chip_state(end, other_total, False)
    arrived = exchange(sent, ("x", "yl"))
    grads_out = gather_z(after(out_grad, sent))
    pre_qg, q_in, local_out = kernel_call(
        second_kernel,
        (shape((TOKENS, WIDE), F32), shape((TOKENS, COLS), BF), shape((TOKENS, COLS), F32)),
        x_all, w_qg, pre_fv, cum, floor,
        flops=2 * TOKENS * D * WIDE,
        order=(sent,),
    )
    w_out = lax.dynamic_index_in_dim(w_out.reshape(PARTS, COLS, D), z, 0, keepdims=False)
    feed_own_weights = kernel_call(
        prepare_feed_kernel, shape((FEED_ROWS, 2 * PAD), BF), z_of, gate_up_weight, gain_two, down_weight,
        order=(q_in, w_out),
    )
    w_feed = lax.all_gather(after(feed_own_weights, arrived, *grads_out), ("x", "yl", "c"))
    own_half, totals = kernel_call(
        functools.partial(carry_kernel, backward=False),
        (near_shape(half_dims, BF), shape((8, HALF, HEAD_DIM), F32)),
        place, arrived,
        order=(feed_own_weights, w_out, *grads_out),
        near=(1,),
    )
    mixed, normed_out, entered, *parts = kernel_call(
        mix_kernel,
        (shape((TOKENS, COLS), F32), shape((TOKENS, COLS), BF), shape(state_dims, BF), *own),
        core, pre_qg, q_in, local_out, own_half, shift(own_half, "c", 1), other_end, other_total, w_out,
        flops=2 * TOKENS * COLS * D,
        near=(4, 5),
    )
    middle, feed_own = kernel_call(
        middle_kernel, (shape((ROWS, D), F32), near_shape((ROWS, D), BF)), hidden, *scatter_z(parts),
        near=(1, 2, 3, 4),
    )
    feed_in = (*gather_z(feed_own), *grads_out, w_feed)
    feed_scratch = [pltpu.VMEM((TOKENS, D), BF), pltpu.VMEM((TOKENS, D), BF), pltpu.VMEM((PAD, D), BF)]
    act, grad_up, *parts = kernel_call(
        feed_kernel,
        (shape((TOKENS, PAD), BF), shape((TOKENS, 2 * PAD), BF), *own),
        *feed_in,
        scratch=feed_scratch,
        flops=2 * TOKENS * D * PAD * 5,
    )
    feed_back = scatter_z(parts)
    feed_grad, *down_parts = kernel_call(
        feed_grad_kernel,
        (shape((16, FEED_ROWS, 2 * PAD), BF), *[shape((ROWS, D), BF)] * 4),
        *feed_in, grad_up, act,
        scratch=feed_scratch,
        flops=2 * TOKENS * D * PAD * 3,
        order=(parts[3],),
    )
    grad_middle, branch_own = kernel_call(
        branch_kernel, (shape((ROWS, D), F32), near_shape((ROWS, D), BF)), middle, out_grad, *feed_back,
        order=(feed_grad,),
        near=(2, 3, 4, 5),
    )
    feed_sum = lax.psum_scatter(after(feed_grad, *feed_back), ("x", "yl", "c"), scatter_dimension=0)
    branch = gather_z(branch_own)
    branch_all, grad_gate, grad_mixed, end_grad = kernel_call(
        head_back_kernel,
        (
            shape((TOKENS, D), BF),
            shape((TOKENS, COLS), BF),
            shape((TOKENS, COLS), BF),
            near_shape(state_dims, BF),
        ),
        *branch, w_out, pre_qg, q_in, mixed,
        flops=2 * TOKENS * COLS * D,
        near=(0, 1, 2, 3),
    )

    sent, other_end = chip_state(end_grad, other_total, True)
    down_parts = scatter_z(after(down_parts, sent))
    arrived = exchange(sent, ("x", "yl"))
    grad_qg, near_log, near_key, near_value, qg_mine, qg_other, out_mine, out_other = kernel_call(
        near_back_kernel,
        (
            shape((TOKENS, WIDE), BF),
            *[shape((TOKENS, COLS), F32)] * 3,
            *[shape((8, 64, WIDE), BF)] * 2,
            *[shape((2, 64, D), BF)] * 2,
        ),
        core, x_all, normed_out, branch_all, pre_qg, pre_fv, cum, floor, q_in, grad_gate, grad_mixed, entered,
        scratch=[pltpu.VMEM((8, 2, 64, WIDE), BF), pltpu.VMEM((2, 2, 64, D), BF)],
        flops=2 * TOKENS * (HEAD_DIM * HEAD_DIM * 12 + D * WIDE),
        order=(sent,),
    )
    own_half = kernel_call(
        functools.partial(carry_kernel, backward=True), near_shape(half_dims, BF), place, arrived, totals,
        order=(grad_qg, *down_parts),
        near=(1,),
    )
    qg_other, out_other = after((qg_other, out_other), own_half)
    floor_part, fv_mine, fv_other, *parts = kernel_call(
        far_back_kernel,
        (shape((1, COLS), F32), *[shape((8, 64, WIDE), BF)] * 2, *[shape((ROWS, D), BF)] * 4),
        core, pre_fv, cum, floor, near_log, near_key, near_value, entered, own_half, shift(own_half, "c", 1), other_end,
        other_total, grad_qg, w_fv, w_qg, x_all,
        scratch=[pltpu.VMEM((TOKENS, WIDE), BF), pltpu.VMEM((8, 2, 64, WIDE), BF)],
        flops=2 * TOKENS * D * D * 2,
    )
    sent = kernel_call(
        pack_kernel, shape((16, 336, 128), BF), fv_mine, shift(fv_other, "c", 1), floor_part,
        shift(floor_part, "c", 1), qg_mine, shift(qg_other, "c", 1), out_mine, shift(out_other, "c", 1),
    )

    arrived = exchange(sent, ("x", "yl", "yh"))
    parts = scatter_z(after(parts, sent))
    feed_other = shift(after(feed_sum, *parts), "yh", 1)
    result = kernel_call(result_kernel, shape((ROWS, D), BF), middle, *down_parts, order=(sent,))
    grad_tokens = kernel_call(last_kernel, shape((ROWS, D), BF), hidden, grad_middle, *parts, order=(result,))
    copies, rows = kernel_call(
        sum_kernel, (shape((8, 272, 128), BF), shape((64, 128), BF)), arrived, order=(feed_other, grad_tokens), near=(0,)
    )
    last_sums = exchange(copies, ("yh", "z"))
    out_sums = gather_z(jnp.concatenate([transpose_xz(rows, 0), transpose_xz(rows, 1)], axis=0))
    feed_total = kernel_call(
        add_kernel, shape((FEED_ROWS, 2 * PAD), BF), feed_sum, feed_other, order=(copies,)
    )
    feed_totals = gather_z(feed_total)
    up_grad, feed_gain_grad, down_grad = kernel_call(
        feed_grads_kernel,
        (shape((64, 2 * FF), F32), shape((1, 64), F32), shape((OWNED, D), F32)),
        z_of, *feed_totals, gate_up_weight, gain_two,
        order=(copies,),
    )
    mix_grad, gain_grad, out_weight_grad, group_gain_grad, floor_grad = kernel_call(
        mix_grads_kernel,
        (
            shape((64, 4 * D), F32),
            shape((1, 64), F32),
            shape((64, D), F32),
            shape((1, 64), F32),
            shape((1, D), F32),
        ),
        z_of, yh_of, last_sums, *out_sums, mixer_weight, gain_one, output_weight, gain_group,
        order=(up_grad,),
        near=(2,),
    )
    return (
        result,
        grad_tokens,
        mix_grad,
        out_weight_grad,
        up_grad,
        down_grad,
        gain_grad.reshape(64),
        group_gain_grad.reshape(64),
        feed_gain_grad.reshape(64),
        floor_grad.reshape(D),
    )


def solution(mesh):
    cut = Mesh(mesh.devices.reshape(2, 4, 4, 2, 2), AXES)
    seq = ("x", "yl", "c")
    rows, weight, vector = P(AXES, None), P(seq, None), P(seq)
    in_specs = (rows, weight, weight, weight, weight, vector, vector, vector, P(), rows)
    out_specs = (rows, rows, weight, weight, weight, weight, vector, vector, vector, P())
    return jax.shard_map(body, mesh=cut, in_specs=in_specs, out_specs=out_specs, check_vma=False)
```

```python
import functools

import jax
import jax.numpy as jnp
from jax import lax
from jax.experimental import pallas as pl
from jax.experimental.pallas import tpu as pltpu
from jax.sharding import Mesh, PartitionSpec as P

D = 1024
HEADS = 8
HEAD_DIM = 128
FF = 2816
EPS = 1e-06

ROWS = 128
PARTS = 4
COLS = D // PARTS
TOKENS = PARTS * ROWS
WIDE = 2 * COLS
PAD = 768
SLOT, TAKEN, OWNED = 48, 44, 176
SLOTS, UNITS = 8 * SLOT, 8 * OWNED
FEED_ROWS = 96
LOCAL_HEADS = 2
STATES = PARTS * LOCAL_HEADS
HALF = STATES // 2
TAIL = 16
BF = jnp.bfloat16
F32 = jnp.float32
AXES = ("yh", "z", "x", "yl", "c")
VMEM = 40 * 1024 * 1024


def shift(value, axis, by):
    n = lax.axis_size(axis)
    return lax.ppermute(value, axis, [(i, (i + by) % n) for i in range(n)])


def gather_z(own):
    return (own, shift(own, "z", 1), shift(own, "z", -1), shift(own, "z", 2))


def scatter_z(parts):
    return (parts[0], shift(parts[1], "z", -1), shift(parts[2], "z", 1), shift(parts[3], "z", 2))


def transpose_xz(value):
    pairs = [(z * 4 + x, x * 4 + z) for z in range(4) for x in range(4)]
    return lax.ppermute(value, ("z", "x"), pairs)


def quarters(z):
    return [lax.rem(z + by, 4) for by in (0, 3, 1, 2)]


def exchange(value, axes):
    return lax.all_to_all(value, axes, 0, 0)


def after(value, *others):
    return lax.optimization_barrier((value, *others))[0]


def kernel_call(body, out_shape, *args, scratch=(), flops=0, order=(), near=()):
    if order:
        args = after(args, *order)
    args = [
        a if a.dtype == jnp.int32 else pltpu.with_memory_space_constraint(a, pltpu.VMEM if i in near else pltpu.HBM)
        for i, a in enumerate(args)
    ]
    in_specs = [
        pl.BlockSpec(memory_space=pltpu.SMEM) if a.dtype == jnp.int32 else pl.BlockSpec(memory_space=pltpu.VMEM)
        for a in args
    ]
    out_specs = jax.tree.map(lambda _: pl.BlockSpec(memory_space=pltpu.VMEM), out_shape)
    return pl.pallas_call(
        body,
        out_shape=out_shape,
        in_specs=in_specs,
        out_specs=out_specs,
        scratch_shapes=list(scratch),
        compiler_params=pltpu.CompilerParams(vmem_limit_bytes=VMEM),
        cost_estimate=pl.CostEstimate(flops=1, bytes_accessed=1, transcendentals=0),
    )(*args)


def shape(dims, dtype):
    return pltpu.HBM(dims, dtype)


def near_shape(dims, dtype):
    return pltpu.VMEM(dims, dtype)


def dot(a, b):
    return jnp.dot(a, b, preferred_element_type=F32)


def dot_t(a, b):
    return lax.dot_general(a, b, (((1,), (1,)), ((), ())), preferred_element_type=F32)


def t_dot(a, b):
    return lax.dot_general(a, b, (((0,), (0,)), ((), ())), preferred_element_type=F32)


def exact_dot(a, b):
    return jnp.dot(a, b, precision=lax.Precision.HIGHEST, preferred_element_type=F32)


def mean_scale(value):
    return lax.rsqrt(jnp.mean(value * value, axis=-1, keepdims=True) + EPS)


def triangle(strict, upper):
    row = lax.broadcasted_iota(jnp.int32, (ROWS, ROWS), 0)
    col = lax.broadcasted_iota(jnp.int32, (ROWS, ROWS), 1)
    if upper:
        row, col = col, row
    return row > col if strict else row >= col


def swish_slope(value, sigma):
    return sigma * (1.0 + value * (1.0 - sigma))


def column(ref):
    return jnp.transpose(ref[...].astype(F32))


def row_sums(value):
    return jnp.sum(jnp.transpose(value), axis=0, keepdims=True)


def lane_blocks(value):
    total = value[:, :128]
    for j in range(128, value.shape[1], 128):
        total = total + value[:, j : j + 128]
    return total


def prepare_kernel(z_ref, w_ref, gain_ref, out_w_ref, out_gain_ref, sent_ref, out_ref):
    start = z_ref[0] * COLS
    gain = column(gain_ref)
    for to, j in enumerate((1, 2, 0, 3)):
        cols = pl.ds(pl.multiple_of(j * D + start, 128), COLS)
        block = (w_ref[:, cols].astype(F32) * gain).astype(BF)
        for i in range(8):
            sent_ref[i, :, to * COLS : (to + 1) * COLS] = block
    out_ref[...] = (out_w_ref[...].astype(F32) * column(out_gain_ref)).astype(BF)


def selection(z, slots, units, slots_first):
    shape_ = (slots, units) if slots_first else (units, slots)
    line = (slots, 1) if slots_first else (1, slots)
    slot = lax.broadcasted_iota(jnp.int32, line, 0 if slots_first else 1)
    owner = jnp.zeros(line, jnp.int32)
    for i in range(1, slots // SLOT):
        owner = owner + (slot >= i * SLOT).astype(jnp.int32)
    place = slot - owner * SLOT
    unit = jnp.where(place < TAKEN, owner * OWNED + z * TAKEN + place, -1)
    return jnp.where(lax.broadcasted_iota(jnp.int32, shape_, 1 if slots_first else 0) == unit, 1.0, 0.0).astype(BF)


def prepare_feed_kernel(z_ref, up_ref, gain_ref, down_ref, out_ref):
    gain = column(gain_ref)
    chosen = selection(z_ref[0], SLOTS, UNITS, False)
    for i in range(4):
        picked = dot(up_ref[:, i * UNITS : (i + 1) * UNITS], chosen)
        out_ref[:64, i * SLOTS : (i + 1) * SLOTS] = (picked * gain).astype(BF)
    rows = dot(selection(z_ref[0], SLOT, OWNED, True), down_ref[...]).astype(BF)
    out_ref[64:, :D] = rows[:32]
    out_ref[64:80, D:] = rows[32:, :512]
    out_ref[80:, D:] = rows[32:, 512:]


def gated(pre, floor):
    sigma = lax.logistic(pre)
    return sigma, floor + (1.0 - floor) * sigma


def swish(value):
    return value * lax.logistic(value)


def head_cols(h):
    return slice(h * HEAD_DIM, (h + 1) * HEAD_DIM)


def part_rows(b):
    return slice(b * ROWS, (b + 1) * ROWS)


def first_kernel(core_ref, x0, x1, x2, x3, mine_ref, other_ref, floor_ref,
                 x_ref, w_ref, w_qg_ref, pre_ref, cum_ref, state_ref, total_ref):
    core = core_ref[0]
    for ref, lanes in ((w_ref, slice(0, WIDE)), (w_qg_ref, slice(WIDE, D))):
        ref[:, pl.ds(core, 1)] = mine_ref[:, :, lanes].reshape(8, 1, 64, WIDE)
        ref[:, pl.ds(1 - core, 1)] = other_ref[:, :, lanes].reshape(8, 1, 64, WIDE)
    for b, part in enumerate((x0, x1, x2, x3)):
        value = part[...].astype(F32)
        x_ref[part_rows(b), :] = (value * mean_scale(value)).astype(BF)
    pre_ref[...] = dot(x_ref[...], w_ref[...].reshape(D, WIDE))
    ones = triangle(False, False).astype(F32)
    floor = floor_ref[...]
    for b in range(PARTS):
        rows = part_rows(b)
        _, decay = gated(pre_ref[rows, :COLS], floor)
        cum_all = exact_dot(ones, jnp.log(decay))
        cum_ref[rows, :] = cum_all
        total_all = cum_all[ROWS - 1 :, :]
        k_out = ((1.0 - decay).astype(BF).astype(F32) * jnp.exp(total_all - cum_all)).astype(BF)
        for h in range(LOCAL_HEADS):
            value = pre_ref[rows, COLS + h * HEAD_DIM : COLS + (h + 1) * HEAD_DIM].astype(BF)
            s = h * PARTS + b
            state_ref[s] = t_dot(k_out[:, head_cols(h)], value).astype(BF)
            total_ref[s : s + 1, :] = total_all[:, head_cols(h)]


def second_kernel(x_ref, w_ref, fv_ref, cum_ref, floor_ref, pre_ref, q_ref, local_ref):
    pre_ref[...] = dot(x_ref[...], w_ref[...].reshape(D, WIDE))
    causal = triangle(False, False)
    floor = floor_ref[...]
    for b in range(PARTS):
        rows = part_rows(b)
        _, decay = gated(fv_ref[rows, :COLS], floor)
        cum = cum_ref[rows, :]
        k_in = ((1.0 - decay).astype(BF).astype(F32) * jnp.exp(-cum)).astype(BF)
        q_in = (swish(pre_ref[rows, :COLS]).astype(BF).astype(F32) * jnp.exp(cum)).astype(BF)
        q_ref[rows, :] = q_in
        value = fv_ref[rows, COLS:].astype(BF)
        for h in range(LOCAL_HEADS):
            cols = head_cols(h)
            scores = jnp.where(causal, dot_t(q_in[:, cols], k_in[:, cols]), 0.0).astype(BF)
            local_ref[rows, cols] = dot(scores, value[:, cols])


def split3(value):
    first = value.astype(BF).astype(F32)
    second = (value - first).astype(BF).astype(F32)
    return first, second, value - first - second


def chip_kernel(core_ref, mine_ref, other_ref, my_total_ref, other_total_ref, out_ref, *, backward):
    core = core_ref[0]
    second = core == (0 if backward else 1)
    base = core * HALF
    my_total = my_total_ref[pl.ds(base, HALF), :]
    other_total = other_total_ref[pl.ds(base, HALF), :]
    last_decay = jnp.exp(jnp.where(second, my_total, other_total))
    for i in range(HALF):
        mine = mine_ref[base + i].astype(F32)
        other = other_ref[base + i].astype(F32)
        last = jnp.where(second, mine, other)
        first = jnp.where(second, other, mine)
        state = (jnp.transpose(last_decay[i : i + 1, :]) * first + last).astype(BF)
        for d in range(8):
            out_ref[d, i * HEAD_DIM : (i + 1) * HEAD_DIM, :] = state
    if not backward:
        pieces = split3(my_total + other_total)
        tail = jnp.concatenate([*pieces, jnp.zeros((HALF, HEAD_DIM), F32)], axis=0).astype(BF)
        for d in range(8):
            out_ref[d, HALF * HEAD_DIM :, :] = tail


def carry_kernel(place_ref, all_ref, *refs, backward):
    place = place_ref[0]
    if backward:
        totals_ref, out_ref = refs
    else:
        out_ref, totals_ref = refs
        for j in range(8):
            tail = all_ref[j, HALF * HEAD_DIM :, :].astype(F32)
            totals_ref[j] = (tail[:HALF] + tail[HALF : 2 * HALF]) + tail[2 * HALF : 3 * HALF]
    for i in range(HALF):
        carried = jnp.zeros((HEAD_DIM, HEAD_DIM), F32)
        decays = jnp.transpose(jnp.exp(jnp.concatenate([totals_ref[j, i : i + 1, :] for j in range(8)], axis=0)))
        for step in range(7):
            j = 7 - step if backward else step
            reached = j > place if backward else j < place
            block = all_ref[j, i * HEAD_DIM : (i + 1) * HEAD_DIM, :].astype(F32)
            carried = jnp.where(reached, decays[:, j : j + 1] * carried + block, carried)
        out_ref[i] = carried.astype(BF)


def enter_state(core, own_half, other_half, other_end, other_total, s, backward):
    h, b = divmod(s, PARTS)
    chip = jnp.where(core == h, own_half[b], other_half[b]).astype(F32)
    later = core == (0 if backward else 1)
    passed = jnp.transpose(jnp.exp(other_total[s : s + 1, :])) * chip + other_end[s].astype(F32)
    return jnp.where(later, passed, chip)


def mix_kernel(core_ref, pre_ref, q_ref, local_ref, own_half, other_half, other_end, other_total, w_ref,
               out_ref, normed_ref, entered_ref, p0, p1, p2, p3):
    core = core_ref[0]
    for b in range(PARTS):
        rows = part_rows(b)
        for h in range(LOCAL_HEADS):
            cols = head_cols(h)
            s = h * PARTS + b
            state = enter_state(core, own_half, other_half, other_end, other_total, s, False).astype(BF)
            entered_ref[s] = state
            mixed = local_ref[rows, cols] + dot(q_ref[rows, cols], state)
            out_ref[rows, cols] = mixed
            gate = pre_ref[rows, COLS + h * HEAD_DIM : COLS + (h + 1) * HEAD_DIM]
            normed_ref[rows, cols] = (mixed * mean_scale(mixed) * swish(gate)).astype(BF)
    product = dot(normed_ref[...], w_ref[...]).astype(BF)
    for b, part in enumerate((p0, p1, p2, p3)):
        part[...] = product[part_rows(b), :]


def sum_parts(p0, p1, p2, p3):
    return (p0[...].astype(F32) + p1[...].astype(F32)) + (p2[...].astype(F32) + p3[...].astype(F32))


def middle_kernel(hidden_ref, p0, p1, p2, p3, middle_ref, normed_ref):
    middle = hidden_ref[...].astype(F32) + sum_parts(p0, p1, p2, p3)
    middle_ref[...] = middle
    normed_ref[...] = (middle * mean_scale(middle)).astype(BF)


def feed_inputs(parts, grads, w_ref, x_ref, g_ref, down_ref):
    for s in range(16):
        at = s * SLOT
        rows = w_ref[s, w_ref.shape[1] - 32 :, :]
        down_ref[at : at + 32, :] = rows[:, :D]
        down_ref[at + 32 : at + 48, :512] = rows[:16, D:]
        down_ref[at + 32 : at + 48, 512:] = rows[16:, D:]
    for b in range(PARTS):
        x_ref[part_rows(b), :] = parts[b][...]
        g_ref[part_rows(b), :] = grads[b][...]


def feed_kernel(x0, x1, x2, x3, g0, g1, g2, g3, w_ref, act_ref, grad_ref, p0, p1, p2, p3, x_ref, g_ref, down_ref):
    feed_inputs((x0, x1, x2, x3), (g0, g1, g2, g3), w_ref, x_ref, g_ref, down_ref)
    for j in range(3):
        lanes = slice(j * COLS, (j + 1) * COLS)
        ups = slice(PAD + j * COLS, PAD + (j + 1) * COLS)
        gate = dot(x_ref[...], w_ref[:, :64, lanes].reshape(D, COLS))
        up = dot(x_ref[...], w_ref[:, :64, ups].reshape(D, COLS))
        grad = dot_t(g_ref[...], down_ref[lanes, :])
        sigma = lax.logistic(gate)
        active = gate * sigma
        act_ref[:, lanes] = (active * up).astype(BF)
        grad_ref[:, lanes] = (grad * up * swish_slope(gate, sigma)).astype(BF)
        grad_ref[:, ups] = (grad * active).astype(BF)
    product = dot_t(grad_ref[...], w_ref[:, :64, :].reshape(D, 2 * PAD)).astype(BF)
    for b, part in enumerate((p0, p1, p2, p3)):
        part[...] = product[part_rows(b), :]


def feed_grad_kernel(x0, x1, x2, x3, g0, g1, g2, g3, w_ref, grad_ref, act_ref, out_ref, p0, p1, p2, p3,
                     x_ref, g_ref, down_ref):
    feed_inputs((x0, x1, x2, x3), (g0, g1, g2, g3), w_ref, x_ref, g_ref, down_ref)
    product = dot(act_ref[...], down_ref[...]).astype(BF)
    for b, part in enumerate((p0, p1, p2, p3)):
        part[...] = product[part_rows(b), :]
    for j in range(0, 2 * PAD, 512):
        out_ref[:, :64, j : j + 512] = t_dot(x_ref[...], grad_ref[:, j : j + 512]).astype(BF).reshape(16, 64, 512)
    rows = t_dot(act_ref[...], g_ref[...]).astype(BF)
    for s in range(16):
        at = s * SLOT
        out_ref[s, 64:, :D] = rows[at : at + 32]
        out_ref[s, 64:80, D:] = rows[at + 32 : at + 48, :512]
        out_ref[s, 80:, D:] = rows[at + 32 : at + 48, 512:]


def add_kernel(a_ref, b_ref, out_ref):
    out_ref[...] = (a_ref[...].astype(F32) + b_ref[...].astype(F32)).astype(BF)


def result_kernel(middle_ref, p0, p1, p2, p3, out_ref):
    out_ref[...] = (middle_ref[...] + sum_parts(p0, p1, p2, p3)).astype(BF)


def norm_back(value_ref, base_ref, u):
    value = value_ref[...].astype(F32)
    scale = mean_scale(value)
    centered = value * scale
    back = scale * (u - centered * jnp.mean(u * centered, axis=-1, keepdims=True))
    return base_ref[...].astype(F32) + back


def branch_kernel(value_ref, base_ref, p0, p1, p2, p3, out_ref, low_ref):
    total = norm_back(value_ref, base_ref, sum_parts(p0, p1, p2, p3))
    out_ref[...] = total
    low_ref[...] = total.astype(BF)


def last_kernel(value_ref, base_ref, p0, p1, p2, p3, low_ref):
    low_ref[...] = norm_back(value_ref, base_ref, sum_parts(p0, p1, p2, p3)).astype(BF)


def head_back_kernel(b0, b1, b2, b3, w_ref, pre_ref, q_ref, mixed_ref, branch_ref, gate_ref, out_grad_ref, state_ref):
    for b, part in enumerate((b0, b1, b2, b3)):
        branch_ref[part_rows(b), :] = part[...]
    grads = dot_t(branch_ref[...], w_ref[...])
    for b in range(PARTS):
        rows = part_rows(b)
        for h in range(LOCAL_HEADS):
            cols = head_cols(h)
            grad = grads[rows, cols]
            mixed = mixed_ref[rows, cols]
            scale = mean_scale(mixed)
            normed = mixed * scale
            gate = pre_ref[rows, COLS + h * HEAD_DIM : COLS + (h + 1) * HEAD_DIM]
            sigma = lax.logistic(gate)
            gate_ref[rows, cols] = (grad * normed * swish_slope(gate, sigma)).astype(BF)
            c = grad * (gate * sigma)
            mixer = (scale * (c - normed * jnp.mean(c * normed, axis=-1, keepdims=True))).astype(BF)
            out_grad_ref[rows, cols] = mixer
            state_ref[h * PARTS + b] = t_dot(q_ref[rows, cols], mixer).astype(BF)


def near_back_kernel(core_ref, x_ref, normed_ref, branch_ref, qg_ref, fv_ref, cum_ref, floor_ref, q_ref, gate_ref,
                     out_grad_ref, entered_ref, grad_ref, log_ref, key_ref, value_ref,
                     mine_ref, other_ref, my_rows_ref, other_rows_ref, all_ref, rows_ref):
    causal = triangle(False, False)
    suffix = triangle(False, True).astype(F32)
    floor = floor_ref[...]
    for b in range(PARTS):
        rows = part_rows(b)
        _, decay = gated(fv_ref[rows, :COLS], floor)
        cum = cum_ref[rows, :]
        grow_all = jnp.exp(cum)
        shrink_all = jnp.exp(-cum)
        k_all = ((1.0 - decay).astype(BF).astype(F32) * shrink_all).astype(BF)
        q_pre = qg_ref[rows, :COLS]
        slope_all = swish_slope(q_pre, lax.logistic(q_pre))
        for h in range(LOCAL_HEADS):
            cols = head_cols(h)
            value = fv_ref[rows, COLS + h * HEAD_DIM : COLS + (h + 1) * HEAD_DIM].astype(BF)
            q_in, k_in = q_ref[rows, cols], k_all[:, cols]
            out_grad = out_grad_ref[rows, cols]
            scores = jnp.where(causal, dot_t(q_in, k_in), 0.0).astype(BF)
            grad_scores = jnp.where(causal, dot_t(out_grad, value), 0.0).astype(BF)
            inner = dot(grad_scores, k_in) + dot_t(out_grad, entered_ref[h * PARTS + b])
            back = t_dot(grad_scores, q_in)
            near = q_in.astype(F32) * inner - k_in.astype(F32) * back
            log_ref[rows, cols] = exact_dot(suffix, near)
            key_ref[rows, cols] = back * shrink_all[:, cols]
            value_ref[rows, cols] = t_dot(scores, out_grad)
            grad_ref[rows, cols] = (inner * grow_all[:, cols] * slope_all[:, cols]).astype(BF)
    grad_ref[:, COLS:] = gate_ref[...]
    column_grad(core_ref[0], x_ref, grad_ref, mine_ref, other_ref, all_ref)
    row_grad(core_ref[0], normed_ref, branch_ref, my_rows_ref, other_rows_ref, rows_ref)


def far_back_kernel(core_ref, fv_ref, cum_ref, floor_ref, log_ref, key_ref, value_ref, entered_ref, own_half, other_half,
                    other_end, other_total, qg_ref, w_fv_ref, w_qg_ref, x_ref,
                    floor_grad_ref, mine_ref, other_ref, p0, p1, p2, p3, grad_ref, all_ref):
    core = core_ref[0]
    before = triangle(True, False).astype(F32)
    floor = floor_ref[...]
    floor_sum = jnp.zeros((1, COLS), F32)
    for b in range(PARTS):
        rows = part_rows(b)
        sigma, decay = gated(fv_ref[rows, :COLS], floor)
        cum = cum_ref[rows, :]
        total = cum[ROWS - 1 :, :]
        to_end = jnp.exp(total - cum)
        k_all = ((1.0 - decay).astype(BF).astype(F32) * to_end).astype(BF)
        aheads, edges = [], []
        for h in range(LOCAL_HEADS):
            cols = head_cols(h)
            s = h * PARTS + b
            following = enter_state(core, own_half, other_half, other_end, other_total, s, True)
            low = following.astype(BF)
            value = fv_ref[rows, COLS + h * HEAD_DIM : COLS + (h + 1) * HEAD_DIM].astype(BF)
            aheads.append(dot_t(value, low))
            edges.append(jnp.transpose(jnp.sum(following * entered_ref[s].astype(F32), axis=1, keepdims=True)))
            grad_value = value_ref[rows, cols] + dot(k_all[:, cols], low)
            grad_ref[rows, COLS + h * HEAD_DIM : COLS + (h + 1) * HEAD_DIM] = grad_value.astype(BF)
        ahead = jnp.concatenate(aheads, axis=1)
        edge = jnp.concatenate(edges, axis=1)
        far = exact_dot(before, k_all.astype(F32) * ahead)
        grad_log = log_ref[rows, :] + far + jnp.exp(total) * edge
        grad_decay = grad_log / decay - (key_ref[rows, :] + ahead * to_end)
        floor_sum = floor_sum + jnp.sum(grad_decay * (1.0 - sigma), axis=0, keepdims=True)
        grad_ref[rows, :COLS] = (grad_decay * (1.0 - floor) * sigma * (1.0 - sigma)).astype(BF)
    floor_grad_ref[...] = floor_sum
    column_grad(core, x_ref, grad_ref, mine_ref, other_ref, all_ref)
    product = dot_t(grad_ref[...], w_fv_ref[...].reshape(D, WIDE)) + dot_t(qg_ref[...], w_qg_ref[...].reshape(D, WIDE))
    product = product.astype(BF)
    for b, part in enumerate((p0, p1, p2, p3)):
        part[...] = product[part_rows(b), :]


def column_grad(core, a_ref, g_ref, mine_ref, other_ref, all_ref):
    n = g_ref.shape[1]
    all_ref[...] = t_dot(a_ref[...], g_ref[...]).astype(BF).reshape(8, 2, 64, n)
    mine_ref[...] = all_ref[:, pl.ds(core, 1)].reshape(8, 64, n)
    other_ref[...] = all_ref[:, pl.ds(1 - core, 1)].reshape(8, 64, n)


def row_grad(core, a_ref, g_ref, mine_ref, other_ref, all_ref):
    rows = mine_ref.shape[1]
    all_ref[...] = t_dot(a_ref[...], g_ref[...]).astype(BF).reshape(2, 2, rows, D)
    mine_ref[...] = all_ref[:, pl.ds(core, 1)].reshape(2, rows, D)
    other_ref[...] = all_ref[:, pl.ds(1 - core, 1)].reshape(2, rows, D)


def pack_columns(mine_ref, other_ref, out_ref, start):
    lanes = mine_ref.shape[2] // 2
    for i in range(8):
        value = (mine_ref[i].astype(F32) + other_ref[i].astype(F32)).astype(BF)
        for half in range(2):
            for j in range(lanes // 128):
                at = half * lanes + j * 128
                out_ref[i * 2 + half, start + j * 64 : start + (j + 1) * 64, :] = value[:, at : at + 128]


def pack_rows(mine_ref, other_ref, out_ref, start):
    for yl in range(2):
        value = (mine_ref[yl].astype(F32) + other_ref[yl].astype(F32)).astype(BF)
        for p in range(8):
            at = start + p % 2 * 64
            for yh in range(2):
                out_ref[p // 2 * 4 + yl * 2 + yh, at : at + 64, :] = value[:, p * 128 : (p + 1) * 128]


def rider_rows(value):
    rows = [piece[:, cols] for piece in split3(value) for cols in (slice(0, 128), slice(128, 256))]
    return jnp.concatenate([*rows, jnp.zeros((10, 128), F32)], axis=0).astype(BF)


def rider_value(rows):
    rows = rows.astype(F32)
    halves = [(rows[i : i + 1] + rows[i + 2 : i + 3]) + rows[i + 4 : i + 5] for i in range(2)]
    return jnp.concatenate(halves, axis=1)


def pack_kernel(mine_ref, other_ref, floor_ref, other_floor_ref, my_qg_ref, other_qg_ref, my_rows_ref, other_rows_ref, out_ref):
    pack_columns(mine_ref, other_ref, out_ref, 0)
    rider = rider_rows(floor_ref[...] + other_floor_ref[...])
    for i in range(16):
        out_ref[i, 128:144, :] = rider
    pack_columns(my_qg_ref, other_qg_ref, out_ref, 144)
    pack_rows(my_rows_ref, other_rows_ref, out_ref, 272)


def total_of(all_ref, rows):
    total = all_ref[0, rows, :].astype(F32)
    for i in range(1, 16):
        total = total + all_ref[i, rows, :].astype(F32)
    return total


def sum_kernel(all_ref, out_ref, rows_ref):
    first = total_of(all_ref, slice(0, 128)).astype(BF)
    floor = rider_value(all_ref[0, 128:144, :])
    for i in range(1, 16):
        floor = floor + rider_value(all_ref[i, 128:144, :])
    rider = rider_rows(floor)
    second = total_of(all_ref, slice(144, 272)).astype(BF)
    for i in range(8):
        out_ref[i, :128, :] = first
        out_ref[i, 128:144, :] = rider
        out_ref[i, 144:, :] = second
    rows_ref[...] = total_of(all_ref, slice(272, 400)).astype(BF)


def feed_grads_kernel(z_ref, s0, s1, s2, s3, w_ref, gain_ref, up_ref, gain_grad_ref, down_ref):
    chosen = jnp.concatenate([selection(z, SLOTS, UNITS, True) for z in quarters(z_ref[0])], axis=0)
    gain = column(gain_ref)
    gain_grad = jnp.zeros((64, 128), F32)
    taken = jnp.concatenate(
        [
            jnp.concatenate([ref[:64, i * SLOTS : (i + 1) * SLOTS] for ref in (s0, s1, s2, s3)], axis=1)
            for i in range(4)
        ],
        axis=0,
    )
    values = dot(taken, chosen)
    for i in range(4):
        value = values[i * 64 : (i + 1) * 64]
        cols = slice(i * UNITS, (i + 1) * UNITS)
        up_ref[:, cols] = value * gain
        gain_grad = gain_grad + lane_blocks(value * w_ref[:, cols].astype(F32))
    gain_grad_ref[...] = row_sums(gain_grad)
    down = jnp.zeros((OWNED, D), F32)
    for z, ref in zip(quarters(z_ref[0]), (s0, s1, s2, s3)):
        last = jnp.concatenate([ref[64:80, D:], ref[80:, D:]], axis=1)
        rows = jnp.concatenate([ref[64:, :D], last], axis=0)
        down = down + dot(selection(z, SLOT, OWNED, False), rows)
    down_ref[...] = down


def mix_grads_kernel(z_ref, all_ref, o0, o1, o2, o3, w_ref, gain_ref, out_w_ref, out_gain_ref,
                     mix_ref, gain_grad_ref, out_ref, out_gain_grad_ref, floor_ref):
    gain, out_gain = column(gain_ref), column(out_gain_ref)
    gain_grad = jnp.zeros((64, 128), F32)
    out_gain_grad = jnp.zeros((64, 128), F32)
    for yh in range(2):
        for z in range(4):
            i = yh * 4 + z
            for start, block in ((0, 2 if yh else 1), (144, 3 if yh else 0)):
                for j in range(2):
                    value = all_ref[i, start + j * 64 : start + (j + 1) * 64, :].astype(F32)
                    at = block * D + z * COLS + j * 128
                    mix_ref[:, at : at + 128] = value * gain
                    gain_grad = gain_grad + value * w_ref[:, at : at + 128].astype(F32)
            if yh == 0:
                floor_ref[:, z * COLS : (z + 1) * COLS] = rider_value(all_ref[i, 128:144, :])
    for z, ref in zip(quarters(z_ref[0]), (o0, o1, o2, o3)):
        for k in range(2):
            cols = pl.ds(pl.multiple_of((z * 2 + k) * 128, 128), 128)
            value = ref[k * 64 : (k + 1) * 64, :].astype(F32)
            out_ref[:, cols] = value * out_gain
            out_gain_grad = out_gain_grad + value * out_w_ref[:, cols].astype(F32)
    gain_grad_ref[...] = row_sums(gain_grad)
    out_gain_grad_ref[...] = row_sums(out_gain_grad)


def scalar(value):
    return value.reshape(1).astype(jnp.int32)


def body(hidden, mixer_weight, output_weight, gate_up_weight, down_weight, mixer_gain, group_gain, feed_gain,
         forget_floor, out_grad):
    z = lax.axis_index("z")
    z_of = scalar(z)
    core = scalar(lax.axis_index("c"))
    place = scalar(lax.axis_index("x") * 2 + lax.axis_index("yl"))
    gain_one, gain_group, gain_two = (g.reshape(1, 64) for g in (mixer_gain, group_gain, feed_gain))
    floor = lax.dynamic_index_in_dim(forget_floor.reshape(PARTS, COLS), z, 0)
    own = [near_shape((ROWS, D), BF)] * 4
    state_dims = (STATES, HEAD_DIM, HEAD_DIM)
    half_dims = (HALF, HEAD_DIM, HEAD_DIM)

    w_sent, out_own = kernel_call(
        prepare_kernel, (shape((8, 64, D), BF), shape((64, D), BF)),
        z_of, mixer_weight, gain_one, output_weight, gain_group,
    )
    tokens = gather_z(hidden)
    w_mine = exchange(w_sent, ("x", "yl"))
    w_out = lax.all_gather(out_own, ("x", "yl", "c"))
    w_other = shift(after(w_mine, *tokens), "c", 1)
    x_all, w_fv, w_qg, pre_fv, cum, end, total = kernel_call(
        first_kernel,
        (
            shape((TOKENS, D), BF),
            shape((8, 2, 64, WIDE), BF),
            shape((8, 2, 64, WIDE), BF),
            shape((TOKENS, WIDE), F32),
            shape((TOKENS, COLS), F32),
            near_shape(state_dims, BF),
            shape((STATES, HEAD_DIM), F32),
        ),
        core, *tokens, w_mine, w_other, floor,
        flops=2 * TOKENS * D * WIDE,
        near=(5, 6),
    )

    def chip_state(end_state, other_total, backward, order=()):
        other_end = shift(end_state, "c", 1)
        sent = kernel_call(
            functools.partial(chip_kernel, backward=backward),
            shape((8, HALF * HEAD_DIM + (0 if backward else TAIL), HEAD_DIM), BF),
            core, end_state, other_end, total, other_total,
            order=order,
            near=(1, 2),
        )
        return sent, other_end

    other_total = shift(total, "c", 1)
    sent, other_end = chip_state(end, other_total, False)
    arrived = exchange(sent, ("x", "yl"))
    grads_out = gather_z(after(out_grad, sent))
    pre_qg, q_in, local_out = kernel_call(
        second_kernel,
        (shape((TOKENS, WIDE), F32), shape((TOKENS, COLS), BF), shape((TOKENS, COLS), F32)),
        x_all, w_qg, pre_fv, cum, floor,
        flops=2 * TOKENS * D * WIDE,
        order=(sent,),
    )
    w_out = lax.dynamic_index_in_dim(w_out.reshape(PARTS, COLS, D), z, 0, keepdims=False)
    feed_own_weights = kernel_call(
        prepare_feed_kernel, shape((FEED_ROWS, 2 * PAD), BF), z_of, gate_up_weight, gain_two, down_weight,
        order=(q_in, w_out),
    )
    w_feed = lax.all_gather(after(feed_own_weights, arrived, *grads_out), ("x", "yl", "c"))
    own_half, totals = kernel_call(
        functools.partial(carry_kernel, backward=False),
        (near_shape(half_dims, BF), shape((8, HALF, HEAD_DIM), F32)),
        place, arrived,
        order=(feed_own_weights, w_out, *grads_out),
        near=(1,),
    )
    mixed, normed_out, entered, *parts = kernel_call(
        mix_kernel,
        (shape((TOKENS, COLS), F32), shape((TOKENS, COLS), BF), shape(state_dims, BF), *own),
        core, pre_qg, q_in, local_out, own_half, shift(own_half, "c", 1), other_end, other_total, w_out,
        flops=2 * TOKENS * COLS * D,
        near=(4, 5),
    )
    middle, feed_own = kernel_call(
        middle_kernel, (shape((ROWS, D), F32), near_shape((ROWS, D), BF)), hidden, *scatter_z(parts),
        near=(1, 2, 3, 4),
    )
    feed_in = (*gather_z(feed_own), *grads_out, w_feed)
    feed_scratch = [pltpu.VMEM((TOKENS, D), BF), pltpu.VMEM((TOKENS, D), BF), pltpu.VMEM((PAD, D), BF)]
    act, grad_up, *parts = kernel_call(
        feed_kernel,
        (shape((TOKENS, PAD), BF), shape((TOKENS, 2 * PAD), BF), *own),
        *feed_in,
        scratch=feed_scratch,
        flops=2 * TOKENS * D * PAD * 5,
    )
    feed_back = scatter_z(parts)
    feed_grad, *down_parts = kernel_call(
        feed_grad_kernel,
        (shape((16, FEED_ROWS, 2 * PAD), BF), *[shape((ROWS, D), BF)] * 4),
        *feed_in, grad_up, act,
        scratch=feed_scratch,
        flops=2 * TOKENS * D * PAD * 3,
        order=(parts[3],),
    )
    grad_middle, branch_own = kernel_call(
        branch_kernel, (shape((ROWS, D), F32), near_shape((ROWS, D), BF)), middle, out_grad, *feed_back,
        order=(feed_grad,),
        near=(2, 3, 4, 5),
    )
    feed_sum = lax.psum_scatter(after(feed_grad, *feed_back), ("x", "yl", "c"), scatter_dimension=0)
    branch = gather_z(branch_own)
    branch_all, grad_gate, grad_mixed, end_grad = kernel_call(
        head_back_kernel,
        (
            shape((TOKENS, D), BF),
            shape((TOKENS, COLS), BF),
            shape((TOKENS, COLS), BF),
            near_shape(state_dims, BF),
        ),
        *branch, w_out, pre_qg, q_in, mixed,
        flops=2 * TOKENS * COLS * D,
        near=(0, 1, 2, 3),
    )

    sent, other_end = chip_state(end_grad, other_total, True)
    down_parts = scatter_z(after(down_parts, sent))
    arrived = exchange(sent, ("x", "yl"))
    grad_qg, near_log, near_key, near_value, qg_mine, qg_other, out_mine, out_other = kernel_call(
        near_back_kernel,
        (
            shape((TOKENS, WIDE), BF),
            *[shape((TOKENS, COLS), F32)] * 3,
            *[shape((8, 64, WIDE), BF)] * 2,
            *[shape((2, 64, D), BF)] * 2,
        ),
        core, x_all, normed_out, branch_all, pre_qg, pre_fv, cum, floor, q_in, grad_gate, grad_mixed, entered,
        scratch=[pltpu.VMEM((8, 2, 64, WIDE), BF), pltpu.VMEM((2, 2, 64, D), BF)],
        flops=2 * TOKENS * (HEAD_DIM * HEAD_DIM * 12 + D * WIDE),
        order=(sent,),
    )
    own_half = kernel_call(
        functools.partial(carry_kernel, backward=True), near_shape(half_dims, BF), place, arrived, totals,
        order=(grad_qg, *down_parts),
        near=(1,),
    )
    qg_other, out_other = after((qg_other, out_other), own_half)
    floor_part, fv_mine, fv_other, *parts = kernel_call(
        far_back_kernel,
        (near_shape((1, COLS), F32), *[near_shape((8, 64, WIDE), BF)] * 2, *[shape((ROWS, D), BF)] * 4),
        core, pre_fv, cum, floor, near_log, near_key, near_value, entered, own_half, shift(own_half, "c", 1), other_end,
        other_total, grad_qg, w_fv, w_qg, x_all,
        scratch=[pltpu.VMEM((TOKENS, WIDE), BF), pltpu.VMEM((8, 2, 64, WIDE), BF)],
        flops=2 * TOKENS * D * D * 2,
        near=(8, 9),
    )
    sent = kernel_call(
        pack_kernel, shape((16, 400, 128), BF), fv_mine, shift(fv_other, "c", 1), floor_part,
        shift(floor_part, "c", 1), qg_mine, shift(qg_other, "c", 1), out_mine, shift(out_other, "c", 1),
        near=(0, 1, 2, 3, 5, 7),
    )

    arrived = exchange(sent, ("x", "yl", "yh"))
    parts = scatter_z(after(parts, sent))
    feed_other = shift(after(feed_sum, *parts), "yh", 1)
    result = kernel_call(result_kernel, shape((ROWS, D), BF), middle, *down_parts, order=(sent,))
    grad_tokens = kernel_call(last_kernel, shape((ROWS, D), BF), hidden, grad_middle, *parts, order=(result,))
    copies, rows = kernel_call(
        sum_kernel, (shape((8, 272, 128), BF), shape((128, 128), BF)), arrived, order=(feed_other, grad_tokens), near=(0,)
    )
    last_sums = exchange(copies, ("yh", "z"))
    out_sums = gather_z(transpose_xz(rows))
    feed_total = kernel_call(
        add_kernel, shape((FEED_ROWS, 2 * PAD), BF), feed_sum, feed_other, order=(copies,)
    )
    feed_totals = gather_z(feed_total)
    up_grad, feed_gain_grad, down_grad = kernel_call(
        feed_grads_kernel,
        (shape((64, 2 * FF), F32), shape((1, 64), F32), shape((OWNED, D), F32)),
        z_of, *feed_totals, gate_up_weight, gain_two,
        order=(copies,),
    )
    mix_grad, gain_grad, out_weight_grad, group_gain_grad, floor_grad = kernel_call(
        mix_grads_kernel,
        (
            shape((64, 4 * D), F32),
            shape((1, 64), F32),
            shape((64, D), F32),
            shape((1, 64), F32),
            shape((1, D), F32),
        ),
        z_of, last_sums, *out_sums, mixer_weight, gain_one, output_weight, gain_group,
        order=(up_grad,),
        near=(1,),
    )
    return (
        result,
        grad_tokens,
        mix_grad,
        out_weight_grad,
        up_grad,
        down_grad,
        gain_grad.reshape(64),
        group_gain_grad.reshape(64),
        feed_gain_grad.reshape(64),
        floor_grad.reshape(D),
    )


def solution(mesh):
    cut = Mesh(mesh.devices.reshape(2, 4, 4, 2, 2), AXES)
    seq = ("x", "yl", "c")
    rows, weight, vector = P(AXES, None), P(seq, None), P(seq)
    in_specs = (rows, weight, weight, weight, weight, vector, vector, vector, P(), rows)
    out_specs = (rows, rows, weight, weight, weight, weight, vector, vector, vector, P())
    return jax.shard_map(body, mesh=cut, in_specs=in_specs, out_specs=out_specs, check_vma=False)
```

```python
import functools

import jax
import jax.numpy as jnp
from jax import lax
from jax.experimental import pallas as pl
from jax.experimental.pallas import tpu as pltpu
from jax.sharding import Mesh, PartitionSpec as P

D = 1024
HEADS = 8
HEAD_DIM = 128
FF = 2816
EPS = 1e-06

ROWS = 128
PARTS = 4
COLS = D // PARTS
TOKENS = PARTS * ROWS
WIDE = 2 * COLS
PAD = 768
SLOT, TAKEN, OWNED = 48, 44, 176
SLOTS, UNITS = 8 * SLOT, 8 * OWNED
FEED_ROWS = 96
LOCAL_HEADS = 2
STATES = PARTS * LOCAL_HEADS
HALF = STATES // 2
TAIL = 16
BF = jnp.bfloat16
F32 = jnp.float32
AXES = ("yh", "z", "x", "yl", "c")
VMEM = 40 * 1024 * 1024


def shift(value, axis, by):
    n = lax.axis_size(axis)
    return lax.ppermute(value, axis, [(i, (i + by) % n) for i in range(n)])


def gather_z(own):
    return (own, shift(own, "z", 1), shift(own, "z", -1), shift(own, "z", 2))


def scatter_z(parts):
    return (parts[0], shift(parts[1], "z", -1), shift(parts[2], "z", 1), shift(parts[3], "z", 2))


def transpose_xz(value):
    pairs = [(z * 4 + x, x * 4 + z) for z in range(4) for x in range(4)]
    return lax.ppermute(value, ("z", "x"), pairs)


def quarters(z):
    return [lax.rem(z + by, 4) for by in (0, 3, 1, 2)]


def exchange(value, axes):
    return lax.all_to_all(value, axes, 0, 0)


def after(value, *others):
    return lax.optimization_barrier((value, *others))[0]


def kernel_call(body, out_shape, *args, scratch=(), flops=0, order=(), near=()):
    if order:
        args = after(args, *order)
    args = [
        a if a.dtype == jnp.int32 else pltpu.with_memory_space_constraint(a, pltpu.VMEM if i in near else pltpu.HBM)
        for i, a in enumerate(args)
    ]
    in_specs = [
        pl.BlockSpec(memory_space=pltpu.SMEM) if a.dtype == jnp.int32 else pl.BlockSpec(memory_space=pltpu.VMEM)
        for a in args
    ]
    out_specs = jax.tree.map(lambda _: pl.BlockSpec(memory_space=pltpu.VMEM), out_shape)
    return pl.pallas_call(
        body,
        out_shape=out_shape,
        in_specs=in_specs,
        out_specs=out_specs,
        scratch_shapes=list(scratch),
        compiler_params=pltpu.CompilerParams(vmem_limit_bytes=VMEM),
        cost_estimate=pl.CostEstimate(flops=1, bytes_accessed=1, transcendentals=0),
    )(*args)


def shape(dims, dtype):
    return pltpu.HBM(dims, dtype)


def near_shape(dims, dtype):
    return pltpu.VMEM(dims, dtype)


def dot(a, b):
    return jnp.dot(a, b, preferred_element_type=F32)


def dot_t(a, b):
    return lax.dot_general(a, b, (((1,), (1,)), ((), ())), preferred_element_type=F32)


def t_dot(a, b):
    return lax.dot_general(a, b, (((0,), (0,)), ((), ())), preferred_element_type=F32)


def exact_dot(a, b):
    return jnp.dot(a, b, precision=lax.Precision.HIGHEST, preferred_element_type=F32)


def mean_scale(value):
    return lax.rsqrt(jnp.mean(value * value, axis=-1, keepdims=True) + EPS)


def triangle(strict, upper):
    row = lax.broadcasted_iota(jnp.int32, (ROWS, ROWS), 0)
    col = lax.broadcasted_iota(jnp.int32, (ROWS, ROWS), 1)
    if upper:
        row, col = col, row
    return row > col if strict else row >= col


def swish_slope(value, sigma):
    return sigma * (1.0 + value * (1.0 - sigma))


def column(ref):
    return jnp.transpose(ref[...].astype(F32))


def row_sums(value):
    return jnp.sum(jnp.transpose(value), axis=0, keepdims=True)


def lane_blocks(value):
    total = value[:, :128]
    for j in range(128, value.shape[1], 128):
        total = total + value[:, j : j + 128]
    return total


def prepare_kernel(z_ref, w_ref, gain_ref, out_w_ref, out_gain_ref, sent_ref, out_ref):
    start = z_ref[0] * COLS
    gain = column(gain_ref)
    for to, j in enumerate((1, 2, 0, 3)):
        cols = pl.ds(pl.multiple_of(j * D + start, 128), COLS)
        block = (w_ref[:, cols].astype(F32) * gain).astype(BF)
        for i in range(8):
            sent_ref[i, :, to * COLS : (to + 1) * COLS] = block
    out_ref[...] = (out_w_ref[...].astype(F32) * column(out_gain_ref)).astype(BF)


def selection(z, slots, units, slots_first):
    shape_ = (slots, units) if slots_first else (units, slots)
    line = (slots, 1) if slots_first else (1, slots)
    slot = lax.broadcasted_iota(jnp.int32, line, 0 if slots_first else 1)
    owner = jnp.zeros(line, jnp.int32)
    for i in range(1, slots // SLOT):
        owner = owner + (slot >= i * SLOT).astype(jnp.int32)
    place = slot - owner * SLOT
    unit = jnp.where(place < TAKEN, owner * OWNED + z * TAKEN + place, -1)
    return jnp.where(lax.broadcasted_iota(jnp.int32, shape_, 1 if slots_first else 0) == unit, 1.0, 0.0).astype(BF)


def prepare_feed_kernel(z_ref, up_ref, gain_ref, down_ref, out_ref):
    gain = column(gain_ref)
    chosen = selection(z_ref[0], SLOTS, UNITS, False)
    for i in range(4):
        picked = dot(up_ref[:, i * UNITS : (i + 1) * UNITS], chosen)
        out_ref[:64, i * SLOTS : (i + 1) * SLOTS] = (picked * gain).astype(BF)
    rows = dot(selection(z_ref[0], SLOT, OWNED, True), down_ref[...]).astype(BF)
    out_ref[64:, :D] = rows[:32]
    out_ref[64:80, D:] = rows[32:, :512]
    out_ref[80:, D:] = rows[32:, 512:]


def gated(pre, floor):
    sigma = lax.logistic(pre)
    return sigma, floor + (1.0 - floor) * sigma


def swish(value):
    return value * lax.logistic(value)


def head_cols(h):
    return slice(h * HEAD_DIM, (h + 1) * HEAD_DIM)


def part_rows(b):
    return slice(b * ROWS, (b + 1) * ROWS)


def first_kernel(core_ref, x0, x1, x2, x3, mine_ref, other_ref, floor_ref,
                 x_ref, w_ref, w_qg_ref, pre_ref, cum_ref, state_ref, total_ref):
    core = core_ref[0]
    for ref, lanes in ((w_ref, slice(0, WIDE)), (w_qg_ref, slice(WIDE, D))):
        ref[:, pl.ds(core, 1)] = mine_ref[:, :, lanes].reshape(8, 1, 64, WIDE)
        ref[:, pl.ds(1 - core, 1)] = other_ref[:, :, lanes].reshape(8, 1, 64, WIDE)
    for b, part in enumerate((x0, x1, x2, x3)):
        value = part[...].astype(F32)
        x_ref[part_rows(b), :] = (value * mean_scale(value)).astype(BF)
    pre_ref[...] = dot(x_ref[...], w_ref[...].reshape(D, WIDE))
    ones = triangle(False, False).astype(F32)
    floor = floor_ref[...]
    for b in range(PARTS):
        rows = part_rows(b)
        _, decay = gated(pre_ref[rows, :COLS], floor)
        cum_all = exact_dot(ones, jnp.log(decay))
        cum_ref[rows, :] = cum_all
        total_all = cum_all[ROWS - 1 :, :]
        k_out = ((1.0 - decay).astype(BF).astype(F32) * jnp.exp(total_all - cum_all)).astype(BF)
        for h in range(LOCAL_HEADS):
            value = pre_ref[rows, COLS + h * HEAD_DIM : COLS + (h + 1) * HEAD_DIM].astype(BF)
            s = h * PARTS + b
            state_ref[s] = t_dot(k_out[:, head_cols(h)], value).astype(BF)
            total_ref[s : s + 1, :] = total_all[:, head_cols(h)]


def second_kernel(x_ref, w_ref, fv_ref, cum_ref, floor_ref, pre_ref, q_ref, local_ref):
    pre_ref[...] = dot(x_ref[...], w_ref[...].reshape(D, WIDE))
    causal = triangle(False, False)
    floor = floor_ref[...]
    for b in range(PARTS):
        rows = part_rows(b)
        _, decay = gated(fv_ref[rows, :COLS], floor)
        cum = cum_ref[rows, :]
        k_in = ((1.0 - decay).astype(BF).astype(F32) * jnp.exp(-cum)).astype(BF)
        q_in = (swish(pre_ref[rows, :COLS]).astype(BF).astype(F32) * jnp.exp(cum)).astype(BF)
        q_ref[rows, :] = q_in
        value = fv_ref[rows, COLS:].astype(BF)
        for h in range(LOCAL_HEADS):
            cols = head_cols(h)
            scores = jnp.where(causal, dot_t(q_in[:, cols], k_in[:, cols]), 0.0).astype(BF)
            local_ref[rows, cols] = dot(scores, value[:, cols])


def split3(value):
    first = value.astype(BF).astype(F32)
    second = (value - first).astype(BF).astype(F32)
    return first, second, value - first - second


def chip_kernel(core_ref, mine_ref, other_ref, my_total_ref, other_total_ref, out_ref, *, backward):
    core = core_ref[0]
    second = core == (0 if backward else 1)
    base = core * HALF
    my_total = my_total_ref[pl.ds(base, HALF), :]
    other_total = other_total_ref[pl.ds(base, HALF), :]
    last_decay = jnp.exp(jnp.where(second, my_total, other_total))
    for i in range(HALF):
        mine = mine_ref[base + i].astype(F32)
        other = other_ref[base + i].astype(F32)
        last = jnp.where(second, mine, other)
        first = jnp.where(second, other, mine)
        state = (jnp.transpose(last_decay[i : i + 1, :]) * first + last).astype(BF)
        for d in range(8):
            out_ref[d, i * HEAD_DIM : (i + 1) * HEAD_DIM, :] = state
    if not backward:
        pieces = split3(my_total + other_total)
        tail = jnp.concatenate([*pieces, jnp.zeros((HALF, HEAD_DIM), F32)], axis=0).astype(BF)
        for d in range(8):
            out_ref[d, HALF * HEAD_DIM :, :] = tail


def carry_kernel(place_ref, all_ref, *refs, backward):
    place = place_ref[0]
    if backward:
        totals_ref, out_ref = refs
    else:
        out_ref, totals_ref = refs
        for j in range(8):
            tail = all_ref[j, HALF * HEAD_DIM :, :].astype(F32)
            totals_ref[j] = (tail[:HALF] + tail[HALF : 2 * HALF]) + tail[2 * HALF : 3 * HALF]
    for i in range(HALF):
        carried = jnp.zeros((HEAD_DIM, HEAD_DIM), F32)
        decays = jnp.transpose(jnp.exp(jnp.concatenate([totals_ref[j, i : i + 1, :] for j in range(8)], axis=0)))
        for step in range(7):
            j = 7 - step if backward else step
            reached = j > place if backward else j < place
            block = all_ref[j, i * HEAD_DIM : (i + 1) * HEAD_DIM, :].astype(F32)
            carried = jnp.where(reached, decays[:, j : j + 1] * carried + block, carried)
        out_ref[i] = carried.astype(BF)


def enter_state(core, own_half, other_half, other_end, other_total, s, backward):
    h, b = divmod(s, PARTS)
    chip = jnp.where(core == h, own_half[b], other_half[b]).astype(F32)
    later = core == (0 if backward else 1)
    passed = jnp.transpose(jnp.exp(other_total[s : s + 1, :])) * chip + other_end[s].astype(F32)
    return jnp.where(later, passed, chip)


def mix_kernel(core_ref, pre_ref, q_ref, local_ref, own_half, other_half, other_end, other_total, w_ref,
               out_ref, normed_ref, entered_ref, p0, p1, p2, p3):
    core = core_ref[0]
    for b in range(PARTS):
        rows = part_rows(b)
        for h in range(LOCAL_HEADS):
            cols = head_cols(h)
            s = h * PARTS + b
            state = enter_state(core, own_half, other_half, other_end, other_total, s, False).astype(BF)
            entered_ref[s] = state
            mixed = local_ref[rows, cols] + dot(q_ref[rows, cols], state)
            out_ref[rows, cols] = mixed
            gate = pre_ref[rows, COLS + h * HEAD_DIM : COLS + (h + 1) * HEAD_DIM]
            normed_ref[rows, cols] = (mixed * mean_scale(mixed) * swish(gate)).astype(BF)
    product = dot(normed_ref[...], w_ref[...]).astype(BF)
    for b, part in enumerate((p0, p1, p2, p3)):
        part[...] = product[part_rows(b), :]


def sum_parts(p0, p1, p2, p3):
    return (p0[...].astype(F32) + p1[...].astype(F32)) + (p2[...].astype(F32) + p3[...].astype(F32))


def middle_kernel(hidden_ref, p0, p1, p2, p3, middle_ref, normed_ref):
    middle = hidden_ref[...].astype(F32) + sum_parts(p0, p1, p2, p3)
    middle_ref[...] = middle
    normed_ref[...] = (middle * mean_scale(middle)).astype(BF)


def feed_inputs(parts, grads, w_ref, x_ref, g_ref, down_ref):
    for s in range(16):
        at = s * SLOT
        rows = w_ref[s, w_ref.shape[1] - 32 :, :]
        down_ref[at : at + 32, :] = rows[:, :D]
        down_ref[at + 32 : at + 48, :512] = rows[:16, D:]
        down_ref[at + 32 : at + 48, 512:] = rows[16:, D:]
    for b in range(PARTS):
        x_ref[part_rows(b), :] = parts[b][...]
        g_ref[part_rows(b), :] = grads[b][...]


def feed_kernel(x0, x1, x2, x3, g0, g1, g2, g3, w_ref, act_ref, grad_ref, p0, p1, p2, p3, x_ref, g_ref, down_ref):
    feed_inputs((x0, x1, x2, x3), (g0, g1, g2, g3), w_ref, x_ref, g_ref, down_ref)
    for j in range(3):
        lanes = slice(j * COLS, (j + 1) * COLS)
        ups = slice(PAD + j * COLS, PAD + (j + 1) * COLS)
        gate = dot(x_ref[...], w_ref[:, :64, lanes].reshape(D, COLS))
        up = dot(x_ref[...], w_ref[:, :64, ups].reshape(D, COLS))
        grad = dot_t(g_ref[...], down_ref[lanes, :])
        sigma = lax.logistic(gate)
        active = gate * sigma
        act_ref[:, lanes] = (active * up).astype(BF)
        grad_ref[:, lanes] = (grad * up * swish_slope(gate, sigma)).astype(BF)
        grad_ref[:, ups] = (grad * active).astype(BF)
    product = dot_t(grad_ref[...], w_ref[:, :64, :].reshape(D, 2 * PAD)).astype(BF)
    for b, part in enumerate((p0, p1, p2, p3)):
        part[...] = product[part_rows(b), :]


def feed_grad_kernel(x0, x1, x2, x3, g0, g1, g2, g3, w_ref, grad_ref, act_ref, out_ref, p0, p1, p2, p3,
                     x_ref, g_ref, down_ref):
    feed_inputs((x0, x1, x2, x3), (g0, g1, g2, g3), w_ref, x_ref, g_ref, down_ref)
    product = dot(act_ref[...], down_ref[...]).astype(BF)
    for b, part in enumerate((p0, p1, p2, p3)):
        part[...] = product[part_rows(b), :]
    for j in range(0, 2 * PAD, 512):
        out_ref[:, :64, j : j + 512] = t_dot(x_ref[...], grad_ref[:, j : j + 512]).astype(BF).reshape(16, 64, 512)
    rows = t_dot(act_ref[...], g_ref[...]).astype(BF)
    for s in range(16):
        at = s * SLOT
        out_ref[s, 64:, :D] = rows[at : at + 32]
        out_ref[s, 64:80, D:] = rows[at + 32 : at + 48, :512]
        out_ref[s, 80:, D:] = rows[at + 32 : at + 48, 512:]


def add_kernel(a_ref, b_ref, out_ref):
    out_ref[...] = (a_ref[...].astype(F32) + b_ref[...].astype(F32)).astype(BF)


def result_kernel(middle_ref, p0, p1, p2, p3, out_ref):
    out_ref[...] = (middle_ref[...] + sum_parts(p0, p1, p2, p3)).astype(BF)


def norm_back(value_ref, base_ref, u):
    value = value_ref[...].astype(F32)
    scale = mean_scale(value)
    centered = value * scale
    back = scale * (u - centered * jnp.mean(u * centered, axis=-1, keepdims=True))
    return base_ref[...].astype(F32) + back


def branch_kernel(value_ref, base_ref, p0, p1, p2, p3, out_ref, low_ref):
    total = norm_back(value_ref, base_ref, sum_parts(p0, p1, p2, p3))
    out_ref[...] = total
    low_ref[...] = total.astype(BF)


def last_kernel(value_ref, base_ref, p0, p1, p2, p3, low_ref):
    low_ref[...] = norm_back(value_ref, base_ref, sum_parts(p0, p1, p2, p3)).astype(BF)


def head_back_kernel(b0, b1, b2, b3, w_ref, pre_ref, q_ref, mixed_ref, branch_ref, gate_ref, out_grad_ref, state_ref):
    for b, part in enumerate((b0, b1, b2, b3)):
        branch_ref[part_rows(b), :] = part[...]
    grads = dot_t(branch_ref[...], w_ref[...])
    for b in range(PARTS):
        rows = part_rows(b)
        for h in range(LOCAL_HEADS):
            cols = head_cols(h)
            grad = grads[rows, cols]
            mixed = mixed_ref[rows, cols]
            scale = mean_scale(mixed)
            normed = mixed * scale
            gate = pre_ref[rows, COLS + h * HEAD_DIM : COLS + (h + 1) * HEAD_DIM]
            sigma = lax.logistic(gate)
            gate_ref[rows, cols] = (grad * normed * swish_slope(gate, sigma)).astype(BF)
            c = grad * (gate * sigma)
            mixer = (scale * (c - normed * jnp.mean(c * normed, axis=-1, keepdims=True))).astype(BF)
            out_grad_ref[rows, cols] = mixer
            state_ref[h * PARTS + b] = t_dot(q_ref[rows, cols], mixer).astype(BF)


def near_back_kernel(core_ref, x_ref, normed_ref, branch_ref, qg_ref, fv_ref, cum_ref, floor_ref, q_ref, gate_ref,
                     out_grad_ref, entered_ref, grad_ref, log_ref, key_ref, value_ref,
                     mine_ref, other_ref, my_rows_ref, other_rows_ref, all_ref, rows_ref):
    causal = triangle(False, False)
    suffix = triangle(False, True).astype(F32)
    floor = floor_ref[...]
    for b in range(PARTS):
        rows = part_rows(b)
        _, decay = gated(fv_ref[rows, :COLS], floor)
        cum = cum_ref[rows, :]
        grow_all = jnp.exp(cum)
        shrink_all = jnp.exp(-cum)
        k_all = ((1.0 - decay).astype(BF).astype(F32) * shrink_all).astype(BF)
        q_pre = qg_ref[rows, :COLS]
        slope_all = swish_slope(q_pre, lax.logistic(q_pre))
        for h in range(LOCAL_HEADS):
            cols = head_cols(h)
            value = fv_ref[rows, COLS + h * HEAD_DIM : COLS + (h + 1) * HEAD_DIM].astype(BF)
            q_in, k_in = q_ref[rows, cols], k_all[:, cols]
            out_grad = out_grad_ref[rows, cols]
            scores = jnp.where(causal, dot_t(q_in, k_in), 0.0).astype(BF)
            grad_scores = jnp.where(causal, dot_t(out_grad, value), 0.0).astype(BF)
            inner = dot(grad_scores, k_in) + dot_t(out_grad, entered_ref[h * PARTS + b])
            back = t_dot(grad_scores, q_in)
            near = q_in.astype(F32) * inner - k_in.astype(F32) * back
            log_ref[rows, cols] = exact_dot(suffix, near)
            key_ref[rows, cols] = (back * shrink_all[:, cols]).astype(BF)
            value_ref[rows, cols] = t_dot(scores, out_grad).astype(BF)
            grad_ref[rows, cols] = (inner * grow_all[:, cols] * slope_all[:, cols]).astype(BF)
    grad_ref[:, COLS:] = gate_ref[...]
    column_grad(core_ref[0], x_ref, grad_ref, mine_ref, other_ref, all_ref)
    row_grad(core_ref[0], normed_ref, branch_ref, my_rows_ref, other_rows_ref, rows_ref)


def far_back_kernel(core_ref, fv_ref, cum_ref, floor_ref, log_ref, key_ref, value_ref, entered_ref, own_half, other_half,
                    other_end, other_total, qg_ref, w_fv_ref, w_qg_ref, x_ref,
                    floor_grad_ref, mine_ref, other_ref, p0, p1, p2, p3, grad_ref, all_ref):
    core = core_ref[0]
    before = triangle(True, False).astype(F32)
    floor = floor_ref[...]
    floor_sum = jnp.zeros((1, COLS), F32)
    for b in range(PARTS):
        rows = part_rows(b)
        sigma, decay = gated(fv_ref[rows, :COLS], floor)
        cum = cum_ref[rows, :]
        total = cum[ROWS - 1 :, :]
        to_end = jnp.exp(total - cum)
        k_all = ((1.0 - decay).astype(BF).astype(F32) * to_end).astype(BF)
        aheads, edges = [], []
        for h in range(LOCAL_HEADS):
            cols = head_cols(h)
            s = h * PARTS + b
            following = enter_state(core, own_half, other_half, other_end, other_total, s, True)
            low = following.astype(BF)
            value = fv_ref[rows, COLS + h * HEAD_DIM : COLS + (h + 1) * HEAD_DIM].astype(BF)
            aheads.append(dot_t(value, low))
            edges.append(jnp.transpose(jnp.sum(following * entered_ref[s].astype(F32), axis=1, keepdims=True)))
            grad_value = value_ref[rows, cols].astype(F32) + dot(k_all[:, cols], low)
            grad_ref[rows, COLS + h * HEAD_DIM : COLS + (h + 1) * HEAD_DIM] = grad_value.astype(BF)
        ahead = jnp.concatenate(aheads, axis=1)
        edge = jnp.concatenate(edges, axis=1)
        far = exact_dot(before, k_all.astype(F32) * ahead)
        grad_log = log_ref[rows, :] + far + jnp.exp(total) * edge
        grad_decay = grad_log / decay - (key_ref[rows, :].astype(F32) + ahead * to_end)
        floor_sum = floor_sum + jnp.sum(grad_decay * (1.0 - sigma), axis=0, keepdims=True)
        grad_ref[rows, :COLS] = (grad_decay * (1.0 - floor) * sigma * (1.0 - sigma)).astype(BF)
    floor_grad_ref[...] = floor_sum
    column_grad(core, x_ref, grad_ref, mine_ref, other_ref, all_ref)
    product = dot_t(grad_ref[...], w_fv_ref[...].reshape(D, WIDE)) + dot_t(qg_ref[...], w_qg_ref[...].reshape(D, WIDE))
    product = product.astype(BF)
    for b, part in enumerate((p0, p1, p2, p3)):
        part[...] = product[part_rows(b), :]


def column_grad(core, a_ref, g_ref, mine_ref, other_ref, all_ref):
    n = g_ref.shape[1]
    all_ref[...] = t_dot(a_ref[...], g_ref[...]).astype(BF).reshape(8, 2, 64, n)
    mine_ref[...] = all_ref[:, pl.ds(core, 1)].reshape(8, 64, n)
    other_ref[...] = all_ref[:, pl.ds(1 - core, 1)].reshape(8, 64, n)


def row_grad(core, a_ref, g_ref, mine_ref, other_ref, all_ref):
    rows = mine_ref.shape[1]
    all_ref[...] = t_dot(a_ref[...], g_ref[...]).astype(BF).reshape(2, 2, rows, D)
    mine_ref[...] = all_ref[:, pl.ds(core, 1)].reshape(2, rows, D)
    other_ref[...] = all_ref[:, pl.ds(1 - core, 1)].reshape(2, rows, D)


def pack_columns(mine_ref, other_ref, out_ref, start):
    lanes = mine_ref.shape[2] // 2
    for i in range(8):
        value = (mine_ref[i].astype(F32) + other_ref[i].astype(F32)).astype(BF)
        for half in range(2):
            for j in range(lanes // 128):
                at = half * lanes + j * 128
                out_ref[i * 2 + half, start + j * 64 : start + (j + 1) * 64, :] = value[:, at : at + 128]


def pack_rows(mine_ref, other_ref, out_ref, start):
    for yl in range(2):
        value = (mine_ref[yl].astype(F32) + other_ref[yl].astype(F32)).astype(BF)
        for p in range(8):
            at = start + p % 2 * 64
            for yh in range(2):
                out_ref[p // 2 * 4 + yl * 2 + yh, at : at + 64, :] = value[:, p * 128 : (p + 1) * 128]


def rider_rows(value):
    rows = [piece[:, cols] for piece in split3(value) for cols in (slice(0, 128), slice(128, 256))]
    return jnp.concatenate([*rows, jnp.zeros((10, 128), F32)], axis=0).astype(BF)


def rider_value(rows):
    rows = rows.astype(F32)
    halves = [(rows[i : i + 1] + rows[i + 2 : i + 3]) + rows[i + 4 : i + 5] for i in range(2)]
    return jnp.concatenate(halves, axis=1)


def pack_kernel(mine_ref, other_ref, floor_ref, other_floor_ref, my_qg_ref, other_qg_ref, my_rows_ref, other_rows_ref, out_ref):
    pack_columns(mine_ref, other_ref, out_ref, 0)
    rider = rider_rows(floor_ref[...] + other_floor_ref[...])
    for i in range(16):
        out_ref[i, 128:144, :] = rider
    pack_columns(my_qg_ref, other_qg_ref, out_ref, 144)
    pack_rows(my_rows_ref, other_rows_ref, out_ref, 272)


def total_of(all_ref, rows):
    total = all_ref[0, rows, :].astype(F32)
    for i in range(1, 16):
        total = total + all_ref[i, rows, :].astype(F32)
    return total


def sum_kernel(all_ref, out_ref, rows_ref):
    first = total_of(all_ref, slice(0, 128)).astype(BF)
    floor = rider_value(all_ref[0, 128:144, :])
    for i in range(1, 16):
        floor = floor + rider_value(all_ref[i, 128:144, :])
    rider = rider_rows(floor)
    second = total_of(all_ref, slice(144, 272)).astype(BF)
    for i in range(8):
        out_ref[i, :128, :] = first
        out_ref[i, 128:144, :] = rider
        out_ref[i, 144:, :] = second
    rows_ref[...] = total_of(all_ref, slice(272, 400)).astype(BF)


def feed_grads_kernel(z_ref, s0, s1, s2, s3, w_ref, gain_ref, up_ref, gain_grad_ref, down_ref):
    chosen = jnp.concatenate([selection(z, SLOTS, UNITS, True) for z in quarters(z_ref[0])], axis=0)
    gain = column(gain_ref)
    gain_grad = jnp.zeros((64, 128), F32)
    taken = jnp.concatenate(
        [
            jnp.concatenate([ref[:64, i * SLOTS : (i + 1) * SLOTS] for ref in (s0, s1, s2, s3)], axis=1)
            for i in range(4)
        ],
        axis=0,
    )
    values = dot(taken, chosen)
    for i in range(4):
        value = values[i * 64 : (i + 1) * 64]
        cols = slice(i * UNITS, (i + 1) * UNITS)
        up_ref[:, cols] = value * gain
        gain_grad = gain_grad + lane_blocks(value * w_ref[:, cols].astype(F32))
    gain_grad_ref[...] = row_sums(gain_grad)
    down = jnp.zeros((OWNED, D), F32)
    for z, ref in zip(quarters(z_ref[0]), (s0, s1, s2, s3)):
        last = jnp.concatenate([ref[64:80, D:], ref[80:, D:]], axis=1)
        rows = jnp.concatenate([ref[64:, :D], last], axis=0)
        down = down + dot(selection(z, SLOT, OWNED, False), rows)
    down_ref[...] = down


def mix_grads_kernel(z_ref, all_ref, o0, o1, o2, o3, w_ref, gain_ref, out_w_ref, out_gain_ref,
                     mix_ref, gain_grad_ref, out_ref, out_gain_grad_ref, floor_ref):
    gain, out_gain = column(gain_ref), column(out_gain_ref)
    gain_grad = jnp.zeros((64, 128), F32)
    out_gain_grad = jnp.zeros((64, 128), F32)
    for yh in range(2):
        for z in range(4):
            i = yh * 4 + z
            for start, block in ((0, 2 if yh else 1), (144, 3 if yh else 0)):
                for j in range(2):
                    value = all_ref[i, start + j * 64 : start + (j + 1) * 64, :].astype(F32)
                    at = block * D + z * COLS + j * 128
                    mix_ref[:, at : at + 128] = value * gain
                    gain_grad = gain_grad + value * w_ref[:, at : at + 128].astype(F32)
            if yh == 0:
                floor_ref[:, z * COLS : (z + 1) * COLS] = rider_value(all_ref[i, 128:144, :])
    for z, ref in zip(quarters(z_ref[0]), (o0, o1, o2, o3)):
        for k in range(2):
            cols = pl.ds(pl.multiple_of((z * 2 + k) * 128, 128), 128)
            value = ref[k * 64 : (k + 1) * 64, :].astype(F32)
            out_ref[:, cols] = value * out_gain
            out_gain_grad = out_gain_grad + value * out_w_ref[:, cols].astype(F32)
    gain_grad_ref[...] = row_sums(gain_grad)
    out_gain_grad_ref[...] = row_sums(out_gain_grad)


def scalar(value):
    return value.reshape(1).astype(jnp.int32)


def body(hidden, mixer_weight, output_weight, gate_up_weight, down_weight, mixer_gain, group_gain, feed_gain,
         forget_floor, out_grad):
    z = lax.axis_index("z")
    z_of = scalar(z)
    core = scalar(lax.axis_index("c"))
    place = scalar(lax.axis_index("x") * 2 + lax.axis_index("yl"))
    gain_one, gain_group, gain_two = (g.reshape(1, 64) for g in (mixer_gain, group_gain, feed_gain))
    floor = lax.dynamic_index_in_dim(forget_floor.reshape(PARTS, COLS), z, 0)
    own = [near_shape((ROWS, D), BF)] * 4
    state_dims = (STATES, HEAD_DIM, HEAD_DIM)
    half_dims = (HALF, HEAD_DIM, HEAD_DIM)

    w_sent, out_own = kernel_call(
        prepare_kernel, (shape((8, 64, D), BF), shape((64, D), BF)),
        z_of, mixer_weight, gain_one, output_weight, gain_group,
    )
    tokens = gather_z(hidden)
    w_mine = exchange(w_sent, ("x", "yl"))
    w_out = lax.all_gather(out_own, ("x", "yl", "c"))
    w_other = shift(after(w_mine, *tokens), "c", 1)
    x_all, w_fv, w_qg, pre_fv, cum, end, total = kernel_call(
        first_kernel,
        (
            shape((TOKENS, D), BF),
            shape((8, 2, 64, WIDE), BF),
            shape((8, 2, 64, WIDE), BF),
            shape((TOKENS, WIDE), F32),
            shape((TOKENS, COLS), F32),
            near_shape(state_dims, BF),
            shape((STATES, HEAD_DIM), F32),
        ),
        core, *tokens, w_mine, w_other, floor,
        flops=2 * TOKENS * D * WIDE,
        near=(5, 6),
    )

    def chip_state(end_state, other_total, backward, order=()):
        other_end = shift(end_state, "c", 1)
        sent = kernel_call(
            functools.partial(chip_kernel, backward=backward),
            shape((8, HALF * HEAD_DIM + (0 if backward else TAIL), HEAD_DIM), BF),
            core, end_state, other_end, total, other_total,
            order=order,
            near=(1, 2),
        )
        return sent, other_end

    other_total = shift(total, "c", 1)
    sent, other_end = chip_state(end, other_total, False)
    arrived = exchange(sent, ("x", "yl"))
    grads_out = gather_z(after(out_grad, sent))
    pre_qg, q_in, local_out = kernel_call(
        second_kernel,
        (shape((TOKENS, WIDE), F32), shape((TOKENS, COLS), BF), shape((TOKENS, COLS), F32)),
        x_all, w_qg, pre_fv, cum, floor,
        flops=2 * TOKENS * D * WIDE,
        order=(sent,),
    )
    w_out = lax.dynamic_index_in_dim(w_out.reshape(PARTS, COLS, D), z, 0, keepdims=False)
    feed_own_weights = kernel_call(
        prepare_feed_kernel, shape((FEED_ROWS, 2 * PAD), BF), z_of, gate_up_weight, gain_two, down_weight,
        order=(q_in, w_out),
    )
    w_feed = lax.all_gather(after(feed_own_weights, arrived, *grads_out), ("x", "yl", "c"))
    own_half, totals = kernel_call(
        functools.partial(carry_kernel, backward=False),
        (near_shape(half_dims, BF), shape((8, HALF, HEAD_DIM), F32)),
        place, arrived,
        order=(feed_own_weights, w_out, *grads_out),
        near=(1,),
    )
    mixed, normed_out, entered, *parts = kernel_call(
        mix_kernel,
        (shape((TOKENS, COLS), F32), shape((TOKENS, COLS), BF), shape(state_dims, BF), *own),
        core, pre_qg, q_in, local_out, own_half, shift(own_half, "c", 1), other_end, other_total, w_out,
        flops=2 * TOKENS * COLS * D,
        near=(4, 5),
    )
    middle, feed_own = kernel_call(
        middle_kernel, (shape((ROWS, D), F32), near_shape((ROWS, D), BF)), hidden, *scatter_z(parts),
        near=(1, 2, 3, 4),
    )
    feed_in = (*gather_z(feed_own), *grads_out, w_feed)
    feed_scratch = [pltpu.VMEM((TOKENS, D), BF), pltpu.VMEM((TOKENS, D), BF), pltpu.VMEM((PAD, D), BF)]
    act, grad_up, *parts = kernel_call(
        feed_kernel,
        (shape((TOKENS, PAD), BF), shape((TOKENS, 2 * PAD), BF), *own),
        *feed_in,
        scratch=feed_scratch,
        flops=2 * TOKENS * D * PAD * 5,
    )
    feed_back = scatter_z(parts)
    feed_grad, *down_parts = kernel_call(
        feed_grad_kernel,
        (shape((16, FEED_ROWS, 2 * PAD), BF), *[shape((ROWS, D), BF)] * 4),
        *feed_in, grad_up, act,
        scratch=feed_scratch,
        flops=2 * TOKENS * D * PAD * 3,
        order=(parts[3],),
    )
    grad_middle, branch_own = kernel_call(
        branch_kernel, (shape((ROWS, D), F32), near_shape((ROWS, D), BF)), middle, out_grad, *feed_back,
        order=(feed_grad,),
        near=(2, 3, 4, 5),
    )
    feed_sum = lax.psum_scatter(after(feed_grad, *feed_back), ("x", "yl", "c"), scatter_dimension=0)
    branch = gather_z(branch_own)
    branch_all, grad_gate, grad_mixed, end_grad = kernel_call(
        head_back_kernel,
        (
            shape((TOKENS, D), BF),
            shape((TOKENS, COLS), BF),
            shape((TOKENS, COLS), BF),
            near_shape(state_dims, BF),
        ),
        *branch, w_out, pre_qg, q_in, mixed,
        flops=2 * TOKENS * COLS * D,
        near=(0, 1, 2, 3),
    )

    sent, other_end = chip_state(end_grad, other_total, True)
    down_parts = scatter_z(after(down_parts, sent))
    arrived = exchange(sent, ("x", "yl"))
    grad_qg, near_log, near_key, near_value, qg_mine, qg_other, out_mine, out_other = kernel_call(
        near_back_kernel,
        (
            shape((TOKENS, WIDE), BF),
            shape((TOKENS, COLS), F32),
            *[shape((TOKENS, COLS), BF)] * 2,
            *[shape((8, 64, WIDE), BF)] * 2,
            *[shape((2, 64, D), BF)] * 2,
        ),
        core, x_all, normed_out, branch_all, pre_qg, pre_fv, cum, floor, q_in, grad_gate, grad_mixed, entered,
        scratch=[pltpu.VMEM((8, 2, 64, WIDE), BF), pltpu.VMEM((2, 2, 64, D), BF)],
        flops=2 * TOKENS * (HEAD_DIM * HEAD_DIM * 12 + D * WIDE),
        order=(sent,),
    )
    own_half = kernel_call(
        functools.partial(carry_kernel, backward=True), near_shape(half_dims, BF), place, arrived, totals,
        order=(grad_qg, *down_parts),
        near=(1,),
    )
    qg_other, out_other = after((qg_other, out_other), own_half)
    floor_part, fv_mine, fv_other, *parts = kernel_call(
        far_back_kernel,
        (near_shape((1, COLS), F32), *[near_shape((8, 64, WIDE), BF)] * 2, *[shape((ROWS, D), BF)] * 4),
        core, pre_fv, cum, floor, near_log, near_key, near_value, entered, own_half, shift(own_half, "c", 1), other_end,
        other_total, grad_qg, w_fv, w_qg, x_all,
        scratch=[pltpu.VMEM((TOKENS, WIDE), BF), pltpu.VMEM((8, 2, 64, WIDE), BF)],
        flops=2 * TOKENS * D * D * 2,
        near=(8, 9),
    )
    sent = kernel_call(
        pack_kernel, shape((16, 400, 128), BF), fv_mine, shift(fv_other, "c", 1), floor_part,
        shift(floor_part, "c", 1), qg_mine, shift(qg_other, "c", 1), out_mine, shift(out_other, "c", 1),
        near=(0, 1, 2, 3, 5, 7),
    )

    arrived = exchange(sent, ("x", "yl", "yh"))
    parts = scatter_z(after(parts, sent))
    feed_other = shift(after(feed_sum, *parts), "yh", 1)
    result = kernel_call(result_kernel, shape((ROWS, D), BF), middle, *down_parts, order=(sent,))
    grad_tokens = kernel_call(last_kernel, shape((ROWS, D), BF), hidden, grad_middle, *parts, order=(result,))
    copies, rows = kernel_call(
        sum_kernel, (shape((8, 272, 128), BF), shape((128, 128), BF)), arrived, order=(feed_other, grad_tokens), near=(0,)
    )
    last_sums = exchange(copies, ("yh", "z"))
    out_sums = gather_z(transpose_xz(rows))
    feed_total = kernel_call(
        add_kernel, shape((FEED_ROWS, 2 * PAD), BF), feed_sum, feed_other, order=(copies,)
    )
    feed_totals = gather_z(feed_total)
    up_grad, feed_gain_grad, down_grad = kernel_call(
        feed_grads_kernel,
        (shape((64, 2 * FF), F32), shape((1, 64), F32), shape((OWNED, D), F32)),
        z_of, *feed_totals, gate_up_weight, gain_two,
        order=(copies,),
    )
    mix_grad, gain_grad, out_weight_grad, group_gain_grad, floor_grad = kernel_call(
        mix_grads_kernel,
        (
            shape((64, 4 * D), F32),
            shape((1, 64), F32),
            shape((64, D), F32),
            shape((1, 64), F32),
            shape((1, D), F32),
        ),
        z_of, last_sums, *out_sums, mixer_weight, gain_one, output_weight, gain_group,
        order=(up_grad,),
        near=(1,),
    )
    return (
        result,
        grad_tokens,
        mix_grad,
        out_weight_grad,
        up_grad,
        down_grad,
        gain_grad.reshape(64),
        group_gain_grad.reshape(64),
        feed_gain_grad.reshape(64),
        floor_grad.reshape(D),
    )


def solution(mesh):
    cut = Mesh(mesh.devices.reshape(2, 4, 4, 2, 2), AXES)
    seq = ("x", "yl", "c")
    rows, weight, vector = P(AXES, None), P(seq, None), P(seq)
    in_specs = (rows, weight, weight, weight, weight, vector, vector, vector, P(), rows)
    out_specs = (rows, rows, weight, weight, weight, weight, vector, vector, vector, P())
    return jax.shard_map(body, mesh=cut, in_specs=in_specs, out_specs=out_specs, check_vma=False)
```
